256 devices in a mesh: dp: 8 (over x, z_lo), mp: 32 (over y, z_hi, core).
Axes of the slice: x: 4, y: 4, z: 8 (z_hi: 4, z_lo: 2; z = z_hi * 2 + z_lo), core: 2. Of those that a mesh axis runs over, the one named last changes fastest.
Arguments:
- tokens: bfloat16 [2048, 4096], P('dp', 'mp'), may hold values from -51 to 51
- gain: bfloat16 [4096], P('mp'), may hold values from 0.099609375 to 1.8984375
- w_qkv: bfloat16 [4096, 12288], P(None, 'mp'), may hold values from -0.09375 to 0.09375
- qk_gain: float32 [2, 4096], P(None, 'mp'), may hold values from 0.5 to 2
- w_up: bfloat16 [4096, 12288], P(None, 'mp'), may hold values from -0.09375 to 0.09375
- w_attn_out: bfloat16 [4096, 4096], P('mp'), may hold values from -0.09375 to 0.09375
- w_down: bfloat16 [12288, 4096], P('mp'), may hold values from -0.0546875 to 0.0546875
- cotangent: bfloat16 [2048, 4096], P('dp', 'mp'), may hold values from -51 to 51
Outputs:
- mixed: bfloat16 [2048, 4096], P('dp', 'mp')
- d_tokens: bfloat16 [2048, 4096], P('dp', 'mp')
- g_gain: float32 [4096], P('mp')
- g_qk: float32 [2, 4096], P(None, 'mp')
- g_qkv: bfloat16 [4096, 12288], P('dp', 'mp')
- g_up: bfloat16 [4096, 12288], P('dp', 'mp')
- g_attn_out: bfloat16 [4096, 4096], P('mp', 'dp')
- g_down: bfloat16 [12288, 4096], P('mp', 'dp')
The draws below stay inside these ranges and needn't reach their ends.
All inputs are finite; a program needn't handle non-finite values.
Results may differ from the reference program's by a relative error of at most 0.024.
Values may be sent and summed in bfloat16 or wider, within the bound.
No kernel may reach another device: no remote copies, remote signals or barrier semaphores. Data moves between devices by JAX's collectives and lax.ppermute only.
A program may use at most 128 MiB of HBM per device.

```python
import math
import jax
import jax.numpy as jnp
from jax import lax

D = 4096
HD = 128
TOK = 256
HEADS = 32
FF = 12288
TOKENS = 2048
N_DP = 8


def spread_scales(key, rows_count, cols_count):
    first, second = jax.random.split(key)
    row_scale = jnp.exp(jax.random.uniform(first, (rows_count, 1), jnp.float32, math.log(0.3), math.log(3.0)))
    column = jnp.arange(cols_count, dtype=jnp.float32) / (cols_count - 1)
    col_scale = jnp.exp(math.log(3.0) * column) * jnp.exp(jax.random.uniform(second, (cols_count,), jnp.float32, math.log(0.7), math.log(1.4)))
    return row_scale * col_scale


def draw_tokens(key, part):
    key = jax.random.fold_in(key, 11)
    first, second = jax.random.split(key)
    base = jnp.clip(jax.random.normal(first, (TOKENS, D), jnp.float32), -4.0, 4.0)
    return (base * spread_scales(second, TOKENS, D)).astype(jnp.bfloat16)


def draw_cotangent(key, part):
    key = jax.random.fold_in(key, 23)
    first, second = jax.random.split(key)
    base = jnp.clip(jax.random.normal(first, (TOKENS, D), jnp.float32), -4.0, 4.0)
    return (base * spread_scales(second, TOKENS, D)).astype(jnp.bfloat16)


def levels(rng, shape, cuts, least, top_value):
    level, own = 1.0, jax.random.fold_in(rng, 6)
    for position, shards_of in cuts:
        draws = jnp.exp(jax.random.uniform(jax.random.fold_in(own, position), (shards_of,), jnp.float32, least / len(cuts), top_value / len(cuts)))
        level = level * jnp.repeat(draws, shape[position] // shards_of).reshape([-1 if axis == position else 1 for axis in range(len(shape))])
    return level


def normal_values(rng, dims, width, reach, cuts=(), kind=jnp.bfloat16):
    level = levels(rng, dims, cuts, -0.22, 0.18) if cuts else 1.0
    values = jax.random.normal(rng, dims, jnp.float32) * width * level
    return jnp.minimum(jnp.maximum(values, -reach), reach).astype(kind)


def setup_inputs(seed: int = 0) -> dict:
    keys = jax.random.split(jax.random.key(seed), 9)
    return {
        "tokens": draw_tokens(jax.random.fold_in(keys[8], 71), 0),
        "gain": jnp.clip(1.0 + 0.18 * jax.random.normal(keys[1], (D,), jnp.float32), 0.099609375, 1.8984375).astype(jnp.bfloat16),
        "w_qkv": normal_values(keys[2], (D, 3 * HEADS * HD), D ** -0.5, 0.09375, ((1, 32),)),
        "qk_gain": jnp.clip(jnp.exp(math.log(2.0) - 1.3862944 * jax.random.uniform(keys[3], (2, HEADS * HD), jnp.float32) ** levels(keys[3], (2, HEADS * HD), ((1, 32),), -0.2, 0.2)), 0.5, 2.0),
        "w_up": normal_values(keys[4], (D, FF), D ** -0.5, 0.09375, ((1, 32),)),
        "w_attn_out": normal_values(keys[5], (HEADS * HD, D), (HEADS * HD) ** -0.5, 0.09375, ((0, 32),)),
        "w_down": normal_values(keys[6], (FF, D), FF ** -0.5, 0.0546875, ((0, 32),)),
        "cotangent": draw_cotangent(jax.random.fold_in(keys[8], 71), 0),
    }


EPS = 1e-06

def unit_rows(block):
    centred = block - lax.optimization_barrier(jnp.mean(block, axis=-1, keepdims=True))
    return centred * lax.rsqrt(lax.optimization_barrier(jnp.mean(centred * centred, axis=-1, keepdims=True)) + EPS)

def one_head(queries, keys_in, values_in, gain_query, gain_key):
    q_normed = (unit_rows(queries) * gain_query).astype(jnp.bfloat16)
    k_normed = (unit_rows(keys_in) * gain_key).astype(jnp.bfloat16)
    scores = jnp.dot(q_normed, k_normed.T, preferred_element_type=jnp.float32) / math.sqrt(queries.shape[-1])
    probs = jax.nn.softmax(scores, axis=-1).astype(jnp.bfloat16)
    return jnp.dot(probs, values_in.astype(jnp.bfloat16), preferred_element_type=jnp.float32)

def smooth_gate(pre_act):
    return jax.nn.gelu(pre_act, approximate=False)

def rounded_term(term):
    return lax.optimization_barrier(term.astype(jnp.bfloat16)).astype(jnp.float32)

def reference(tokens, gain, w_qkv, qk_gain, w_up, w_attn_out, w_down, cotangent):
    all_heads = jax.vmap(one_head)
    gain_f = gain.astype(jnp.float32)
    head_gains = qk_gain.reshape(2, HEADS, HD)

    def image_step(totals, pair):
        image, upstream = pair
        image_f = image.astype(jnp.float32)
        centred = image_f - lax.optimization_barrier(jnp.mean(image_f, axis=1, keepdims=True))
        inverse = lax.rsqrt(lax.optimization_barrier(jnp.mean(centred * centred, axis=1, keepdims=True)) + EPS)
        unit_tokens = centred * inverse
        normed = (unit_tokens * gain_f).astype(jnp.bfloat16)
        projected = jnp.dot(normed, w_qkv, preferred_element_type=jnp.float32).reshape(TOK, HEADS, 3, HD)
        queries = jnp.transpose(projected[:, :, 0], (1, 0, 2))
        keys_in = jnp.transpose(projected[:, :, 1], (1, 0, 2))
        values_in = jnp.transpose(projected[:, :, 2], (1, 0, 2))
        attended, attn_back = jax.vjp(all_heads, queries, keys_in, values_in, head_gains[0], head_gains[1])
        att_rows = jnp.transpose(attended, (1, 0, 2)).reshape(TOK, HEADS * HD).astype(jnp.bfloat16)
        up_pre = jnp.dot(normed, w_up, preferred_element_type=jnp.float32)
        activated, gate_back = jax.vjp(smooth_gate, up_pre)
        act_rows = activated.astype(jnp.bfloat16)
        branch_sum = jnp.dot(att_rows, w_attn_out, preferred_element_type=jnp.float32) + jnp.dot(act_rows, w_down, preferred_element_type=jnp.float32)
        mixed = (image_f + branch_sum).astype(jnp.bfloat16)
        d_att = jnp.dot(upstream, w_attn_out.T, preferred_element_type=jnp.float32)
        d_act = jnp.dot(upstream, w_down.T, preferred_element_type=jnp.float32)
        grad_q, grad_k, grad_v, grad_gq, grad_gk = attn_back(jnp.transpose(d_att.reshape(TOK, HEADS, HD), (1, 0, 2)))
        d_qkv = jnp.transpose(jnp.stack([grad_q, grad_k, grad_v], axis=1), (2, 0, 1, 3)).reshape(TOK, 3 * HEADS * HD).astype(jnp.bfloat16)
        d_up = gate_back(d_act)[0].astype(jnp.bfloat16)
        d_normed = jnp.dot(d_qkv, w_qkv.T, preferred_element_type=jnp.float32) + jnp.dot(d_up, w_up.T, preferred_element_type=jnp.float32)
        scaled = d_normed * gain_f
        first_mean = lax.optimization_barrier(jnp.mean(scaled, axis=1, keepdims=True))
        second_mean = lax.optimization_barrier(jnp.mean(scaled * unit_tokens, axis=1, keepdims=True))
        d_image = (upstream.astype(jnp.float32) + inverse * (scaled - first_mean - unit_tokens * second_mean)).astype(jnp.bfloat16)
        sum_qkv, sum_up, sum_out, sum_down, sum_gain, sum_qk = totals
        sum_qkv = sum_qkv + rounded_term(jnp.dot(normed.T, d_qkv, preferred_element_type=jnp.float32))
        sum_up = sum_up + rounded_term(jnp.dot(normed.T, d_up, preferred_element_type=jnp.float32))
        sum_out = sum_out + rounded_term(jnp.dot(att_rows.T, upstream, preferred_element_type=jnp.float32))
        sum_down = sum_down + rounded_term(jnp.dot(act_rows.T, upstream, preferred_element_type=jnp.float32))
        sum_gain = sum_gain + lax.optimization_barrier(jnp.sum(d_normed * unit_tokens, axis=0))
        sum_qk = sum_qk + jnp.stack([grad_gq, grad_gk]).reshape(2, HEADS * HD)
        return ((sum_qkv, sum_up, sum_out, sum_down, sum_gain, sum_qk), (mixed, d_image))
    start = (jnp.zeros((D, 3 * HEADS * HD), jnp.float32), jnp.zeros((D, FF), jnp.float32), jnp.zeros((HEADS * HD, D), jnp.float32), jnp.zeros((FF, D), jnp.float32), jnp.zeros((D,), jnp.float32), jnp.zeros((2, HEADS * HD), jnp.float32))
    images = (tokens.reshape(N_DP, TOK, D), cotangent.reshape(N_DP, TOK, D))
    totals, outputs = lax.scan(image_step, start, images)
    sum_qkv, sum_up, sum_out, sum_down, sum_gain, sum_qk = totals
    mixed = outputs[0].reshape(TOKENS, D)
    d_tokens = outputs[1].reshape(TOKENS, D)
    return (mixed, d_tokens, sum_gain, sum_qk, sum_qkv.astype(jnp.bfloat16), sum_up.astype(jnp.bfloat16), sum_out.astype(jnp.bfloat16), sum_down.astype(jnp.bfloat16))
```

```python
import math

import jax
import jax.numpy as jnp
from jax import lax
from jax.sharding import PartitionSpec as P

D = 4096
HD = 128
EPS = 1e-06
F32 = jnp.float32
BF16 = jnp.bfloat16


def mp_perm(dy, dz, dc):
    return [
        (
            (y * 4 + z) * 2 + c,
            ((y + dy) % 4 * 4 + (z + dz) % 4) * 2 + (c + dc) % 2,
        )
        for y in range(4)
        for z in range(4)
        for c in range(2)
    ]


def dp_perm(dx, dz):
    return [
        (x * 2 + z, (x + dx) % 4 * 2 + (z + dz) % 2) for x in range(4) for z in range(2)
    ]


SPREAD = [(i * 32 + m, m // 4 * 32 + i * 4 + m % 4) for i in range(8) for m in range(32)]


def shift_y(block, by):
    return lax.ppermute(block, "mp", mp_perm(by, 0, 0))


def shift_z(block, by):
    return lax.ppermute(block, "mp", mp_perm(0, by, 0))


def swap_core(block):
    return lax.ppermute(block, "mp", mp_perm(0, 0, 1))


def shift_x(block, by):
    return lax.ppermute(block, "dp", dp_perm(by, 0))


def swap_z(block):
    return lax.ppermute(block, "dp", dp_perm(0, 1))


def placed(pieces, me):
    n = len(pieces)
    out = jnp.zeros((n, *pieces[0].shape), pieces[0].dtype)
    for k, piece in enumerate(pieces):
        out = lax.dynamic_update_index_in_dim(out, piece, (me + k) % n, 0)
    return out


def gather4(block, shift, me):
    return placed([block, shift(block, -1), shift(block, 2), shift(block, 1)], me)


def pair(block, other, me):
    return jnp.where(me == 0, jnp.stack([block, other]), jnp.stack([other, block]))


def scatter4(blocks, shift, me):
    total = lax.dynamic_index_in_dim(blocks, me, 0, keepdims=False).astype(F32)
    for by in (1, 2, 3):
        piece = lax.dynamic_index_in_dim(blocks, (me + by) % 4, 0, keepdims=False)
        total = total + shift(piece, by if by < 3 else -1).astype(F32)
    return total


def sum4(block, shift):
    return block + shift(block, 1) + shift(block, 2) + shift(block, -1)


def unit_rows(block):
    centred = block - jnp.mean(block, axis=-1, keepdims=True)
    return centred * lax.rsqrt(jnp.mean(centred * centred, axis=-1, keepdims=True) + EPS)


def one_head(queries, keys_in, values_in, gain_query, gain_key):
    q_normed = (unit_rows(queries) * gain_query).astype(BF16)
    k_normed = (unit_rows(keys_in) * gain_key).astype(BF16)
    scores = jnp.dot(q_normed, k_normed.T, preferred_element_type=F32) / math.sqrt(
        queries.shape[-1]
    )
    probs = jax.nn.softmax(scores, axis=-1).astype(BF16)
    return jnp.dot(probs, values_in.astype(BF16), preferred_element_type=F32)


def smooth_gate(pre_act):
    return jax.nn.gelu(pre_act, approximate=False)


def inner_rows(left, right):
    return lax.dot_general(left, right, (((0,), (0,)), ((), ())), preferred_element_type=F32)


def cross_last(left, right):
    return lax.dot_general(left, right, (((1,), (1,)), ((), ())), preferred_element_type=F32)


def body(tokens, gain, w_qkv, qk_gain, w_up, w_attn_out, w_down, cotangent):
    mp, dp = lax.axis_index("mp"), lax.axis_index("dp")
    y, zh, core = mp // 8, mp // 2 % 4, mp % 2
    x, zl = dp // 2, dp % 2
    rows = tokens.shape[0]

    def gather_y_core(block):
        ring = gather4(block, shift_y, y)
        both = pair(ring, swap_core(ring), core)
        return jnp.transpose(both, (3, 1, 2, 0, 4)).reshape(block.shape[1], -1)

    def scatter_mp(full):
        halves = full.reshape(16, 2, -1, full.shape[1])
        away = lax.dynamic_index_in_dim(halves, 1 - core, 1, keepdims=False)
        mine = lax.dynamic_index_in_dim(halves, core, 1, keepdims=False)
        mine = (mine.astype(F32) + swap_core(away).astype(F32)).astype(BF16)
        ring = scatter4(mine.reshape(4, -1, full.shape[1]), shift_y, y).astype(BF16)
        return scatter4(ring.reshape(4, -1, full.shape[1]), shift_z, zh)

    def sum_mp(block):
        block = block + swap_core(block)
        return sum4(sum4(block, shift_y), shift_z)

    def gather_dp(block):
        two = pair(block, swap_z(block), zl)
        low, high = shift_x(two, 1), shift_x(two, -1)
        half = rows // 2
        far = jnp.concatenate(
            [shift_x(low[:, :half], 1), shift_x(high[:, half:], -1)], axis=1
        )
        return placed([two, high, far, low], x).reshape(8 * rows, -1)

    gain_rows = jnp.broadcast_to(gain[None, :], (16, HD))
    own = jnp.concatenate([tokens, gain_rows, cotangent])
    spread = lax.ppermute(jnp.concatenate([tokens, cotangent]), ("dp", "mp"), SPREAD)
    columns = lax.all_gather(spread, "mp", axis=0, tiled=False)
    columns = jnp.transpose(columns.reshape(8, 4, 2, rows, HD), (2, 0, 3, 1, 4))
    columns = columns.reshape(2, 8 * rows, 4 * HD)

    ring = gather4(own, shift_z, zh)
    full = gather_y_core(ring[:, : rows + 16])
    upstream = gather_y_core(ring[:, rows + 16 :])
    image, gain_all = full[:rows].astype(F32), full[rows].astype(F32)
    row_mean = jnp.mean(image, axis=1, keepdims=True)
    centred = image - row_mean
    inverse = lax.rsqrt(jnp.mean(centred * centred, axis=1, keepdims=True) + EPS)
    normed = (centred * inverse * gain_all).astype(BF16)

    up_pre = jnp.dot(normed, w_up, preferred_element_type=F32)
    projected = jnp.dot(normed, w_qkv, preferred_element_type=F32)
    activated, gate_back = jax.vjp(smooth_gate, up_pre)
    act_rows = activated.astype(BF16)
    queries, keys_in, values_in = (projected[:, k * HD : (k + 1) * HD] for k in range(3))
    attended, attn_back = jax.vjp(
        one_head, queries, keys_in, values_in, qk_gain[0], qk_gain[1]
    )
    att_rows = attended.astype(BF16)
    forward_all = gather_dp(jnp.concatenate([act_rows, att_rows], axis=1))
    branch = scatter_mp(
        (
            lax.dot_general(
                w_attn_out, att_rows, (((0,), (1,)), ((), ())), preferred_element_type=F32
            )
            + lax.dot_general(
                w_down, act_rows, (((0,), (1,)), ((), ())), preferred_element_type=F32
            )
        ).astype(BF16)
    )
    mixed = (tokens.astype(F32) + branch.T).astype(BF16)

    d_up = gate_back(cross_last(upstream, w_down))[0].astype(BF16)
    d_up_all = gather_dp(d_up)
    grad_q, grad_k, grad_v, grad_gq, grad_gk = attn_back(cross_last(upstream, w_attn_out))
    d_qkv = jnp.concatenate([grad_q, grad_k, grad_v], axis=1).astype(BF16)
    d_qkv_all = gather_dp(d_qkv)

    gain_up = jnp.dot(full[rows:], w_up, preferred_element_type=F32)[:1]
    gain_qkv = jnp.dot(full[rows:], w_qkv, preferred_element_type=F32)[:1]
    d_up_f, d_qkv_f = d_up.astype(F32), d_qkv.astype(F32)
    first_sum = jnp.sum(d_up_f * gain_up, axis=1) + jnp.sum(d_qkv_f * gain_qkv, axis=1)
    second_sum = jnp.sum(d_up_f * up_pre, axis=1) + jnp.sum(d_qkv_f * projected, axis=1)
    means = sum_mp(jnp.stack([first_sum, second_sum])) / D

    d_normed = scatter_mp((cross_last(w_qkv, d_qkv) + cross_last(w_up, d_up)).astype(BF16)).T
    unit_local = (tokens.astype(F32) - row_mean) * inverse
    scaled = d_normed * gain.astype(F32)
    d_tokens = (
        cotangent.astype(F32)
        + inverse * (scaled - means[0][:, None] - unit_local * means[1][:, None])
    ).astype(BF16)
    gain_term = jnp.sum(d_normed * unit_local, axis=0)
    scales = jnp.stack([gain_term, grad_gq, grad_gk])
    scales = sum4(scales + swap_z(scales), shift_x)

    stats = jnp.concatenate([row_mean, inverse], axis=1).T
    stats = placed(
        [
            s
            for two in [pair(stats, swap_z(stats), zl)]
            for s in (two, shift_x(two, -1), shift_x(two, 2), shift_x(two, 1))
        ],
        x,
    )
    stats = jnp.transpose(stats.reshape(8, 2, rows), (1, 0, 2)).reshape(2, 8 * rows, 1)
    gain_row = lax.dynamic_slice_in_dim(gain_all, dp * 4 * HD, 4 * HD)
    normed_cols = ((columns[0].astype(F32) - stats[0]) * stats[1] * gain_row).astype(BF16)
    upstream_cols = columns[1]
    ff = act_rows.shape[1]
    g_qkv = inner_rows(normed_cols, d_qkv_all).astype(BF16)
    g_up = inner_rows(normed_cols, d_up_all).astype(BF16)
    g_down = inner_rows(forward_all[:, :ff], upstream_cols).astype(BF16)
    g_attn_out = inner_rows(forward_all[:, ff:], upstream_cols).astype(BF16)
    return mixed, d_tokens, scales[0], scales[1:], g_qkv, g_up, g_attn_out, g_down


def solution(mesh):
    in_specs = (
        P("dp", "mp"),
        P("mp"),
        P(None, "mp"),
        P(None, "mp"),
        P(None, "mp"),
        P("mp", None),
        P("mp", None),
        P("dp", "mp"),
    )
    out_specs = (
        P("dp", "mp"),
        P("dp", "mp"),
        P("mp"),
        P(None, "mp"),
        P("dp", "mp"),
        P("dp", "mp"),
        P("mp", "dp"),
        P("mp", "dp"),
    )
    return jax.shard_map(body, mesh=mesh, in_specs=in_specs, out_specs=out_specs, check_vma=False)
```

```python
import functools
import math

import jax
import jax.numpy as jnp
from jax import lax
from jax.experimental import pallas as pl
from jax.experimental.pallas import tpu as pltpu
from jax.sharding import PartitionSpec as P

D = 4096
HD = 128
EPS = 1e-06
F32 = jnp.float32
BF16 = jnp.bfloat16


def mp_perm(dy, dz, dc):
    return [
        (
            (y * 4 + z) * 2 + c,
            ((y + dy) % 4 * 4 + (z + dz) % 4) * 2 + (c + dc) % 2,
        )
        for y in range(4)
        for z in range(4)
        for c in range(2)
    ]


def dp_perm(dx, dz):
    return [
        (x * 2 + z, (x + dx) % 4 * 2 + (z + dz) % 2) for x in range(4) for z in range(2)
    ]


SPREAD = [(i * 32 + m, m // 4 * 32 + i * 4 + m % 4) for i in range(8) for m in range(32)]


def shift_y(block, by):
    return lax.ppermute(block, "mp", mp_perm(by, 0, 0))


def shift_z(block, by):
    return lax.ppermute(block, "mp", mp_perm(0, by, 0))


def swap_core(block):
    return lax.ppermute(block, "mp", mp_perm(0, 0, 1))


def shift_x(block, by):
    return lax.ppermute(block, "dp", dp_perm(by, 0))


def swap_z(block):
    return lax.ppermute(block, "dp", dp_perm(0, 1))

MIB = 1 << 20
VMEM = pl.BlockSpec(memory_space=pltpu.VMEM)
SMEM = pl.BlockSpec(memory_space=pltpu.SMEM)
ANY = pl.BlockSpec(memory_space=pl.ANY)


def whole(kernel, out_shape, operands, scalars=0, extra=(), limit=40):
    n = len(operands)

    def run(*refs):
        kernel(*refs[:n], *refs[n + len(extra) :])

    specs = [SMEM] * scalars + [VMEM] * (n - scalars) + [ANY] * len(extra)
    return pl.pallas_call(
        run,
        out_shape=out_shape,
        in_specs=specs,
        out_specs=jax.tree.map(lambda _: VMEM, out_shape),
        compiler_params=pltpu.CompilerParams(vmem_limit_bytes=limit * MIB),
    )(*operands, *extra)


def place(pos, pieces, put):
    for core, rings in enumerate((pieces[:4], pieces[4:])):
        for dy, ring in enumerate(rings):
            for dz in range(4):
                index = ((pos[0] + dy) % 4 * 4 + (pos[1] + dz) % 4) * 2 + (pos[2] + core) % 2
                put(ring.at[dz], pl.multiple_of(index * HD, HD))


def norm_kernel(pos, *refs):
    *pieces, normed, mean_ref, inverse_ref, image = refs
    rows = image.shape[0]

    def put(block, at):
        image[:, pl.ds(at, HD)] = block[:rows]
        normed[rows:, pl.ds(at, HD)] = block[rows:]

    place(pos, pieces, put)
    step = 64
    for r in range(0, rows, step):
        values = image[r : r + step].astype(F32)
        mean = jnp.mean(values, axis=1, keepdims=True)
        centred = values - mean
        inverse = lax.rsqrt(jnp.mean(centred * centred, axis=1, keepdims=True) + EPS)
        gains = normed[rows : rows + 1].astype(F32)
        normed[r : r + step] = (centred * inverse * gains).astype(BF16)
        mean_ref[r : r + step] = mean
        inverse_ref[r : r + step] = inverse


def join_kernel(pos, *refs):
    *pieces, out = refs

    def put(block, at):
        out[:, pl.ds(at, HD)] = block[...]

    place(pos, pieces, put)


def split_kernel(pos, rows_ref, wa_ref, wb_ref, away, mine, *, transposed):
    na = wa_ref.shape[0] if not transposed else wa_ref.shape[1]
    for dz in range(4):
        at = pl.ds(pl.multiple_of((pos[1] + dz) % 4 * 256, 256), 256)
        if transposed:
            block = cross_last(rows_ref[:, :na], wa_ref[at, :]) + cross_last(
                rows_ref[:, na:], wb_ref[at, :]
            )
        else:
            block = jnp.dot(
                rows_ref[:, :na], wa_ref[:, at], preferred_element_type=F32
            ) + jnp.dot(rows_ref[:, na:], wb_ref[:, at], preferred_element_type=F32)
        block = block.astype(BF16)
        low, high = block[:, :HD], block[:, HD:]
        first = pos[2] == 0
        mine[0, dz] = jnp.where(first, low, high)
        away[0, dz] = jnp.where(first, high, low)


def split(pos, rows, wa, wb, transposed):
    n = rows.shape[0]

    def weight_spec(w):
        if transposed:
            return pl.BlockSpec((1024, w.shape[1]), lambda k, pos: ((pos[0] + k) % 4, 0))
        return pl.BlockSpec((w.shape[0], 1024), lambda k, pos: (0, (pos[0] + k) % 4))

    out = jax.ShapeDtypeStruct((4, 4, n, HD), BF16)
    out_spec = pl.BlockSpec((1, 4, n, HD), lambda k, pos: (k, 0, 0, 0))
    return pl.pallas_call(
        functools.partial(split_kernel, transposed=transposed),
        out_shape=(out, out),
        grid_spec=pltpu.PrefetchScalarGridSpec(
            num_scalar_prefetch=1,
            grid=(4,),
            in_specs=[
                pl.BlockSpec(rows.shape, lambda k, pos: (0, 0)),
                weight_spec(wa),
                weight_spec(wb),
            ],
            out_specs=(out_spec, out_spec),
        ),
        compiler_params=pltpu.CompilerParams(vmem_limit_bytes=24 * MIB),
    )(pos, rows, wa, wb)


def packed(sums):
    twice = jnp.concatenate([sums, sums])
    high = twice.astype(BF16).astype(F32)
    row = lax.broadcasted_iota(jnp.int32, twice.shape, 0)
    return jnp.where(row < 8, high, twice - high).astype(BF16)


def unpacked(rows):
    rows = rows.astype(F32)
    return rows[:8] + rows[8:]


def pair_sum_kernel(mine, came, *refs):
    n = mine.shape[2]
    outs = refs[-4:]
    for dy, out in enumerate(outs):
        for dz in range(4):
            both = mine[dy, dz].astype(F32) + came[dy, dz].astype(F32)
            out[dz * n : (dz + 1) * n] = both.astype(BF16)
        if len(refs) > 4:
            out[4 * n :] = packed(refs[0][...] + refs[1][...])


def ring_sum_kernel(*refs):
    parts, outs = refs[:4], refs[4:]
    n = outs[0].shape[0] // 256 * 256
    for dz, out in enumerate(outs):
        total = parts[0][dz * n : (dz + 1) * n].astype(F32)
        for part in parts[1:]:
            total = total + part[dz * n : (dz + 1) * n].astype(F32)
        out[:n] = total.astype(BF16)
        if out.shape[0] > n:
            sums = unpacked(parts[0][4 * n :])
            for part in parts[1:]:
                sums = sums + unpacked(part[4 * n :])
            out[n:] = packed(sums)


def columns_kernel(pos, block, mean, inverse, gains, normed, upstream):
    rows = mean.shape[1]
    for k in range(4):
        at = slice(k * HD, (k + 1) * HD)
        centred = block[0, k, :rows].astype(F32) - mean[0]
        scale = gains[:1, at].astype(F32)
        normed[:, at] = (centred * inverse[0] * scale).astype(BF16)
        upstream[:, at] = block[0, k, rows:]


def columns_of_images(pos, blocks, mean, inverse, gains):
    rows = mean.shape[1]
    width = 4 * HD

    def image(r, pos):
        return (pos[3] + r // 2) % 4 * 2 + (pos[4] + r) % 2

    out = jax.ShapeDtypeStruct((8 * rows, width), BF16)
    out_spec = pl.BlockSpec((rows, width), lambda r, pos: (r, 0))
    stat_spec = pl.BlockSpec((1, rows, 1), lambda r, pos: (r, 0, 0))
    return pl.pallas_call(
        columns_kernel,
        out_shape=(out, out),
        grid_spec=pltpu.PrefetchScalarGridSpec(
            num_scalar_prefetch=1,
            grid=(8,),
            in_specs=[
                pl.BlockSpec((1, 4, 2 * rows, HD), lambda r, pos: (image(r, pos), 0, 0, 0)),
                stat_spec,
                stat_spec,
                pl.BlockSpec((16, width), lambda r, pos: (rows // 16, pos[3] * 2 + pos[4])),
            ],
            out_specs=(out_spec, out_spec),
        ),
        compiler_params=pltpu.CompilerParams(vmem_limit_bytes=16 * MIB),
    )(pos, blocks, mean, inverse, gains)


def struct(*shape, kind=BF16):
    return jax.ShapeDtypeStruct(shape, kind)


def ring4(block, shift):
    return [block, shift(block, -1), shift(block, 2), shift(block, 1)]


def to_ring(messages, shift):
    return [messages[0], shift(messages[1], 1), shift(messages[2], 2), shift(messages[3], -1)]


def thirds(values):
    parts = []
    for _ in range(3):
        part = lax.reduce_precision(values, 8, 7)
        parts.append(part.astype(BF16))
        values = values - part
    return parts


def gather_dp(block):
    two = jnp.stack([block, swap_z(block)])
    low, high = shift_x(two, 1), shift_x(two, -1)
    far = [shift_x(low[0], 1), shift_x(high[1], -1)]
    return [two[0], two[1], high[0], high[1], *far, low[0], low[1]]


def unit_rows(block):
    centred = block - jnp.mean(block, axis=-1, keepdims=True)
    return centred * lax.rsqrt(jnp.mean(centred * centred, axis=-1, keepdims=True) + EPS)


def one_head(queries, keys_in, values_in, gain_query, gain_key):
    q_normed = (unit_rows(queries) * gain_query).astype(BF16)
    k_normed = (unit_rows(keys_in) * gain_key).astype(BF16)
    scores = jnp.dot(q_normed, k_normed.T, preferred_element_type=F32) / math.sqrt(
        queries.shape[-1]
    )
    probs = jax.nn.softmax(scores, axis=-1).astype(BF16)
    return jnp.dot(probs, values_in.astype(BF16), preferred_element_type=F32)


def smooth_gate(pre_act):
    return jax.nn.gelu(pre_act, approximate=False)


def inner_rows(left, right):
    return lax.dot_general(left, right, (((0,), (0,)), ((), ())), preferred_element_type=F32)


def cross_last(left, right):
    return lax.dot_general(left, right, (((1,), (1,)), ((), ())), preferred_element_type=F32)


def body(tokens, gain, w_qkv, qk_gain, w_up, w_attn_out, w_down, cotangent):
    mp, dp = lax.axis_index("mp"), lax.axis_index("dp")
    rows = tokens.shape[0]
    pos = jnp.stack([mp // 8, mp // 2 % 4, mp % 2, dp // 2, dp % 2]).astype(jnp.int32)

    own = jnp.concatenate([tokens, jnp.broadcast_to(gain[None, :], (16, HD)), cotangent])
    pieces = ring4(own, shift_z)
    cut = rows + 16
    tok_ring = jnp.stack([piece[:cut] for piece in pieces])
    cot_ring = jnp.stack([piece[cut:] for piece in pieces])
    tok_rings = ring4(tok_ring, shift_y)
    cot_ring, _ = lax.optimization_barrier((cot_ring, tok_rings[2]))
    spread = lax.ppermute(jnp.concatenate([tokens, cotangent]), ("dp", "mp"), SPREAD)
    cot_rings = ring4(cot_ring, shift_y)
    columns = lax.all_gather(spread, "mp", axis=0, tiled=False)

    normed, row_mean, inverse, _ = whole(
        norm_kernel,
        (
            struct(cut, D),
            struct(rows, 1, kind=F32),
            struct(rows, 1, kind=F32),
            struct(rows, D),
        ),
        [pos, *tok_rings, *(swap_core(ring) for ring in tok_rings)],
        scalars=1,
        extra=(spread,),
    )

    up_all = jnp.dot(normed, w_up, preferred_element_type=F32)
    qkv_all = jnp.dot(normed, w_qkv, preferred_element_type=F32)
    up_pre, projected = up_all[:rows], qkv_all[:rows]
    gain_up, gain_qkv = up_all[rows : rows + 1], qkv_all[rows : rows + 1]
    activated, gate_back = jax.vjp(smooth_gate, up_pre)
    queries, keys_in, values_in = (projected[:, k * HD : (k + 1) * HD] for k in range(3))
    attended, attn_back = jax.vjp(
        one_head, queries, keys_in, values_in, qk_gain[0], qk_gain[1]
    )
    forward = jnp.concatenate([activated, attended], axis=1).astype(BF16)
    ff = activated.shape[1]
    stats = jnp.stack(thirds(row_mean[:, 0]) + thirds(inverse[:, 0])).reshape(3, -1)
    stats = jnp.pad(stats, ((0, 13), (0, 0)))
    forward_all = gather_dp(jnp.concatenate([forward, stats]))

    away, mine = split(pos, forward, w_down, w_attn_out, transposed=False)
    messages = whole(
        pair_sum_kernel, [struct(4 * rows, HD)] * 4, [mine, swap_core(away)]
    )
    messages = whole(
        ring_sum_kernel, [struct(rows, HD)] * 4, to_ring(messages, shift_y)
    )
    branch = sum(part.astype(F32) for part in to_ring(messages, shift_z))
    mixed = (tokens.astype(F32) + branch).astype(BF16)

    upstream = whole(
        join_kernel,
        struct(rows, D),
        [pos, *cot_rings, *(swap_core(ring) for ring in cot_rings)],
        scalars=1,
    )
    d_up = gate_back(cross_last(upstream, w_down))[0].astype(BF16)
    grad_q, grad_k, grad_v, grad_gq, grad_gk = attn_back(cross_last(upstream, w_attn_out))
    d_cat = jnp.concatenate(
        [grad_q.astype(BF16), grad_k.astype(BF16), grad_v.astype(BF16), d_up], axis=1
    )
    d_all = gather_dp(d_cat)

    d_f = d_cat.astype(F32)
    pre = jnp.concatenate([projected, up_pre], axis=1)
    gain_pre = jnp.concatenate([gain_qkv, gain_up], axis=1)
    sums = jnp.stack([jnp.sum(d_f * gain_pre, axis=1), jnp.sum(d_f * pre, axis=1)])
    sums = jnp.pad(sums.reshape(-1, HD), ((0, 8 - 2 * rows // HD), (0, 0)))

    away, mine = split(pos, d_cat, w_qkv, w_up, transposed=True)
    messages = whole(
        pair_sum_kernel,
        [struct(4 * rows + 16, HD)] * 4,
        [mine, swap_core(away), sums, swap_core(sums)],
    )
    messages = whole(
        ring_sum_kernel, [struct(rows + 16, HD)] * 4, to_ring(messages, shift_y)
    )
    parts = [part.astype(F32) for part in to_ring(messages, shift_z)]
    total = sum(parts)
    d_normed = total[:rows]
    means = (total[rows : rows + 8] + total[rows + 8 :])[: 2 * rows // HD] / D
    means = means.reshape(2, rows, 1)
    unit_local = (tokens.astype(F32) - row_mean) * inverse
    scaled = d_normed * gain.astype(F32)
    d_tokens = (
        cotangent.astype(F32) + inverse * (scaled - means[0] - unit_local * means[1])
    ).astype(BF16)
    gain_term = jnp.sum(d_normed * unit_local, axis=0)
    scales = jnp.stack([gain_term, grad_gq, grad_gk])
    scales = sum(ring4(scales + swap_z(scales), shift_x))

    stats = jnp.stack([piece[rows : rows + 3] for piece in forward_all]).astype(F32)
    stats = jnp.sum(stats.reshape(8, 2, 3, rows), axis=2)
    normed_cols, upstream_cols = columns_of_images(
        pos,
        columns.reshape(8, 4, 2 * rows, HD),
        stats[:, 0].reshape(8, rows, 1),
        stats[:, 1].reshape(8, rows, 1),
        normed,
    )
    forward_all = jnp.concatenate([piece[:rows] for piece in forward_all])
    g_forward = inner_rows(forward_all, upstream_cols).astype(BF16)
    g_back = inner_rows(normed_cols, jnp.concatenate(d_all)).astype(BF16)
    return (
        mixed,
        d_tokens,
        scales[0],
        scales[1:],
        g_back[:, : 3 * HD],
        g_back[:, 3 * HD :],
        g_forward[ff:],
        g_forward[:ff],
    )


def solution(mesh):
    in_specs = (
        P("dp", "mp"),
        P("mp"),
        P(None, "mp"),
        P(None, "mp"),
        P(None, "mp"),
        P("mp", None),
        P("mp", None),
        P("dp", "mp"),
    )
    out_specs = (
        P("dp", "mp"),
        P("dp", "mp"),
        P("mp"),
        P(None, "mp"),
        P("dp", "mp"),
        P("dp", "mp"),
        P("mp", "dp"),
        P("mp", "dp"),
    )
    return jax.shard_map(body, mesh=mesh, in_specs=in_specs, out_specs=out_specs, check_vma=False)
```

```python
import functools
import math

import jax
import jax.numpy as jnp
from jax import lax
from jax.experimental import pallas as pl
from jax.experimental.pallas import tpu as pltpu
from jax.sharding import PartitionSpec as P

D = 4096
HD = 128
EPS = 1e-06
F32 = jnp.float32
BF16 = jnp.bfloat16


def mp_perm(dy, dz, dc):
    return [
        (
            (y * 4 + z) * 2 + c,
            ((y + dy) % 4 * 4 + (z + dz) % 4) * 2 + (c + dc) % 2,
        )
        for y in range(4)
        for z in range(4)
        for c in range(2)
    ]


def dp_perm(dx, dz):
    return [
        (x * 2 + z, (x + dx) % 4 * 2 + (z + dz) % 2) for x in range(4) for z in range(2)
    ]


SPREAD = [(i * 32 + m, m // 4 * 32 + i * 4 + m % 4) for i in range(8) for m in range(32)]


def shift_y(block, by):
    return lax.ppermute(block, "mp", mp_perm(by, 0, 0))


def shift_z(block, by):
    return lax.ppermute(block, "mp", mp_perm(0, by, 0))


def swap_core(block):
    return lax.ppermute(block, "mp", mp_perm(0, 0, 1))


def shift_x(block, by):
    return lax.ppermute(block, "dp", dp_perm(by, 0))


def swap_z(block):
    return lax.ppermute(block, "dp", dp_perm(0, 1))


MIB = 1 << 20
VMEM = pl.BlockSpec(memory_space=pltpu.VMEM)
SMEM = pl.BlockSpec(memory_space=pltpu.SMEM)
ANY = pl.BlockSpec(memory_space=pl.ANY)


def struct(*shape, kind=BF16):
    return jax.ShapeDtypeStruct(shape, kind)


def cost(us):
    return pl.CostEstimate(flops=0, bytes_accessed=int(us * 3.5e6), transcendentals=0)


def whole(kernel, out_shape, operands, us, scalars=0, extra=(), limit=16, scratch=()):
    n = len(operands)

    def run(*refs):
        kernel(*refs[:n], *refs[n + len(extra) :])

    specs = [SMEM] * scalars + [VMEM] * (n - scalars) + [ANY] * len(extra)
    return pl.pallas_call(
        run,
        out_shape=out_shape,
        in_specs=specs,
        out_specs=jax.tree.map(lambda _: VMEM, out_shape),
        scratch_shapes=scratch,
        cost_estimate=cost(us),
        compiler_params=pltpu.CompilerParams(vmem_limit_bytes=limit * MIB),
    )(*operands, *extra)


def inner_rows(left, right):
    return lax.dot_general(left, right, (((0,), (0,)), ((), ())), preferred_element_type=F32)


def cross_last(left, right):
    return lax.dot_general(left, right, (((1,), (1,)), ((), ())), preferred_element_type=F32)


def mean_last(block):
    return jnp.mean(block, axis=-1, keepdims=True)


def as_columns(first, second):
    lane = lax.broadcasted_iota(jnp.int32, (first.shape[0], HD), 1)
    return jnp.where(lane == 0, first, jnp.where(lane == 1, second, 0.0))


def as_rows(columns):
    return jnp.transpose(columns)[:8]


def from_rows(rows):
    pad = jnp.zeros((HD - 8, rows.shape[1]), F32)
    return jnp.transpose(jnp.concatenate([rows, pad]))


def rounded(values):
    return values.astype(BF16).astype(F32)


def stacked(upper, lower):
    twice = jnp.concatenate([upper, lower])
    return twice.astype(BF16)


def packed(rows):
    high = rounded(rows)
    return stacked(high, rows - high)


def unpacked(rows):
    rows = rows.astype(F32)
    return rows[:8] + rows[8:]


def unit_rows(block):
    centred = block - mean_last(block)
    inverse = lax.rsqrt(mean_last(centred * centred) + EPS)
    return centred * inverse, inverse


def unit_rows_back(unit, inverse, grad):
    return inverse * (grad - mean_last(grad) - unit * mean_last(grad * unit))


def place(pos, pieces, put):
    for core, rings in enumerate((pieces[:4], pieces[4:])):
        for dy, ring in enumerate(rings):
            for dz in range(4):
                index = ((pos[0] + dy) % 4 * 4 + (pos[1] + dz) % 4) * 2 + (pos[2] + core) % 2
                put(ring.at[dz], pl.multiple_of(index * HD, HD))


def cut_kernel(*refs):
    pieces, (tok, cot) = refs[:4], refs[4:]
    n = tok.shape[1]
    for k, piece in enumerate(pieces):
        tok[k] = piece[:n]
        cot[k] = piece[n:]


def forward_kernel(pos, *refs):
    pieces, (w_qkv, w_up, qk_gain), outs = refs[:8], refs[8:11], refs[11:]
    message, pre, probs_ref, stats_ref, gains, normed, image = outs
    rows = image.shape[0]
    ff = w_up.shape[1]

    def put(block, at):
        image[:, pl.ds(at, HD)] = block[:rows]
        normed[rows:, pl.ds(at, HD)] = block[rows:]

    place(pos, pieces, put)
    step = 64
    for r in range(0, rows, step):
        values = image[r : r + step].astype(F32)
        mean = mean_last(values)
        centred = values - mean
        inverse = lax.rsqrt(mean_last(centred * centred) + EPS)
        scale = normed[rows : rows + 1].astype(F32)
        normed[r : r + step] = (centred * inverse * scale).astype(BF16)
        stats_ref[r : r + step] = as_columns(mean, inverse)
    gains[...] = normed[rows:]
    stats = as_rows(stats_ref[...])
    high = rounded(stats)
    middle = rounded(stats - high)
    message[rows:, :rows] = stacked(high, middle)
    message[rows:, rows:] = stacked(stats - high - middle, jnp.zeros_like(stats))

    pre[:, : 3 * HD] = jnp.dot(normed[...], w_qkv[...], preferred_element_type=F32)
    pre[:, 3 * HD :] = jnp.dot(normed[...], w_up[...], preferred_element_type=F32)
    up = pre[:rows, 3 * HD :]
    message[:rows, :ff] = (0.5 * up * (1.0 + lax.erf(up * math.sqrt(0.5)))).astype(BF16)
    q_normed = (unit_rows(pre[:rows, :HD])[0] * qk_gain[0:1]).astype(BF16)
    k_normed = (unit_rows(pre[:rows, HD : 2 * HD])[0] * qk_gain[1:2]).astype(BF16)
    scores = cross_last(q_normed, k_normed) / math.sqrt(HD)
    powers = jnp.exp(scores - jnp.max(scores, axis=-1, keepdims=True))
    probs = powers / jnp.sum(powers, axis=-1, keepdims=True)
    probs_ref[...] = probs
    values_in = pre[:rows, 2 * HD : 3 * HD].astype(BF16)
    message[:rows, ff:] = jnp.dot(
        probs.astype(BF16), values_in, preferred_element_type=F32
    ).astype(BF16)


def backward_kernel(pos, *refs):
    pieces, (w_out, w_down, pre, probs_ref, qk_gain), outs = refs[:8], refs[8:13], refs[13:]
    d_cat, sums, scales, upstream = outs
    rows = upstream.shape[0]

    def put(block, at):
        upstream[:, pl.ds(at, HD)] = block[...]

    place(pos, pieces, put)
    d_att = cross_last(upstream[...], w_out[...]).astype(BF16)
    d_act = cross_last(upstream[...], w_down[...])
    up = pre[:rows, 3 * HD :]
    slope = 0.5 * (1.0 + lax.erf(up * math.sqrt(0.5))) + up * jnp.exp(-0.5 * up * up) * (
        1.0 / math.sqrt(2.0 * math.pi)
    )
    d_cat[:, 3 * HD :] = (d_act * slope).astype(BF16)

    unit_q, inverse_q = unit_rows(pre[:rows, :HD])
    unit_k, inverse_k = unit_rows(pre[:rows, HD : 2 * HD])
    q_normed = (unit_q * qk_gain[0:1]).astype(BF16)
    k_normed = (unit_k * qk_gain[1:2]).astype(BF16)
    values_in = pre[:rows, 2 * HD : 3 * HD].astype(BF16)
    probs = probs_ref[...]
    d_cat[:, 2 * HD : 3 * HD] = inner_rows(probs.astype(BF16), d_att).astype(BF16)
    d_probs = rounded(cross_last(d_att, values_in))
    d_scores = probs * (d_probs - jnp.sum(d_probs * probs, axis=-1, keepdims=True))
    d_scores = (d_scores / math.sqrt(HD)).astype(BF16)
    d_q = rounded(jnp.dot(d_scores, k_normed, preferred_element_type=F32))
    d_k = rounded(inner_rows(d_scores, q_normed))
    d_cat[:, :HD] = unit_rows_back(unit_q, inverse_q, d_q * qk_gain[0:1]).astype(BF16)
    d_cat[:, HD : 2 * HD] = unit_rows_back(unit_k, inverse_k, d_k * qk_gain[1:2]).astype(BF16)
    scales[0:1] = jnp.sum(d_q * unit_q, axis=0, keepdims=True)
    scales[1:2] = jnp.sum(d_k * unit_k, axis=0, keepdims=True)

    values = d_cat[...].astype(F32)
    first = jnp.sum(values * pre[rows : rows + 1], axis=1, keepdims=True)
    second = jnp.sum(values * pre[:rows], axis=1, keepdims=True)
    sums[...] = as_rows(as_columns(first, second))


def split_kernel(pos, rows_ref, wa_ref, wb_ref, away, mine, *, transposed):
    na = wa_ref.shape[0] if not transposed else wa_ref.shape[1]
    for dz in range(4):
        at = pl.ds(pl.multiple_of((pos[1] + dz) % 4 * 256, 256), 256)
        if transposed:
            block = cross_last(rows_ref[:, :na], wa_ref[at, :]) + cross_last(
                rows_ref[:, na:], wb_ref[at, :]
            )
        else:
            block = jnp.dot(
                rows_ref[:, :na], wa_ref[:, at], preferred_element_type=F32
            ) + jnp.dot(rows_ref[:, na:], wb_ref[:, at], preferred_element_type=F32)
        block = block.astype(BF16)
        low, high = block[:, :HD], block[:, HD:]
        first = pos[2] == 0
        mine[0, dz] = jnp.where(first, low, high)
        away[0, dz] = jnp.where(first, high, low)


def split(pos, rows, wa, wb, transposed):
    n = rows.shape[0]

    def weight_spec(w):
        if transposed:
            return pl.BlockSpec((1024, w.shape[1]), lambda k, pos: ((pos[0] + k) % 4, 0))
        return pl.BlockSpec((w.shape[0], 1024), lambda k, pos: (0, (pos[0] + k) % 4))

    out = jax.ShapeDtypeStruct((4, 4, n, HD), BF16)
    out_spec = pl.BlockSpec((1, 4, n, HD), lambda k, pos: (k, 0, 0, 0))
    return pl.pallas_call(
        functools.partial(split_kernel, transposed=transposed),
        out_shape=(out, out),
        grid_spec=pltpu.PrefetchScalarGridSpec(
            num_scalar_prefetch=1,
            grid=(4,),
            in_specs=[
                pl.BlockSpec(rows.shape, lambda k, pos: (0, 0)),
                weight_spec(wa),
                weight_spec(wb),
            ],
            out_specs=(out_spec, out_spec),
        ),
        cost_estimate=cost(4),
        compiler_params=pltpu.CompilerParams(vmem_limit_bytes=16 * MIB),
    )(pos, rows, wa, wb)

def pair_sum_kernel(mine, came, *refs):
    n = mine.shape[2]
    outs = refs[-4:]
    for dy, out in enumerate(outs):
        for dz in range(4):
            both = mine[dy, dz].astype(F32) + came[dy, dz].astype(F32)
            out[dz * n : (dz + 1) * n] = both.astype(BF16)
        if len(refs) > 4:
            both = packed(refs[0][...] + refs[1][...])
            out[4 * n : 4 * n + 16] = both[:, :HD]
            out[4 * n + 16 :] = both[:, HD:]


def tail_sums(parts, n):
    total = None
    for part in parts:
        one = jnp.concatenate([unpacked(part[n : n + 16]), unpacked(part[n + 16 :])], axis=1)
        total = one if total is None else total + one
    return total


def ring_sum_kernel(*refs):
    parts, outs = refs[:4], refs[4:]
    n = outs[0].shape[0] // 256 * 256
    for dz, out in enumerate(outs):
        total = parts[0][dz * n : (dz + 1) * n].astype(F32)
        for part in parts[1:]:
            total = total + part[dz * n : (dz + 1) * n].astype(F32)
        out[:n] = total.astype(BF16)
        if out.shape[0] > n:
            both = packed(tail_sums(parts, 4 * n))
            out[n : n + 16] = both[:, :HD]
            out[n + 16 :] = both[:, HD:]


def finish_kernel(*refs):
    parts, (tokens, cotangent, gain, stats, d_scales, d_tokens, scales) = refs[:4], refs[4:]
    n = tokens.shape[0]
    d_normed = parts[0][:n].astype(F32)
    for part in parts[1:]:
        d_normed = d_normed + part[:n].astype(F32)
    means = from_rows(tail_sums(parts, n)) / D
    mean, inverse = stats[:, 0:1], stats[:, 1:2]
    unit = (tokens[...].astype(F32) - mean) * inverse
    scaled = d_normed * gain[...].astype(F32)
    d_tokens[...] = (
        cotangent[...].astype(F32) + inverse * (scaled - means[:, 0:1] - unit * means[:, 1:2])
    ).astype(BF16)
    scales[...] = jnp.zeros_like(scales)
    scales[0:1] = jnp.sum(d_normed * unit, axis=0, keepdims=True)
    scales[1:3] = d_scales[...]


def image_of(pos, r):
    return (pos[3] + r // 2) % 4 * 2 + (pos[4] + r) % 2


def forward_grads_kernel(pos, columns, gains, *refs):
    pieces, (g_out, g_down, normed, rows_all, upstream) = refs[:8], refs[8:]
    rows = columns.shape[2] // 2
    ff = g_down.shape[0]
    width = 4 * HD
    at = pl.multiple_of((pos[3] * 2 + pos[4]) * width, width)
    scale = gains[0:1, pl.ds(at, width)].astype(F32)
    for r, piece in enumerate(pieces):
        here = slice(r * rows, (r + 1) * rows)
        rows_all[here] = piece[:rows]
        tail = piece[rows:].astype(F32)
        stats = from_rows(tail[:8, :rows] + tail[8:, :rows] + tail[:8, rows:])
        mean, inverse = stats[:, 0:1], stats[:, 1:2]
        image = image_of(pos, r)
        for k in range(4):
            lanes = slice(k * HD, (k + 1) * HD)
            centred = columns[image, k, :rows].astype(F32) - mean
            normed[here, lanes] = (centred * inverse * scale[:, lanes]).astype(BF16)
            upstream[here, lanes] = columns[image, k, rows:]
    g_down[...] = inner_rows(rows_all[:, :ff], upstream[...]).astype(BF16)
    g_out[...] = inner_rows(rows_all[:, ff:], upstream[...]).astype(BF16)


def backward_grads_kernel(normed, *refs):
    pieces, (g_qkv, g_up, d_all) = refs[:8], refs[8:]
    rows = pieces[0].shape[0]
    for r, piece in enumerate(pieces):
        d_all[r * rows : (r + 1) * rows] = piece[...]
    grads = inner_rows(normed[...], d_all[...]).astype(BF16)
    g_qkv[...] = grads[:, : 3 * HD]
    g_up[...] = grads[:, 3 * HD :]


def ring4(block, shift):
    return [block, shift(block, -1), shift(block, 2), shift(block, 1)]


def to_ring(messages, shift):
    return [messages[0], shift(messages[1], 1), shift(messages[2], 2), shift(messages[3], -1)]


def gather_dp(block):
    other = swap_z(block)
    low, high = shift_x(block, 1), shift_x(block, -1)
    low_other, high_other = shift_x(other, 1), shift_x(other, -1)
    far, far_other = shift_x(low, 1), shift_x(high_other, -1)
    return [block, other, high, high_other, far, far_other, low, low_other]


def body(tokens, gain, w_qkv, qk_gain, w_up, w_attn_out, w_down, cotangent):
    mp, dp = lax.axis_index("mp"), lax.axis_index("dp")
    rows, ff = tokens.shape[0], w_up.shape[1]
    pos = jnp.stack([mp // 8, mp // 2 % 4, mp % 2, dp // 2, dp % 2]).astype(jnp.int32)

    own = jnp.concatenate([tokens, jnp.broadcast_to(gain[None, :], (16, HD)), cotangent])
    cut = rows + 16
    tok_ring, cot_ring = whole(
        cut_kernel, (struct(4, cut, HD), struct(4, rows, HD)), ring4(own, shift_z), 1
    )
    tok_rings = ring4(tok_ring, shift_y)
    cot_ring, _ = lax.optimization_barrier((cot_ring, tok_rings[2]))
    spread = lax.ppermute(jnp.concatenate([tokens, cotangent]), ("dp", "mp"), SPREAD)
    cot_rings = ring4(cot_ring, shift_y)
    columns = lax.all_gather(spread, "mp", axis=0, tiled=False)

    forward, pre, probs, stats, gains = whole(
        forward_kernel,
        (
            struct(cut, ff + HD),
            struct(cut, 3 * HD + ff, kind=F32),
            struct(rows, rows, kind=F32),
            struct(rows, HD, kind=F32),
            struct(16, D),
        ),
        [pos, *tok_rings, *(swap_core(ring) for ring in tok_rings), w_qkv, w_up, qk_gain],
        12,
        scalars=1,
        limit=32,
        scratch=[pltpu.VMEM((cut, D), BF16), pltpu.VMEM((rows, D), BF16)],
    )
    forward_all = gather_dp(forward)

    away, mine = split(pos, forward[:rows], w_down, w_attn_out, transposed=False)
    branch_messages = whole(
        pair_sum_kernel, [struct(4 * rows, HD)] * 4, [mine, swap_core(away)], 1
    )
    messages = whole(
        ring_sum_kernel, [struct(rows, HD)] * 4, to_ring(branch_messages, shift_y), 1
    )
    branch = sum(part.astype(F32) for part in to_ring(messages, shift_z))
    mixed = (tokens.astype(F32) + branch).astype(BF16)

    d_cat, sums, d_scales = whole(
        backward_kernel,
        (struct(rows, 3 * HD + ff), struct(8, rows, kind=F32), struct(2, HD, kind=F32)),
        [
            pos,
            *cot_rings,
            *(swap_core(ring) for ring in cot_rings),
            w_attn_out,
            w_down,
            pre,
            probs,
            qk_gain,
        ],
        10,
        scalars=1,
        limit=32,
        scratch=[pltpu.VMEM((rows, D), BF16)],
        extra=(branch_messages[1],),
    )
    d_all = gather_dp(d_cat)
    away, mine = split(pos, d_cat, w_qkv, w_up, transposed=True)
    messages = whole(
        pair_sum_kernel,
        [struct(4 * rows + 32, HD)] * 4,
        [mine, swap_core(away), sums, swap_core(sums)],
        1,
    )
    messages = whole(
        ring_sum_kernel, [struct(rows + 32, HD)] * 4, to_ring(messages, shift_y), 1
    )
    d_tokens, scales = whole(
        finish_kernel,
        (struct(rows, HD), struct(8, HD, kind=F32)),
        [*to_ring(messages, shift_z), tokens, cotangent, gain[None, :], stats, d_scales],
        1,
    )
    scales = sum(ring4(scales + swap_z(scales), shift_x))

    g_attn_out, g_down, normed = whole(
        forward_grads_kernel,
        (struct(HD, 4 * HD), struct(ff, 4 * HD), struct(8 * rows, 4 * HD)),
        [pos, columns.reshape(8, 4, 2 * rows, HD), gains, *forward_all],
        6,
        scalars=1,
        limit=32,
        scratch=[pltpu.VMEM((8 * rows, ff + HD), BF16), pltpu.VMEM((8 * rows, 4 * HD), BF16)],
    )
    g_qkv, g_up = whole(
        backward_grads_kernel,
        (struct(4 * HD, 3 * HD), struct(4 * HD, ff)),
        [normed, *d_all],
        6,
        limit=32,
        scratch=[pltpu.VMEM((8 * rows, 3 * HD + ff), BF16)],
    )
    return mixed, d_tokens, scales[0], scales[1:3], g_qkv, g_up, g_attn_out, g_down


def solution(mesh):
    in_specs = (
        P("dp", "mp"),
        P("mp"),
        P(None, "mp"),
        P(None, "mp"),
        P(None, "mp"),
        P("mp", None),
        P("mp", None),
        P("dp", "mp"),
    )
    out_specs = (
        P("dp", "mp"),
        P("dp", "mp"),
        P("mp"),
        P(None, "mp"),
        P("dp", "mp"),
        P("dp", "mp"),
        P("mp", "dp"),
        P("mp", "dp"),
    )
    return jax.shard_map(body, mesh=mesh, in_specs=in_specs, out_specs=out_specs, check_vma=False)
```

```python
import functools
import math

import jax
import jax.numpy as jnp
from jax import lax
from jax.experimental import pallas as pl
from jax.experimental.pallas import tpu as pltpu
from jax.sharding import PartitionSpec as P

D = 4096
HD = 128
EPS = 1e-06
F32 = jnp.float32
BF16 = jnp.bfloat16


def mp_perm(dy, dz, dc):
    return [
        (
            (y * 4 + z) * 2 + c,
            ((y + dy) % 4 * 4 + (z + dz) % 4) * 2 + (c + dc) % 2,
        )
        for y in range(4)
        for z in range(4)
        for c in range(2)
    ]


def dp_perm(dx, dz):
    return [
        (x * 2 + z, (x + dx) % 4 * 2 + (z + dz) % 2) for x in range(4) for z in range(2)
    ]


SPREAD = [(i * 32 + m, m // 4 * 32 + i * 4 + m % 4) for i in range(8) for m in range(32)]


def shift_y(block, by):
    return lax.ppermute(block, "mp", mp_perm(by, 0, 0))


def shift_z(block, by):
    return lax.ppermute(block, "mp", mp_perm(0, by, 0))


def swap_core(block):
    return lax.ppermute(block, "mp", mp_perm(0, 0, 1))


def shift_x(block, by):
    return lax.ppermute(block, "dp", dp_perm(by, 0))


def swap_z(block):
    return lax.ppermute(block, "dp", dp_perm(0, 1))


MIB = 1 << 20
VMEM = pl.BlockSpec(memory_space=pltpu.VMEM)
SMEM = pl.BlockSpec(memory_space=pltpu.SMEM)
ANY = pl.BlockSpec(memory_space=pl.ANY)


def struct(*shape, kind=BF16):
    return jax.ShapeDtypeStruct(shape, kind)


def cost(us):
    return pl.CostEstimate(flops=0, bytes_accessed=int(us * 3.5e6), transcendentals=0)


def whole(kernel, out_shape, operands, us, scalars=0, extra=(), limit=16, scratch=()):
    n = len(operands)

    def run(*refs):
        kernel(*refs[:n], *refs[n + len(extra) :])

    specs = [SMEM] * scalars + [VMEM] * (n - scalars) + [ANY] * len(extra)
    return pl.pallas_call(
        run,
        out_shape=out_shape,
        in_specs=specs,
        out_specs=jax.tree.map(lambda _: VMEM, out_shape),
        scratch_shapes=scratch,
        cost_estimate=cost(us),
        compiler_params=pltpu.CompilerParams(vmem_limit_bytes=limit * MIB),
    )(*operands, *extra)


def inner_rows(left, right):
    return lax.dot_general(left, right, (((0,), (0,)), ((), ())), preferred_element_type=F32)


def cross_last(left, right):
    return lax.dot_general(left, right, (((1,), (1,)), ((), ())), preferred_element_type=F32)


def mean_last(block):
    return jnp.mean(block, axis=-1, keepdims=True)


def as_columns(first, second):
    lane = lax.broadcasted_iota(jnp.int32, (first.shape[0], HD), 1)
    return jnp.where(lane == 0, first, jnp.where(lane == 1, second, 0.0))


def as_rows(columns):
    return jnp.transpose(columns)[:8]


def from_rows(rows):
    pad = jnp.zeros((HD - 8, rows.shape[1]), F32)
    return jnp.transpose(jnp.concatenate([rows, pad]))


def rounded(values):
    return values.astype(BF16).astype(F32)


def stacked(upper, lower):
    twice = jnp.concatenate([upper, lower])
    return twice.astype(BF16)


def packed(rows):
    high = rounded(rows)
    return stacked(high, rows - high)


def unpacked(rows):
    rows = rows.astype(F32)
    return rows[:8] + rows[8:]


def unit_rows(block):
    centred = block - mean_last(block)
    inverse = lax.rsqrt(mean_last(centred * centred) + EPS)
    return centred * inverse, inverse


def unit_rows_back(unit, inverse, grad):
    return inverse * (grad - mean_last(grad) - unit * mean_last(grad * unit))


def place(pos, pieces, put):
    for core, rings in enumerate((pieces[:4], pieces[4:])):
        for dy, ring in enumerate(rings):
            for dz in range(4):
                index = ((pos[0] + dy) % 4 * 4 + (pos[1] + dz) % 4) * 2 + (pos[2] + core) % 2
                put(ring.at[dz], pl.multiple_of(index * HD, HD))


def stack_kernel(*refs):
    pieces, (out,) = refs[:4], refs[4:]
    for k, piece in enumerate(pieces):
        out[k] = piece[...]


def layer_kernel(pos, *refs):
    pieces, weights, (qk_gain, *outs) = refs[:8], refs[8:12], refs[12:]
    message, sums, scales, stats_ref, gains, *scratch = outs
    image, normed, pre, *held, sems = scratch
    rows = image.shape[0]
    cut = normed.shape[0]
    w_qkv, w_up, w_out, w_down = held
    ff = w_up.shape[1]
    copies = [
        pltpu.make_async_copy(weight, place, sems.at[k])
        for k, (weight, place) in enumerate(zip(weights, held))
    ]
    for copy in copies:
        copy.start()

    def put_tokens(block, at):
        image[:, pl.ds(at, HD)] = block[:rows]
        normed[rows:, pl.ds(at, HD)] = block[rows:cut]

    def put_cotangent(block, at):
        image[:, pl.ds(at, HD)] = block[cut:]

    place(pos, pieces, put_tokens)
    step = 64
    for r in range(0, rows, step):
        values = image[r : r + step].astype(F32)
        mean = mean_last(values)
        centred = values - mean
        inverse = lax.rsqrt(mean_last(centred * centred) + EPS)
        scale = normed[rows : rows + 1].astype(F32)
        normed[r : r + step] = (centred * inverse * scale).astype(BF16)
        stats_ref[r : r + step] = as_columns(mean, inverse)
    gains[...] = normed[rows:]
    stats = as_rows(stats_ref[...])
    high = rounded(stats)
    middle = rounded(stats - high)
    message[rows:, :rows] = stacked(high, middle)
    message[rows:, rows : 2 * rows] = stacked(stats - high - middle, jnp.zeros_like(stats))
    message[rows:, 2 * rows :] = jnp.zeros((cut - rows, message.shape[1] - 2 * rows), BF16)

    copies[0].wait()
    pre[:, : 3 * HD] = jnp.dot(normed[...], w_qkv[...], preferred_element_type=F32)
    copies[1].wait()
    pre[:, 3 * HD :] = jnp.dot(normed[...], w_up[...], preferred_element_type=F32)
    place(pos, pieces, put_cotangent)
    up = pre[:rows, 3 * HD :]
    below = 0.5 * (1.0 + lax.erf(up * math.sqrt(0.5)))
    message[:rows, :ff] = (up * below).astype(BF16)
    unit_q, inverse_q = unit_rows(pre[:rows, :HD])
    unit_k, inverse_k = unit_rows(pre[:rows, HD : 2 * HD])
    q_normed = (unit_q * qk_gain[0:1]).astype(BF16)
    k_normed = (unit_k * qk_gain[1:2]).astype(BF16)
    values_in = pre[:rows, 2 * HD : 3 * HD].astype(BF16)
    scores = cross_last(q_normed, k_normed) / math.sqrt(HD)
    powers = jnp.exp(scores - jnp.max(scores, axis=-1, keepdims=True))
    probs = powers / jnp.sum(powers, axis=-1, keepdims=True)
    message[:rows, ff : ff + HD] = jnp.dot(
        probs.astype(BF16), values_in, preferred_element_type=F32
    ).astype(BF16)

    d_qkv = message.at[:rows, ff + HD : ff + 4 * HD]
    copies[2].wait()
    d_att = cross_last(image[...], w_out[...]).astype(BF16)
    copies[3].wait()
    d_act = cross_last(image[...], w_down[...])
    slope = below + up * jnp.exp(-0.5 * up * up) * (1.0 / math.sqrt(2.0 * math.pi))
    message[:rows, ff + 4 * HD :] = (d_act * slope).astype(BF16)
    d_qkv[:, 2 * HD :] = inner_rows(probs.astype(BF16), d_att).astype(BF16)
    d_probs = rounded(cross_last(d_att, values_in))
    d_scores = probs * (d_probs - jnp.sum(d_probs * probs, axis=-1, keepdims=True))
    d_scores = (d_scores / math.sqrt(HD)).astype(BF16)
    d_q = rounded(jnp.dot(d_scores, k_normed, preferred_element_type=F32))
    d_k = rounded(inner_rows(d_scores, q_normed))
    d_qkv[:, :HD] = unit_rows_back(unit_q, inverse_q, d_q * qk_gain[0:1]).astype(BF16)
    d_qkv[:, HD : 2 * HD] = unit_rows_back(unit_k, inverse_k, d_k * qk_gain[1:2]).astype(BF16)
    scales[0:1] = jnp.sum(d_q * unit_q, axis=0, keepdims=True)
    scales[1:2] = jnp.sum(d_k * unit_k, axis=0, keepdims=True)

    values = message[:rows, ff + HD :].astype(F32)
    first = jnp.sum(values * pre[rows : rows + 1], axis=1, keepdims=True)
    second = jnp.sum(values * pre[:rows], axis=1, keepdims=True)
    sums[...] = as_rows(as_columns(first, second))


def split_kernel(pos, message, w_down, w_out, w_qkv, w_up, away, mine):
    rows, ff = away.shape[2], w_down.shape[0]
    first = pos[2] == 0

    def put(at, block):
        block = block.astype(BF16)
        low, high = block[:, :HD], block[:, HD:]
        mine[0, at] = jnp.where(first, low, high)
        away[0, at] = jnp.where(first, high, low)

    for dz in range(4):
        at = pl.ds(pl.multiple_of((pos[1] + dz) % 4 * 256, 256), 256)
        put(
            dz,
            jnp.dot(message[:rows, :ff], w_down[:, at], preferred_element_type=F32)
            + jnp.dot(
                message[:rows, ff : ff + HD], w_out[:, at], preferred_element_type=F32
            ),
        )
        put(
            4 + dz,
            cross_last(message[:rows, ff + HD : ff + 4 * HD], w_qkv[at, :])
            + cross_last(message[:rows, ff + 4 * HD :], w_up[at, :]),
        )


def split(pos, message, w_down, w_out, w_qkv, w_up):
    rows = message.shape[0] // 256 * 256

    def over_columns(w):
        return pl.BlockSpec((w.shape[0], 1024), lambda k, pos: (0, (pos[0] + k) % 4))

    def over_rows(w):
        return pl.BlockSpec((1024, w.shape[1]), lambda k, pos: ((pos[0] + k) % 4, 0))

    out = struct(4, 8, rows, HD)
    out_spec = pl.BlockSpec((1, 8, rows, HD), lambda k, pos: (k, 0, 0, 0))
    return pl.pallas_call(
        split_kernel,
        out_shape=(out, out),
        grid_spec=pltpu.PrefetchScalarGridSpec(
            num_scalar_prefetch=1,
            grid=(4,),
            in_specs=[
                pl.BlockSpec(message.shape, lambda k, pos: (0, 0)),
                over_columns(w_down),
                over_columns(w_out),
                over_rows(w_qkv),
                over_rows(w_up),
            ],
            out_specs=(out_spec, out_spec),
        ),
        cost_estimate=cost(7),
        compiler_params=pltpu.CompilerParams(vmem_limit_bytes=24 * MIB),
    )(pos, message, w_down, w_out, w_qkv, w_up)


def pair_sum_kernel(mine, came, sums, sums_came, *outs):
    n = mine.shape[2]
    tail = packed(sums[...] + sums_came[...])
    for dy, out in enumerate(outs):
        for at in range(8):
            both = mine[dy, at].astype(F32) + came[dy, at].astype(F32)
            out[at * n : (at + 1) * n] = both.astype(BF16)
        out[8 * n : 8 * n + 16] = tail[:, :HD]
        out[8 * n + 16 :] = tail[:, HD:]


def tail_sums(parts, n):
    total = None
    for part in parts:
        one = jnp.concatenate([unpacked(part[n : n + 16]), unpacked(part[n + 16 :])], axis=1)
        total = one if total is None else total + one
    return total


def ring_sum_kernel(*refs):
    parts, outs = refs[:4], refs[4:]
    n = (outs[0].shape[0] - 32) // 2
    tail = packed(tail_sums(parts, 8 * n))
    for dz, out in enumerate(outs):
        for half in range(2):
            at = slice((half * 4 + dz) * n, (half * 4 + dz + 1) * n)
            total = parts[0][at].astype(F32)
            for part in parts[1:]:
                total = total + part[at].astype(F32)
            out[half * n : (half + 1) * n] = total.astype(BF16)
        out[2 * n : 2 * n + 16] = tail[:, :HD]
        out[2 * n + 16 :] = tail[:, HD:]


def finish_kernel(*refs):
    parts, (tokens, cotangent, gain, stats, d_scales, mixed, d_tokens, scales) = refs[:4], refs[4:]
    n = tokens.shape[0]
    branch = parts[0][:n].astype(F32)
    d_normed = parts[0][n : 2 * n].astype(F32)
    for part in parts[1:]:
        branch = branch + part[:n].astype(F32)
        d_normed = d_normed + part[n : 2 * n].astype(F32)
    image = tokens[...].astype(F32)
    mixed[...] = (image + branch).astype(BF16)
    means = from_rows(tail_sums(parts, 2 * n)) / D
    mean, inverse = stats[:, 0:1], stats[:, 1:2]
    unit = (image - mean) * inverse
    scaled = d_normed * gain[...].astype(F32)
    d_tokens[...] = (
        cotangent[...].astype(F32) + inverse * (scaled - means[:, 0:1] - unit * means[:, 1:2])
    ).astype(BF16)
    scales[...] = jnp.zeros_like(scales)
    scales[0:1] = jnp.sum(d_normed * unit, axis=0, keepdims=True)
    scales[1:3] = d_scales[...]


def image_of(pos, r):
    return (pos[3] + r // 2) % 4 * 2 + (pos[4] + r) % 2


def grads_kernel(pos, gains, columns, *refs):
    pieces, (g_out, g_down, g_qkv, g_up, *scratch) = refs[:8], refs[8:]
    held, tails, blocks, normed, upstream, sems = scratch
    rows = blocks.shape[2] // 2
    ff = g_down.shape[0]
    width = 4 * HD
    copies = []
    for r, piece in enumerate(pieces):
        here = slice(r * rows, (r + 1) * rows)
        copies.append(
            [
                pltpu.make_async_copy(piece.at[rows:], tails.at[r], sems.at[0, r]),
                pltpu.make_async_copy(
                    columns.at[image_of(pos, r)], blocks.at[r], sems.at[1, r]
                ),
                pltpu.make_async_copy(piece.at[:rows], held.at[here], sems.at[2, r]),
            ]
        )
        for copy in copies[-1]:
            copy.start()
    at = pl.multiple_of((pos[3] * 2 + pos[4]) * width, width)
    scale = gains[0:1, pl.ds(at, width)].astype(F32)
    for r in range(8):
        here = slice(r * rows, (r + 1) * rows)
        for copy in copies[r]:
            copy.wait()
        tail = tails[r].astype(F32)
        stats = from_rows(
            tail[:8, :rows] + tail[8:, :rows] + tail[:8, rows : 2 * rows]
        )
        mean, inverse = stats[:, 0:1], stats[:, 1:2]
        for k in range(4):
            lanes = slice(k * HD, (k + 1) * HD)
            centred = blocks[r, k, :rows].astype(F32) - mean
            normed[here, lanes] = (centred * inverse * scale[:, lanes]).astype(BF16)
            upstream[here, lanes] = blocks[r, k, rows:]
    g_down[...] = inner_rows(held[:, :ff], upstream[...]).astype(BF16)
    g_out[...] = inner_rows(held[:, ff : ff + HD], upstream[...]).astype(BF16)
    g_qkv[...] = inner_rows(normed[...], held[:, ff + HD : ff + 4 * HD]).astype(BF16)
    g_up[...] = inner_rows(normed[...], held[:, ff + 4 * HD :]).astype(BF16)


def ring4(block, shift):
    return [block, shift(block, -1), shift(block, 2), shift(block, 1)]


def to_ring(messages, shift):
    return [messages[0], shift(messages[1], 1), shift(messages[2], 2), shift(messages[3], -1)]


def gather_dp(block):
    other = swap_z(block)
    low, high = shift_x(block, 1), shift_x(block, -1)
    low_other, high_other = shift_x(other, 1), shift_x(other, -1)
    far, far_other = shift_x(low, 1), shift_x(high_other, -1)
    return [block, other, high, high_other, far, far_other, low, low_other]


def body(tokens, gain, w_qkv, qk_gain, w_up, w_attn_out, w_down, cotangent):
    mp, dp = lax.axis_index("mp"), lax.axis_index("dp")
    rows, ff = tokens.shape[0], w_up.shape[1]
    pos = jnp.stack([mp // 8, mp // 2 % 4, mp % 2, dp // 2, dp % 2]).astype(jnp.int32)

    own = jnp.concatenate([tokens, jnp.broadcast_to(gain[None, :], (16, HD)), cotangent])
    cut, both = rows + 16, 2 * rows + 16
    ring = whole(stack_kernel, struct(4, both, HD), ring4(own, shift_z), 1)
    spread = lax.ppermute(jnp.concatenate([tokens, cotangent]), ("dp", "mp"), SPREAD)
    columns = lax.all_gather(spread, "mp", axis=0, tiled=False)
    rings = ring4(ring, shift_y)

    width = 2 * ff + 4 * HD
    hbm, vmem = [ANY] * 4, [VMEM] * 8
    message, sums, d_scales, stats, gains = pl.pallas_call(
        layer_kernel,
        out_shape=(
            struct(cut, width),
            struct(8, rows, kind=F32),
            struct(2, HD, kind=F32),
            struct(rows, HD, kind=F32),
            struct(16, D),
        ),
        in_specs=[SMEM, *vmem, *hbm, VMEM],
        out_specs=[VMEM] * 5,
        scratch_shapes=[
            pltpu.VMEM((rows, D), BF16),
            pltpu.VMEM((cut, D), BF16),
            pltpu.VMEM((cut, 3 * HD + ff), F32),
            *(pltpu.VMEM(w.shape, BF16) for w in (w_qkv, w_up, w_attn_out, w_down)),
            pltpu.SemaphoreType.DMA((4,)),
        ],
        cost_estimate=cost(10),
        compiler_params=pltpu.CompilerParams(vmem_limit_bytes=40 * MIB),
    )(
        pos,
        *rings,
        *(swap_core(ring) for ring in rings),
        w_qkv,
        w_up,
        w_attn_out,
        w_down,
        qk_gain,
    )
    images = gather_dp(message)

    away, mine = split(pos, message, w_down, w_attn_out, w_qkv, w_up)
    messages = whole(
        pair_sum_kernel,
        [struct(8 * rows + 32, HD)] * 4,
        [mine, swap_core(away), sums, swap_core(sums)],
        1,
        limit=24,
    )
    messages = whole(
        ring_sum_kernel,
        [struct(2 * rows + 32, HD)] * 4,
        to_ring(messages, shift_y),
        1,
        extra=(images[3], images[7]),
    )
    mixed, d_tokens, scales = whole(
        finish_kernel,
        (struct(rows, HD), struct(rows, HD), struct(8, HD, kind=F32)),
        [*to_ring(messages, shift_z), tokens, cotangent, gain[None, :], stats, d_scales],
        1,
    )
    scales = sum(ring4(scales + swap_z(scales), shift_x))

    g_attn_out, g_down, g_qkv, g_up = pl.pallas_call(
        grads_kernel,
        out_shape=(
            struct(HD, 4 * HD),
            struct(ff, 4 * HD),
            struct(4 * HD, 3 * HD),
            struct(4 * HD, ff),
        ),
        in_specs=[SMEM, VMEM, *[ANY] * 9],
        out_specs=[VMEM] * 4,
        scratch_shapes=[
            pltpu.VMEM((8 * rows, width), BF16),
            pltpu.VMEM((8, 16, width), BF16),
            pltpu.VMEM((8, 4, 2 * rows, HD), BF16),
            pltpu.VMEM((8 * rows, 4 * HD), BF16),
            pltpu.VMEM((8 * rows, 4 * HD), BF16),
            pltpu.SemaphoreType.DMA((3, 8)),
        ],
        cost_estimate=cost(8),
        compiler_params=pltpu.CompilerParams(vmem_limit_bytes=40 * MIB),
    )(pos, gains, columns.reshape(8, 4, 2 * rows, HD), *images)
    return mixed, d_tokens, scales[0], scales[1:3], g_qkv, g_up, g_attn_out, g_down


def solution(mesh):
    in_specs = (
        P("dp", "mp"),
        P("mp"),
        P(None, "mp"),
        P(None, "mp"),
        P(None, "mp"),
        P("mp", None),
        P("mp", None),
        P("dp", "mp"),
    )
    out_specs = (
        P("dp", "mp"),
        P("dp", "mp"),
        P("mp"),
        P(None, "mp"),
        P("dp", "mp"),
        P("dp", "mp"),
        P("mp", "dp"),
        P("mp", "dp"),
    )
    return jax.shard_map(body, mesh=mesh, in_specs=in_specs, out_specs=out_specs, check_vma=False)
```

```python
import functools
import math

import jax
import jax.numpy as jnp
from jax import lax
from jax.experimental import pallas as pl
from jax.experimental.pallas import tpu as pltpu
from jax.sharding import PartitionSpec as P

D = 4096
HD = 128
EPS = 1e-06
F32 = jnp.float32
BF16 = jnp.bfloat16


def mp_perm(dy, dz, dc):
    return [
        (
            (y * 4 + z) * 2 + c,
            ((y + dy) % 4 * 4 + (z + dz) % 4) * 2 + (c + dc) % 2,
        )
        for y in range(4)
        for z in range(4)
        for c in range(2)
    ]


def dp_perm(dx, dz):
    return [
        (x * 2 + z, (x + dx) % 4 * 2 + (z + dz) % 2) for x in range(4) for z in range(2)
    ]


SPREAD = [(i * 32 + m, m // 4 * 32 + i * 4 + m % 4) for i in range(8) for m in range(32)]


def shift_y(block, by):
    return lax.ppermute(block, "mp", mp_perm(by, 0, 0))


def shift_z(block, by):
    return lax.ppermute(block, "mp", mp_perm(0, by, 0))


def swap_core(block):
    return lax.ppermute(block, "mp", mp_perm(0, 0, 1))


def shift_x(block, by):
    return lax.ppermute(block, "dp", dp_perm(by, 0))


def swap_z(block):
    return lax.ppermute(block, "dp", dp_perm(0, 1))


MIB = 1 << 20
VMEM = pl.BlockSpec(memory_space=pltpu.VMEM)
SMEM = pl.BlockSpec(memory_space=pltpu.SMEM)
ANY = pl.BlockSpec(memory_space=pl.ANY)
HBM = pl.BlockSpec(memory_space=pltpu.HBM)


def struct(*shape, kind=BF16):
    return jax.ShapeDtypeStruct(shape, kind)


def cost(us):
    return pl.CostEstimate(flops=0, bytes_accessed=int(us * 3.5e6), transcendentals=0)


def whole(kernel, out_shape, operands, us, scalars=0, extra=(), limit=16, scratch=()):
    n = len(operands)

    def run(*refs):
        kernel(*refs[:n], *refs[n + len(extra) :])

    specs = [SMEM] * scalars + [VMEM] * (n - scalars) + [ANY] * len(extra)
    return pl.pallas_call(
        run,
        out_shape=out_shape,
        in_specs=specs,
        out_specs=jax.tree.map(lambda _: VMEM, out_shape),
        scratch_shapes=scratch,
        cost_estimate=cost(us),
        compiler_params=pltpu.CompilerParams(vmem_limit_bytes=limit * MIB),
    )(*operands, *extra)


def inner_rows(left, right):
    return lax.dot_general(left, right, (((0,), (0,)), ((), ())), preferred_element_type=F32)


def cross_last(left, right):
    return lax.dot_general(left, right, (((1,), (1,)), ((), ())), preferred_element_type=F32)


def mean_last(block):
    return jnp.mean(block, axis=-1, keepdims=True)


def as_columns(first, second):
    lane = lax.broadcasted_iota(jnp.int32, (first.shape[0], HD), 1)
    return jnp.where(lane == 0, first, jnp.where(lane == 1, second, 0.0))


def as_rows(columns):
    return jnp.transpose(columns)[:8]


def from_rows(rows):
    pad = jnp.zeros((HD - 8, rows.shape[1]), F32)
    return jnp.transpose(jnp.concatenate([rows, pad]))


def rounded(values):
    return values.astype(BF16).astype(F32)


def stacked(upper, lower):
    twice = jnp.concatenate([upper, lower])
    return twice.astype(BF16)


def packed(rows):
    high = rounded(rows)
    return stacked(high, rows - high)


def unpacked(rows):
    rows = rows.astype(F32)
    return rows[:8] + rows[8:]


def unit_rows(block):
    centred = block - mean_last(block)
    inverse = lax.rsqrt(mean_last(centred * centred) + EPS)
    return centred * inverse, inverse


def unit_rows_back(unit, inverse, grad):
    return inverse * (grad - mean_last(grad) - unit * mean_last(grad * unit))


def place(pos, pieces, put):
    for core, rings in enumerate(pieces):
        for dy in range(4):
            for dz in range(4):
                index = ((pos[0] + dy) % 4 * 4 + (pos[1] + dz) % 4) * 2 + (pos[2] + core) % 2
                put(rings.at[dy, dz], pl.multiple_of(index * HD, HD))


def stack_kernel(*refs):
    pieces, (out,) = refs[:4], refs[4:]
    for k, piece in enumerate(pieces):
        out[k] = piece[...]


def layer_kernel(pos, *refs):
    pieces, weights, (qk_gain, *outs) = refs[:2], refs[2:6], refs[6:]
    away, mine, message, sums, scales, stats_ref, gains, *scratch = outs
    image, normed, pre, *held, sems = scratch
    rows = image.shape[0]
    cut = normed.shape[0]
    w_qkv, w_up, w_out, w_down = held
    ff = w_up.shape[1]
    copies = [
        pltpu.make_async_copy(weight, place, sems.at[k])
        for k, (weight, place) in enumerate(zip(weights, held))
    ]
    for copy in copies:
        copy.start()

    def put_tokens(block, at):
        image[:, pl.ds(at, HD)] = block[:rows]
        normed[rows:, pl.ds(at, HD)] = block[rows:cut]

    def put_cotangent(block, at):
        image[:, pl.ds(at, HD)] = block[cut:]

    place(pos, pieces, put_tokens)
    step = 64
    for r in range(0, rows, step):
        values = image[r : r + step].astype(F32)
        mean = mean_last(values)
        centred = values - mean
        inverse = lax.rsqrt(mean_last(centred * centred) + EPS)
        scale = normed[rows : rows + 1].astype(F32)
        normed[r : r + step] = (centred * inverse * scale).astype(BF16)
        stats_ref[r : r + step] = as_columns(mean, inverse)
    gains[...] = normed[rows:]
    stats = as_rows(stats_ref[...])
    high = rounded(stats)
    middle = rounded(stats - high)
    message[rows:, :rows] = stacked(high, middle)
    message[rows:, rows : 2 * rows] = stacked(stats - high - middle, jnp.zeros_like(stats))
    message[rows:, 2 * rows :] = jnp.zeros((cut - rows, message.shape[1] - 2 * rows), BF16)

    copies[0].wait()
    pre[:, : 3 * HD] = jnp.dot(normed[...], w_qkv[...], preferred_element_type=F32)
    copies[1].wait()
    pre[:, 3 * HD :] = jnp.dot(normed[...], w_up[...], preferred_element_type=F32)
    place(pos, pieces, put_cotangent)
    up = pre[:rows, 3 * HD :]
    below = 0.5 * (1.0 + lax.erf(up * math.sqrt(0.5)))
    message[:rows, :ff] = (up * below).astype(BF16)
    unit_q, inverse_q = unit_rows(pre[:rows, :HD])
    unit_k, inverse_k = unit_rows(pre[:rows, HD : 2 * HD])
    q_normed = (unit_q * qk_gain[0:1]).astype(BF16)
    k_normed = (unit_k * qk_gain[1:2]).astype(BF16)
    values_in = pre[:rows, 2 * HD : 3 * HD].astype(BF16)
    scores = cross_last(q_normed, k_normed) / math.sqrt(HD)
    powers = jnp.exp(scores - jnp.max(scores, axis=-1, keepdims=True))
    probs = powers / jnp.sum(powers, axis=-1, keepdims=True)
    message[:rows, ff : ff + HD] = jnp.dot(
        probs.astype(BF16), values_in, preferred_element_type=F32
    ).astype(BF16)

    d_qkv = message.at[:rows, ff + HD : ff + 4 * HD]
    copies[2].wait()
    d_att = cross_last(image[...], w_out[...]).astype(BF16)
    copies[3].wait()
    d_act = cross_last(image[...], w_down[...])
    slope = below + up * jnp.exp(-0.5 * up * up) * (1.0 / math.sqrt(2.0 * math.pi))
    message[:rows, ff + 4 * HD :] = (d_act * slope).astype(BF16)
    d_qkv[:, 2 * HD :] = inner_rows(probs.astype(BF16), d_att).astype(BF16)
    d_probs = rounded(cross_last(d_att, values_in))
    d_scores = probs * (d_probs - jnp.sum(d_probs * probs, axis=-1, keepdims=True))
    d_scores = (d_scores / math.sqrt(HD)).astype(BF16)
    d_q = rounded(jnp.dot(d_scores, k_normed, preferred_element_type=F32))
    d_k = rounded(inner_rows(d_scores, q_normed))
    d_qkv[:, :HD] = unit_rows_back(unit_q, inverse_q, d_q * qk_gain[0:1]).astype(BF16)
    d_qkv[:, HD : 2 * HD] = unit_rows_back(unit_k, inverse_k, d_k * qk_gain[1:2]).astype(BF16)
    scales[0:1] = jnp.sum(d_q * unit_q, axis=0, keepdims=True)
    scales[1:2] = jnp.sum(d_k * unit_k, axis=0, keepdims=True)

    values = message[:rows, ff + HD :].astype(F32)
    first = jnp.sum(values * pre[rows : rows + 1], axis=1, keepdims=True)
    second = jnp.sum(values * pre[:rows], axis=1, keepdims=True)
    sums[...] = as_rows(as_columns(first, second))

    tail = packed(sums[...])
    away[32 * rows : 32 * rows + 16] = tail[:, :HD]
    away[32 * rows + 16 :] = tail[:, HD:]
    mine_first = pos[2] == 0

    def put(dy, at, block):
        block = block.astype(BF16)
        low, high = block[:, :HD], block[:, HD:]
        mine[dy, at] = jnp.where(mine_first, low, high)
        start = (dy * 8 + at) * rows
        away[start : start + rows] = jnp.where(mine_first, high, low)

    for dy in range(4):
        for dz in range(4):
            index = (pos[0] + dy) % 4 * 4 + (pos[1] + dz) % 4
            at = pl.ds(pl.multiple_of(index * 256, 256), 256)
            put(
                dy,
                dz,
                jnp.dot(message[:rows, :ff], w_down[:, at], preferred_element_type=F32)
                + jnp.dot(
                    message[:rows, ff : ff + HD], w_out[:, at], preferred_element_type=F32
                ),
            )
            put(
                dy,
                4 + dz,
                cross_last(message[:rows, ff + HD : ff + 4 * HD], w_qkv[at, :])
                + cross_last(message[:rows, ff + 4 * HD :], w_up[at, :]),
            )


def pair_sum_kernel(mine, came, sums, message, other, *refs):
    shares, (*outs, two, columns) = refs[:4], refs[4:]
    two[0] = message[...]
    two[1] = other[...]
    for dy, share in enumerate(shares):
        columns[dy] = share[...]
    n = mine.shape[2]
    tail = packed(sums[...] + tail_sums([came], 32 * n))
    for dy, out in enumerate(outs):
        for at in range(8):
            start = (dy * 8 + at) * n
            both = mine[dy, at].astype(F32) + came[start : start + n].astype(F32)
            out[at * n : (at + 1) * n] = both.astype(BF16)
        out[8 * n : 8 * n + 16] = tail[:, :HD]
        out[8 * n + 16 :] = tail[:, HD:]


def tail_sums(parts, n):
    total = None
    for part in parts:
        one = jnp.concatenate([unpacked(part[n : n + 16]), unpacked(part[n + 16 :])], axis=1)
        total = one if total is None else total + one
    return total


def ring_sum_kernel(*refs):
    parts, outs = refs[:4], refs[4:]
    n = (outs[0].shape[0] - 32) // 2
    tail = packed(tail_sums(parts, 8 * n))
    for dz, out in enumerate(outs):
        for half in range(2):
            at = slice((half * 4 + dz) * n, (half * 4 + dz + 1) * n)
            total = parts[0][at].astype(F32)
            for part in parts[1:]:
                total = total + part[at].astype(F32)
            out[half * n : (half + 1) * n] = total.astype(BF16)
        out[2 * n : 2 * n + 16] = tail[:, :HD]
        out[2 * n + 16 :] = tail[:, HD:]


def finish_kernel(*refs):
    parts, (tokens, cotangent, gain, stats, d_scales, mixed, d_tokens, scales) = refs[:4], refs[4:]
    n = tokens.shape[0]
    branch = parts[0][:n].astype(F32)
    d_normed = parts[0][n : 2 * n].astype(F32)
    for part in parts[1:]:
        branch = branch + part[:n].astype(F32)
        d_normed = d_normed + part[n : 2 * n].astype(F32)
    image = tokens[...].astype(F32)
    mixed[...] = (image + branch).astype(BF16)
    means = from_rows(tail_sums(parts, 2 * n)) / D
    mean, inverse = stats[:, 0:1], stats[:, 1:2]
    unit = (image - mean) * inverse
    scaled = d_normed * gain[...].astype(F32)
    d_tokens[...] = (
        cotangent[...].astype(F32) + inverse * (scaled - means[:, 0:1] - unit * means[:, 1:2])
    ).astype(BF16)
    scales[...] = jnp.zeros_like(scales)
    scales[0:1] = jnp.sum(d_normed * unit, axis=0, keepdims=True)
    scales[1:3] = d_scales[...]


def image_of(pos, r):
    return (pos[3] + r // 2) % 4 * 2 + (pos[4] + r) % 2


def grads_kernel(pos, gains, columns, columns_other, *refs):
    (two, high, far, far_other, low), _, (g_out, g_down, g_qkv, g_up, *scratch) = (
        refs[:5],
        refs[5],
        refs[6:],
    )
    pieces = [two.at[0], two.at[1], high.at[0], high.at[1], far, far_other, low.at[0], low.at[1]]
    held, tails, blocks, others, normed, upstream, sems = scratch
    rows = blocks.shape[2] // 2
    ff = g_down.shape[0]
    width = 4 * HD
    copies = []
    for r, piece in enumerate(pieces):
        here = slice(r * rows, (r + 1) * rows)
        moves = [(piece.at[rows:], tails.at[r]), (piece.at[:rows], held.at[here])]
        for k in range(2):
            index = image_of(pos, r) * 2 + k
            dy, dz = (index // 4 + 4 - pos[0]) % 4, (index % 4 + 4 - pos[1]) % 4
            moves.append((columns.at[dy, dz], blocks.at[r, k]))
            moves.append((columns_other.at[dy, dz], others.at[r, k]))
        copies.append(
            [
                pltpu.make_async_copy(src, dst, sems.at[k, r])
                for k, (src, dst) in enumerate(moves)
            ]
        )
        for copy in copies[-1]:
            copy.start()
    first = pl.multiple_of((pos[3] * 2 + pos[4]) * width, width)
    for r in range(8):
        here = slice(r * rows, (r + 1) * rows)
        for copy in copies[r]:
            copy.wait()
        tail = tails[r].astype(F32)
        stats = from_rows(
            tail[:8, :rows] + tail[8:, :rows] + tail[:8, rows : 2 * rows]
        )
        mean, inverse = stats[:, 0:1], stats[:, 1:2]
        for core, came in enumerate((blocks, others)):
            for k in range(2):
                at = pl.multiple_of((2 * k + (pos[2] + core) % 2) * HD, HD)
                centred = came[r, k, :rows].astype(F32) - mean
                scale = gains[0:1, pl.ds(first + at, HD)].astype(F32)
                normed[here, pl.ds(at, HD)] = (centred * inverse * scale).astype(BF16)
                upstream[here, pl.ds(at, HD)] = came[r, k, rows:]
    g_down[...] = inner_rows(held[:, :ff], upstream[...]).astype(BF16)
    g_out[...] = inner_rows(held[:, ff : ff + HD], upstream[...]).astype(BF16)
    g_qkv[...] = inner_rows(normed[...], held[:, ff + HD : ff + 4 * HD]).astype(BF16)
    g_up[...] = inner_rows(normed[...], held[:, ff + 4 * HD :]).astype(BF16)


def ring4(block, shift):
    return [block, shift(block, -1), shift(block, 2), shift(block, 1)]


def to_ring(messages, shift):
    return [messages[0], shift(messages[1], 1), shift(messages[2], 2), shift(messages[3], -1)]


def body(tokens, gain, w_qkv, qk_gain, w_up, w_attn_out, w_down, cotangent):
    mp, dp = lax.axis_index("mp"), lax.axis_index("dp")
    rows, ff = tokens.shape[0], w_up.shape[1]
    pos = jnp.stack([mp // 8, mp // 2 % 4, mp % 2, dp // 2, dp % 2]).astype(jnp.int32)

    own = jnp.concatenate([tokens, jnp.broadcast_to(gain[None, :], (16, HD)), cotangent])
    cut, both = rows + 16, 2 * rows + 16
    spread = lax.ppermute(jnp.concatenate([tokens, cotangent]), ("dp", "mp"), SPREAD)
    ring = whole(
        stack_kernel, struct(4, both, HD), ring4(own, shift_z), 1, extra=(spread,)
    )
    share_ring = whole(
        stack_kernel, struct(4, 2 * rows, HD), ring4(spread, shift_z), 1, extra=(ring,)
    )
    rings = whole(
        stack_kernel,
        struct(4, 4, both, HD),
        ring4(ring, shift_y),
        1,
        extra=(share_ring,),
    )
    share_rings = ring4(share_ring, shift_y)

    width = 2 * ff + 4 * HD
    hbm, vmem = [HBM] * 4, [VMEM] * 2
    away, mine, message, sums, d_scales, stats, gains = pl.pallas_call(
        layer_kernel,
        out_shape=(
            struct(32 * rows + 32, HD),
            struct(4, 8, rows, HD),
            struct(cut, width),
            struct(8, rows, kind=F32),
            struct(2, HD, kind=F32),
            struct(rows, HD, kind=F32),
            struct(16, D),
        ),
        in_specs=[SMEM, *vmem, *hbm, VMEM],
        out_specs=[VMEM] * 7,
        scratch_shapes=[
            pltpu.VMEM((rows, D), BF16),
            pltpu.VMEM((cut, D), BF16),
            pltpu.VMEM((cut, 3 * HD + ff), F32),
            *(pltpu.VMEM(w.shape, BF16) for w in (w_qkv, w_up, w_attn_out, w_down)),
            pltpu.SemaphoreType.DMA((4,)),
        ],
        cost_estimate=cost(15),
        compiler_params=pltpu.CompilerParams(vmem_limit_bytes=44 * MIB),
    )(
        pos,
        rings,
        swap_core(rings),
        w_qkv,
        w_up,
        w_attn_out,
        w_down,
        qk_gain,
    )
    *messages, two, columns = whole(
        pair_sum_kernel,
        [struct(8 * rows + 32, HD)] * 4
        + [struct(2, *message.shape), struct(4, 4, 2 * rows, HD)],
        [mine, swap_core(away), sums, message, swap_z(message), *share_rings],
        1,
        limit=32,
    )
    low, high = shift_x(two, 1), shift_x(two, -1)
    messages = whole(
        ring_sum_kernel,
        [struct(2 * rows + 32, HD)] * 4,
        to_ring(messages, shift_y),
        1,
        extra=(low, high),
    )
    (ahead, back), _ = lax.optimization_barrier(((low[0], high[1]), messages[0]))
    images = [two, high, shift_x(ahead, 1), shift_x(back, -1), low]
    mixed, d_tokens, scales = whole(
        finish_kernel,
        (struct(rows, HD), struct(rows, HD), struct(8, HD, kind=F32)),
        [*to_ring(messages, shift_z), tokens, cotangent, gain[None, :], stats, d_scales],
        1,
        extra=tuple(images[2:4]),
    )
    columns, _ = lax.optimization_barrier((columns, mixed))
    columns_other = swap_core(columns)
    scales = scales + swap_z(scales)

    g_attn_out, g_down, g_qkv, g_up = pl.pallas_call(
        grads_kernel,
        out_shape=(
            struct(HD, 4 * HD),
            struct(ff, 4 * HD),
            struct(4 * HD, 3 * HD),
            struct(4 * HD, ff),
        ),
        in_specs=[SMEM, VMEM, HBM, ANY, *[HBM] * 5, ANY],
        out_specs=[VMEM] * 4,
        scratch_shapes=[
            pltpu.VMEM((8 * rows, width), BF16),
            pltpu.VMEM((8, 16, width), BF16),
            pltpu.VMEM((8, 2, 2 * rows, HD), BF16),
            pltpu.VMEM((8, 2, 2 * rows, HD), BF16),
            pltpu.VMEM((8 * rows, 4 * HD), BF16),
            pltpu.VMEM((8 * rows, 4 * HD), BF16),
            pltpu.SemaphoreType.DMA((6, 8)),
        ],
        cost_estimate=cost(8),
        compiler_params=pltpu.CompilerParams(vmem_limit_bytes=40 * MIB),
    )(pos, gains, columns, columns_other, *images, scales)
    scales = sum(ring4(scales, shift_x))
    return mixed, d_tokens, scales[0], scales[1:3], g_qkv, g_up, g_attn_out, g_down


def solution(mesh):
    in_specs = (
        P("dp", "mp"),
        P("mp"),
        P(None, "mp"),
        P(None, "mp"),
        P(None, "mp"),
        P("mp", None),
        P("mp", None),
        P("dp", "mp"),
    )
    out_specs = (
        P("dp", "mp"),
        P("dp", "mp"),
        P("mp"),
        P(None, "mp"),
        P("dp", "mp"),
        P("dp", "mp"),
        P("mp", "dp"),
        P("mp", "dp"),
    )
    return jax.shard_map(body, mesh=mesh, in_specs=in_specs, out_specs=out_specs, check_vma=False)
```

```python
import functools
import math

import jax
import jax.numpy as jnp
from jax import lax
from jax.experimental import pallas as pl
from jax.experimental.pallas import tpu as pltpu
from jax.sharding import PartitionSpec as P

D = 4096
HD = 128
EPS = 1e-06
F32 = jnp.float32
BF16 = jnp.bfloat16


def mp_perm(dy, dz, dc):
    return [
        (
            (y * 4 + z) * 2 + c,
            ((y + dy) % 4 * 4 + (z + dz) % 4) * 2 + (c + dc) % 2,
        )
        for y in range(4)
        for z in range(4)
        for c in range(2)
    ]


def dp_perm(dx, dz):
    return [
        (x * 2 + z, (x + dx) % 4 * 2 + (z + dz) % 2) for x in range(4) for z in range(2)
    ]


SPREAD = [(i * 32 + m, m // 4 * 32 + i * 4 + m % 4) for i in range(8) for m in range(32)]


def shift_y(block, by):
    return lax.ppermute(block, "mp", mp_perm(by, 0, 0))


def shift_z(block, by):
    return lax.ppermute(block, "mp", mp_perm(0, by, 0))


def swap_core(block):
    return lax.ppermute(block, "mp", mp_perm(0, 0, 1))


def shift_x(block, by):
    return lax.ppermute(block, "dp", dp_perm(by, 0))


def swap_z(block):
    return lax.ppermute(block, "dp", dp_perm(0, 1))


MIB = 1 << 20
UPPER = 144
VMEM = pl.BlockSpec(memory_space=pltpu.VMEM)
SMEM = pl.BlockSpec(memory_space=pltpu.SMEM)
ANY = pl.BlockSpec(memory_space=pl.ANY)
HBM = pl.BlockSpec(memory_space=pltpu.HBM)


def struct(*shape, kind=BF16):
    return jax.ShapeDtypeStruct(shape, kind)


def cost(us):
    return pl.CostEstimate(flops=0, bytes_accessed=int(us * 3.5e6), transcendentals=0)


def whole(kernel, out_shape, operands, us, scalars=0, extra=(), limit=16, scratch=()):
    n = len(operands)

    def run(*refs):
        kernel(*refs[:n], *refs[n + len(extra) :])

    specs = [SMEM] * scalars + [VMEM] * (n - scalars) + [ANY] * len(extra)
    return pl.pallas_call(
        run,
        out_shape=out_shape,
        in_specs=specs,
        out_specs=jax.tree.map(lambda _: VMEM, out_shape),
        scratch_shapes=scratch,
        cost_estimate=cost(us),
        compiler_params=pltpu.CompilerParams(vmem_limit_bytes=limit * MIB),
    )(*operands, *extra)


def inner_rows(left, right):
    return lax.dot_general(left, right, (((0,), (0,)), ((), ())), preferred_element_type=F32)


def cross_last(left, right):
    return lax.dot_general(left, right, (((1,), (1,)), ((), ())), preferred_element_type=F32)


def mean_last(block):
    return jnp.mean(block, axis=-1, keepdims=True)


def as_columns(first, second):
    lane = lax.broadcasted_iota(jnp.int32, (first.shape[0], HD), 1)
    return jnp.where(lane == 0, first, jnp.where(lane == 1, second, 0.0))


def as_rows(columns):
    return jnp.transpose(columns)[:8]


def from_rows(rows):
    pad = jnp.zeros((HD - 8, rows.shape[1]), F32)
    return jnp.transpose(jnp.concatenate([rows, pad]))


def rounded(values):
    return values.astype(BF16).astype(F32)


def stacked(upper, lower):
    twice = jnp.concatenate([upper, lower])
    return twice.astype(BF16)


def packed(rows):
    high = rounded(rows)
    return stacked(high, rows - high)


def unpacked(rows):
    rows = rows.astype(F32)
    return rows[:8] + rows[8:]


def unit_rows(block):
    centred = block - mean_last(block)
    inverse = lax.rsqrt(mean_last(centred * centred) + EPS)
    return centred * inverse, inverse


def unit_rows_back(unit, inverse, grad):
    return inverse * (grad - mean_last(grad) - unit * mean_last(grad * unit))


def place(pos, pieces, put):
    for core, rings in enumerate(pieces):
        for dy in range(4):
            for dz in range(4):
                index = ((pos[0] + dy) % 4 * 4 + (pos[1] + dz) % 4) * 2 + (pos[2] + core) % 2
                put(rings.at[dy, dz], pl.multiple_of(index * HD, HD))


def stack_kernel(*refs):
    pieces, (out,) = refs[:4], refs[4:]
    for k, piece in enumerate(pieces):
        out[k] = piece[...]


def layer_kernel(pos, *refs):
    pieces, weights, (qk_gain, *outs) = refs[:2], refs[2:6], refs[6:]
    away, mine, message, sums, scales, stats_ref, gains, *scratch = outs
    image, normed, pre, *held, sems = scratch
    rows = image.shape[0]
    cut = normed.shape[0]
    w_qkv, w_up, w_out, w_down = held
    ff = w_up.shape[1]
    copies = [
        pltpu.make_async_copy(weight, place, sems.at[k])
        for k, (weight, place) in enumerate(zip(weights, held))
    ]
    for copy in copies:
        copy.start()

    def put_tokens(block, at):
        image[:, pl.ds(at, HD)] = block[:rows]
        normed[rows:, pl.ds(at, HD)] = block[rows:cut]

    def put_cotangent(block, at):
        image[:, pl.ds(at, HD)] = block[cut:]

    place(pos, pieces, put_tokens)
    step = 64
    for r in range(0, rows, step):
        values = image[r : r + step].astype(F32)
        mean = mean_last(values)
        centred = values - mean
        inverse = lax.rsqrt(mean_last(centred * centred) + EPS)
        scale = normed[rows : rows + 1].astype(F32)
        normed[r : r + step] = (centred * inverse * scale).astype(BF16)
        stats_ref[r : r + step] = as_columns(mean, inverse)
    gains[...] = normed[rows:]
    stats = as_rows(stats_ref[...])
    high = rounded(stats)
    middle = rounded(stats - high)
    message[rows:, :rows] = stacked(high, middle)
    message[rows:, rows : 2 * rows] = stacked(stats - high - middle, jnp.zeros_like(stats))
    message[rows:, 2 * rows :] = jnp.zeros((cut - rows, message.shape[1] - 2 * rows), BF16)

    copies[0].wait()
    pre[:, : 3 * HD] = jnp.dot(normed[...], w_qkv[...], preferred_element_type=F32)
    copies[1].wait()
    pre[:, 3 * HD :] = jnp.dot(normed[...], w_up[...], preferred_element_type=F32)
    place(pos, pieces, put_cotangent)
    up = pre[:rows, 3 * HD :]
    below = 0.5 * (1.0 + lax.erf(up * math.sqrt(0.5)))
    message[:rows, :ff] = (up * below).astype(BF16)
    unit_q, inverse_q = unit_rows(pre[:rows, :HD])
    unit_k, inverse_k = unit_rows(pre[:rows, HD : 2 * HD])
    q_normed = (unit_q * qk_gain[0:1]).astype(BF16)
    k_normed = (unit_k * qk_gain[1:2]).astype(BF16)
    values_in = pre[:rows, 2 * HD : 3 * HD].astype(BF16)
    scores = cross_last(q_normed, k_normed) / math.sqrt(HD)
    powers = jnp.exp(scores - jnp.max(scores, axis=-1, keepdims=True))
    probs = powers / jnp.sum(powers, axis=-1, keepdims=True)
    message[:rows, ff : ff + HD] = jnp.dot(
        probs.astype(BF16), values_in, preferred_element_type=F32
    ).astype(BF16)

    d_qkv = message.at[:rows, ff + HD : ff + 4 * HD]
    copies[2].wait()
    d_att = cross_last(image[...], w_out[...]).astype(BF16)
    copies[3].wait()
    d_act = cross_last(image[...], w_down[...])
    slope = below + up * jnp.exp(-0.5 * up * up) * (1.0 / math.sqrt(2.0 * math.pi))
    message[:rows, ff + 4 * HD :] = (d_act * slope).astype(BF16)
    d_qkv[:, 2 * HD :] = inner_rows(probs.astype(BF16), d_att).astype(BF16)
    d_probs = rounded(cross_last(d_att, values_in))
    d_scores = probs * (d_probs - jnp.sum(d_probs * probs, axis=-1, keepdims=True))
    d_scores = (d_scores / math.sqrt(HD)).astype(BF16)
    d_q = rounded(jnp.dot(d_scores, k_normed, preferred_element_type=F32))
    d_k = rounded(inner_rows(d_scores, q_normed))
    d_qkv[:, :HD] = unit_rows_back(unit_q, inverse_q, d_q * qk_gain[0:1]).astype(BF16)
    d_qkv[:, HD : 2 * HD] = unit_rows_back(unit_k, inverse_k, d_k * qk_gain[1:2]).astype(BF16)
    scales[0:1] = jnp.sum(d_q * unit_q, axis=0, keepdims=True)
    scales[1:2] = jnp.sum(d_k * unit_k, axis=0, keepdims=True)

    values = message[:rows, ff + HD :].astype(F32)
    first = jnp.sum(values * pre[rows : rows + 1], axis=1, keepdims=True)
    second = jnp.sum(values * pre[:rows], axis=1, keepdims=True)
    sums[...] = as_rows(as_columns(first, second))

    tail = packed(sums[...])
    away[32 * rows : 32 * rows + 16] = tail[:, :HD]
    away[32 * rows + 16 :] = tail[:, HD:]
    mine_first = pos[2] == 0

    def put(dy, at, block):
        block = block.astype(BF16)
        low, high = block[:, :HD], block[:, HD:]
        mine[dy, at] = jnp.where(mine_first, low, high)
        start = (dy * 8 + at) * rows
        away[start : start + rows] = jnp.where(mine_first, high, low)

    for dy in range(4):
        for dz in range(4):
            index = (pos[0] + dy) % 4 * 4 + (pos[1] + dz) % 4
            at = pl.ds(pl.multiple_of(index * 256, 256), 256)
            put(
                dy,
                dz,
                jnp.dot(message[:rows, :ff], w_down[:, at], preferred_element_type=F32)
                + jnp.dot(
                    message[:rows, ff : ff + HD], w_out[:, at], preferred_element_type=F32
                ),
            )
            put(
                dy,
                4 + dz,
                cross_last(message[:rows, ff + HD : ff + 4 * HD], w_qkv[at, :])
                + cross_last(message[:rows, ff + 4 * HD :], w_up[at, :]),
            )


def pair_sum_kernel(mine, came, sums, other, low, high, *outs):
    *outs, to_right, to_left = outs
    rows = other.shape[0]
    to_right[:rows] = other[...]
    to_right[rows:] = low[:UPPER]
    to_left[:rows] = other[...]
    to_left[rows:] = high[UPPER:]
    n = mine.shape[2]
    tail = packed(sums[...] + tail_sums([came], 32 * n))
    for dy, out in enumerate(outs):
        for at in range(8):
            start = (dy * 8 + at) * n
            both = mine[dy, at].astype(F32) + came[start : start + n].astype(F32)
            out[at * n : (at + 1) * n] = both.astype(BF16)
        out[8 * n : 8 * n + 16] = tail[:, :HD]
        out[8 * n + 16 :] = tail[:, HD:]


def tail_sums(parts, n):
    total = None
    for part in parts:
        one = jnp.concatenate([unpacked(part[n : n + 16]), unpacked(part[n + 16 :])], axis=1)
        total = one if total is None else total + one
    return total


def ring_sum_kernel(*refs):
    parts, outs = refs[:4], refs[4:]
    n = (outs[0].shape[0] - 32) // 2
    tail = packed(tail_sums(parts, 8 * n))
    for dz, out in enumerate(outs):
        for half in range(2):
            at = slice((half * 4 + dz) * n, (half * 4 + dz + 1) * n)
            total = parts[0][at].astype(F32)
            for part in parts[1:]:
                total = total + part[at].astype(F32)
            out[half * n : (half + 1) * n] = total.astype(BF16)
        out[2 * n : 2 * n + 16] = tail[:, :HD]
        out[2 * n + 16 :] = tail[:, HD:]


def finish_kernel(*refs):
    parts, shares, refs = refs[:4], refs[4:7], refs[7:]
    tokens, cotangent, gain, stats, d_scales, mixed, d_tokens, scales, near = refs
    for k, share in enumerate(shares):
        near[k] = share[...]
    n = tokens.shape[0]
    branch = parts[0][:n].astype(F32)
    d_normed = parts[0][n : 2 * n].astype(F32)
    for part in parts[1:]:
        branch = branch + part[:n].astype(F32)
        d_normed = d_normed + part[n : 2 * n].astype(F32)
    image = tokens[...].astype(F32)
    mixed[...] = (image + branch).astype(BF16)
    means = from_rows(tail_sums(parts, 2 * n)) / D
    mean, inverse = stats[:, 0:1], stats[:, 1:2]
    unit = (image - mean) * inverse
    scaled = d_normed * gain[...].astype(F32)
    d_tokens[...] = (
        cotangent[...].astype(F32) + inverse * (scaled - means[:, 0:1] - unit * means[:, 1:2])
    ).astype(BF16)
    scales[...] = jnp.zeros_like(scales)
    scales[0:1] = jnp.sum(d_normed * unit, axis=0, keepdims=True)
    scales[1:3] = d_scales[...]


def image_of(pos, r):
    return (pos[3] + r // 2) % 4 * 2 + (pos[4] + r) % 2


def grads_kernel(pos, gains, *refs):
    shares, (own, other, high, left, right, far_other, low) = refs[:4], refs[4:11]
    g_out, g_down, g_qkv, g_up, *scratch = refs[11:]
    forward, backward, tails, blocks, normed, upstream, sems = scratch
    rows = blocks.shape[3] // 2
    ff = g_down.shape[0]
    cut, split, width = rows + 16, ff + HD, 4 * HD
    moves = []
    for core in range(2):
        near, share_far = shares[core * 2 : core * 2 + 2]
        share_rings = [near.at[0], near.at[1], share_far, near.at[2]]
        for dy in range(4):
            for dz in range(4):
                index = (pos[0] + dy) % 4 * 4 + (pos[1] + dz) % 4
                image, k = index // 2, index % 2
                r = (image // 2 + 4 - pos[3]) % 4 * 2 + (image % 2 + pos[4]) % 2
                moves.append((share_rings[dy].at[dz], blocks.at[core, r, k]))
    pieces = [
        (own, [(0, 0, rows)], rows),
        (other, [(0, 0, rows)], rows),
        (high, [(0, 0, rows)], rows),
        (left, [(0, 0, rows)], rows),
        (right, [(cut, 0, UPPER)], None),
        (far_other, [(0, 0, rows)], rows),
        (low, [(0, 0, rows)], rows),
        (right, [(0, 0, rows)], rows),
        (left, [(cut, UPPER, rows - UPPER)], 2 * cut - UPPER - 16),
    ]
    for r, (ref, spans, tail) in enumerate(pieces):
        r = r if r < 8 else 4
        for src, dst, n in spans:
            here = slice(r * rows + dst, r * rows + dst + n)
            moves.append((ref.at[src : src + n, :split], forward.at[here]))
            moves.append((ref.at[src : src + n, split:], backward.at[here]))
        if tail is not None:
            moves.append((ref.at[tail : tail + 16, :split], tails.at[r]))
    copies = [
        pltpu.make_async_copy(src, dst, sems.at[k]) for k, (src, dst) in enumerate(moves)
    ]
    for copy in copies:
        copy.start()
    for copy in copies:
        copy.wait()
    first = pl.multiple_of((pos[3] * 2 + pos[4]) * width, width)
    for r in range(8):
        here = slice(r * rows, (r + 1) * rows)
        tail = tails[r].astype(F32)
        stats = from_rows(
            tail[:8, :rows] + tail[8:, :rows] + tail[:8, rows : 2 * rows]
        )
        mean, inverse = stats[:, 0:1], stats[:, 1:2]
        for core in range(2):
            for k in range(2):
                at = pl.multiple_of((2 * k + (pos[2] + core) % 2) * HD, HD)
                centred = blocks[core, r, k, :rows].astype(F32) - mean
                scale = gains[0:1, pl.ds(first + at, HD)].astype(F32)
                normed[here, pl.ds(at, HD)] = (centred * inverse * scale).astype(BF16)
                upstream[here, pl.ds(at, HD)] = blocks[core, r, k, rows:]
    grads = inner_rows(forward[...], upstream[...]).astype(BF16)
    g_down[...] = grads[:ff]
    g_out[...] = grads[ff:]
    grads = inner_rows(normed[...], backward[...]).astype(BF16)
    g_qkv[...] = grads[:, : 3 * HD]
    g_up[...] = grads[:, 3 * HD :]


def ring4(block, shift):
    return [block, shift(block, -1), shift(block, 2), shift(block, 1)]


def to_ring(messages, shift):
    return [messages[0], shift(messages[1], 1), shift(messages[2], 2), shift(messages[3], -1)]


def body(tokens, gain, w_qkv, qk_gain, w_up, w_attn_out, w_down, cotangent):
    mp, dp = lax.axis_index("mp"), lax.axis_index("dp")
    rows, ff = tokens.shape[0], w_up.shape[1]
    pos = jnp.stack([mp // 8, mp // 2 % 4, mp % 2, dp // 2, dp % 2]).astype(jnp.int32)

    own = jnp.concatenate([tokens, jnp.broadcast_to(gain[None, :], (16, HD)), cotangent])
    cut, both = rows + 16, 2 * rows + 16
    ring = whole(stack_kernel, struct(4, both, HD), ring4(own, shift_z), 1)
    share, _ = lax.optimization_barrier((jnp.concatenate([tokens, cotangent]), ring))
    spread = lax.ppermute(share, ("dp", "mp"), SPREAD)
    share_ring = whole(
        stack_kernel, struct(4, 2 * rows, HD), ring4(spread, shift_z), 1, extra=(ring,)
    )
    rings = whole(
        stack_kernel,
        struct(4, 4, both, HD),
        ring4(ring, shift_y),
        1,
        extra=(share_ring,),
    )

    width = 2 * ff + 4 * HD
    hbm, vmem = [HBM] * 4, [VMEM] * 2
    away, mine, message, sums, d_scales, stats, gains = pl.pallas_call(
        layer_kernel,
        out_shape=(
            struct(32 * rows + 32, HD),
            struct(4, 8, rows, HD),
            struct(cut, width),
            struct(8, rows, kind=F32),
            struct(2, HD, kind=F32),
            struct(rows, HD, kind=F32),
            struct(16, D),
        ),
        in_specs=[SMEM, *vmem, *hbm, VMEM],
        out_specs=[VMEM] * 7,
        scratch_shapes=[
            pltpu.VMEM((rows, D), BF16),
            pltpu.VMEM((cut, D), BF16),
            pltpu.VMEM((cut, 3 * HD + ff), F32),
            *(pltpu.VMEM(w.shape, BF16) for w in (w_qkv, w_up, w_attn_out, w_down)),
            pltpu.SemaphoreType.DMA((4,)),
        ],
        cost_estimate=cost(15),
        compiler_params=pltpu.CompilerParams(vmem_limit_bytes=44 * MIB),
    )(
        pos,
        rings,
        swap_core(rings),
        w_qkv,
        w_up,
        w_attn_out,
        w_down,
        qk_gain,
    )
    other, low, high = swap_z(message), shift_x(message, 1), shift_x(message, -1)
    share_behind = shift_y(share_ring, 1)
    *messages, to_right, to_left = whole(
        pair_sum_kernel,
        [struct(8 * rows + 32, HD)] * 4
        + [struct(cut + UPPER, width), struct(2 * cut - UPPER, width)],
        [mine, swap_core(away), sums, other, low, high],
        1,
        limit=32,
        extra=(share_behind,),
    )
    right, left = shift_x(to_right, 1), shift_x(to_left, -1)
    messages = whole(
        ring_sum_kernel,
        [struct(2 * rows + 32, HD)] * 4,
        to_ring(messages, shift_y),
        1,
        extra=(right, left),
    )
    (last, share_last), _ = lax.optimization_barrier(((right[:cut], share_ring), messages[0]))
    far_other, share_ahead = shift_x(last, 1), shift_y(share_last, -1)
    mixed, d_tokens, scales, near = whole(
        finish_kernel,
        (
            struct(rows, HD),
            struct(rows, HD),
            struct(8, HD, kind=F32),
            struct(3, 4, 2 * rows, HD),
        ),
        [
            *to_ring(messages, shift_z),
            *(share_ring, share_ahead, share_behind),
            *(tokens, cotangent, gain[None, :], stats, d_scales),
        ],
        1,
        extra=(far_other,),
    )
    share_last, _ = lax.optimization_barrier((share_ring, mixed))
    share_far = shift_y(share_last, 2)
    scales = sum(ring4(scales + swap_z(scales), shift_x))
    share_last, _ = lax.optimization_barrier((share_far, scales))
    shares = [near, share_far, swap_core(near), swap_core(share_last)]
    images = [message, other, high, left, right, far_other, low]

    g_attn_out, g_down, g_qkv, g_up = pl.pallas_call(
        grads_kernel,
        out_shape=(
            struct(HD, 4 * HD),
            struct(ff, 4 * HD),
            struct(4 * HD, 3 * HD),
            struct(4 * HD, ff),
        ),
        in_specs=[SMEM, VMEM, *[ANY] * 11],
        out_specs=[VMEM] * 4,
        scratch_shapes=[
            pltpu.VMEM((8 * rows, ff + HD), BF16),
            pltpu.VMEM((8 * rows, 3 * HD + ff), BF16),
            pltpu.VMEM((8, 16, ff + HD), BF16),
            pltpu.VMEM((2, 8, 2, 2 * rows, HD), BF16),
            pltpu.VMEM((8 * rows, 4 * HD), BF16),
            pltpu.VMEM((8 * rows, 4 * HD), BF16),
            pltpu.SemaphoreType.DMA((64,)),
        ],
        cost_estimate=cost(8),
        compiler_params=pltpu.CompilerParams(vmem_limit_bytes=28 * MIB),
    )(pos, gains, *shares, *images)
    return mixed, d_tokens, scales[0], scales[1:3], g_qkv, g_up, g_attn_out, g_down


def solution(mesh):
    in_specs = (
        P("dp", "mp"),
        P("mp"),
        P(None, "mp"),
        P(None, "mp"),
        P(None, "mp"),
        P("mp", None),
        P("mp", None),
        P("dp", "mp"),
    )
    out_specs = (
        P("dp", "mp"),
        P("dp", "mp"),
        P("mp"),
        P(None, "mp"),
        P("dp", "mp"),
        P("dp", "mp"),
        P("mp", "dp"),
        P("mp", "dp"),
    )
    return jax.shard_map(body, mesh=mesh, in_specs=in_specs, out_specs=out_specs, check_vma=False)
```

```python
import functools
import math

import jax
import jax.numpy as jnp
from jax import lax
from jax.experimental import pallas as pl
from jax.experimental.pallas import tpu as pltpu
from jax.sharding import PartitionSpec as P

D = 4096
HD = 128
EPS = 1e-06
F32 = jnp.float32
BF16 = jnp.bfloat16


def mp_perm(dy, dz, dc):
    return [
        (
            (y * 4 + z) * 2 + c,
            ((y + dy) % 4 * 4 + (z + dz) % 4) * 2 + (c + dc) % 2,
        )
        for y in range(4)
        for z in range(4)
        for c in range(2)
    ]


def dp_perm(dx, dz):
    return [
        (x * 2 + z, (x + dx) % 4 * 2 + (z + dz) % 2) for x in range(4) for z in range(2)
    ]


SPREAD = [(i * 32 + m, m // 4 * 32 + i * 4 + m % 4) for i in range(8) for m in range(32)]


def shift_y(block, by):
    return lax.ppermute(block, "mp", mp_perm(by, 0, 0))


def shift_z(block, by):
    return lax.ppermute(block, "mp", mp_perm(0, by, 0))


def swap_core(block):
    return lax.ppermute(block, "mp", mp_perm(0, 0, 1))


def shift_x(block, by):
    return lax.ppermute(block, "dp", dp_perm(by, 0))


def swap_z(block):
    return lax.ppermute(block, "dp", dp_perm(0, 1))


MIB = 1 << 20
ONE_CORE = [[place * 2 + core for place in range(16)] for core in range(2)]
UPPER = 144
VMEM = pl.BlockSpec(memory_space=pltpu.VMEM)
SMEM = pl.BlockSpec(memory_space=pltpu.SMEM)
ANY = pl.BlockSpec(memory_space=pl.ANY)
HBM = pl.BlockSpec(memory_space=pltpu.HBM)


def struct(*shape, kind=BF16):
    return jax.ShapeDtypeStruct(shape, kind)


def cost(us):
    return pl.CostEstimate(flops=0, bytes_accessed=int(us * 3.5e6), transcendentals=0)


def whole(kernel, out_shape, operands, us, scalars=0, extra=(), limit=16, scratch=()):
    n = len(operands)

    def run(*refs):
        kernel(*refs[:n], *refs[n + len(extra) :])

    specs = [SMEM] * scalars + [VMEM] * (n - scalars) + [ANY] * len(extra)
    return pl.pallas_call(
        run,
        out_shape=out_shape,
        in_specs=specs,
        out_specs=jax.tree.map(lambda _: VMEM, out_shape),
        scratch_shapes=scratch,
        cost_estimate=cost(us),
        compiler_params=pltpu.CompilerParams(vmem_limit_bytes=limit * MIB),
    )(*operands, *extra)


def inner_rows(left, right):
    return lax.dot_general(left, right, (((0,), (0,)), ((), ())), preferred_element_type=F32)


def cross_last(left, right):
    return lax.dot_general(left, right, (((1,), (1,)), ((), ())), preferred_element_type=F32)


def mean_last(block):
    return jnp.mean(block, axis=-1, keepdims=True)


def as_columns(first, second):
    lane = lax.broadcasted_iota(jnp.int32, (first.shape[0], HD), 1)
    return jnp.where(lane == 0, first, jnp.where(lane == 1, second, 0.0))


def as_rows(columns):
    return jnp.transpose(columns)[:8]


def from_rows(rows):
    pad = jnp.zeros((HD - 8, rows.shape[1]), F32)
    return jnp.transpose(jnp.concatenate([rows, pad]))


def rounded(values):
    return values.astype(BF16).astype(F32)


def stacked(upper, lower):
    twice = jnp.concatenate([upper, lower])
    return twice.astype(BF16)


def packed(rows):
    high = rounded(rows)
    return stacked(high, rows - high)


def unpacked(rows):
    rows = rows.astype(F32)
    return rows[:8] + rows[8:]


def unit_rows(block):
    centred = block - mean_last(block)
    inverse = lax.rsqrt(mean_last(centred * centred) + EPS)
    return centred * inverse, inverse


def unit_rows_back(unit, inverse, grad):
    return inverse * (grad - mean_last(grad) - unit * mean_last(grad * unit))


def place(pos, pieces, put):
    for core, rings in enumerate(pieces):
        for dy in range(4):
            for dz in range(4):
                index = ((pos[0] + dy) % 4 * 4 + (pos[1] + dz) % 4) * 2 + (pos[2] + core) % 2
                put(rings.at[dy, dz], pl.multiple_of(index * HD, HD))


def stack_kernel(*refs):
    pieces, (out,) = refs[:4], refs[4:]
    for k, piece in enumerate(pieces):
        out[k] = piece[...]


def layer_kernel(pos, *refs):
    pieces, weights, (qk_gain, *outs) = refs[:2], refs[2:6], refs[6:]
    away, mine, message, sums, scales, stats_ref, gains, *scratch = outs
    image, normed, pre, *held, sems = scratch
    rows = image.shape[0]
    cut = normed.shape[0]
    w_qkv, w_up, w_out, w_down = held
    ff = w_up.shape[1]
    copies = [
        pltpu.make_async_copy(weight, place, sems.at[k])
        for k, (weight, place) in enumerate(zip(weights, held))
    ]
    for copy in copies:
        copy.start()

    def put_tokens(block, at):
        image[:, pl.ds(at, HD)] = block[:rows]
        normed[rows:, pl.ds(at, HD)] = block[rows:cut]

    def put_cotangent(block, at):
        image[:, pl.ds(at, HD)] = block[cut:]

    place(pos, pieces, put_tokens)
    step = 64
    for r in range(0, rows, step):
        values = image[r : r + step].astype(F32)
        mean = mean_last(values)
        centred = values - mean
        inverse = lax.rsqrt(mean_last(centred * centred) + EPS)
        scale = normed[rows : rows + 1].astype(F32)
        normed[r : r + step] = (centred * inverse * scale).astype(BF16)
        stats_ref[r : r + step] = as_columns(mean, inverse)
    gains[...] = normed[rows:]
    stats = as_rows(stats_ref[...])
    high = rounded(stats)
    middle = rounded(stats - high)
    message[rows:, :rows] = stacked(high, middle)
    message[rows:, rows : 2 * rows] = stacked(stats - high - middle, jnp.zeros_like(stats))
    message[rows:, 2 * rows :] = jnp.zeros((cut - rows, message.shape[1] - 2 * rows), BF16)

    copies[0].wait()
    pre[:, : 3 * HD] = jnp.dot(normed[...], w_qkv[...], preferred_element_type=F32)
    copies[1].wait()
    pre[:, 3 * HD :] = jnp.dot(normed[...], w_up[...], preferred_element_type=F32)
    place(pos, pieces, put_cotangent)
    up = pre[:rows, 3 * HD :]
    below = 0.5 * (1.0 + lax.erf(up * math.sqrt(0.5)))
    message[:rows, :ff] = (up * below).astype(BF16)
    unit_q, inverse_q = unit_rows(pre[:rows, :HD])
    unit_k, inverse_k = unit_rows(pre[:rows, HD : 2 * HD])
    q_normed = (unit_q * qk_gain[0:1]).astype(BF16)
    k_normed = (unit_k * qk_gain[1:2]).astype(BF16)
    values_in = pre[:rows, 2 * HD : 3 * HD].astype(BF16)
    scores = cross_last(q_normed, k_normed) / math.sqrt(HD)
    powers = jnp.exp(scores - jnp.max(scores, axis=-1, keepdims=True))
    probs = powers / jnp.sum(powers, axis=-1, keepdims=True)
    message[:rows, ff : ff + HD] = jnp.dot(
        probs.astype(BF16), values_in, preferred_element_type=F32
    ).astype(BF16)

    d_qkv = message.at[:rows, ff + HD : ff + 4 * HD]
    copies[2].wait()
    d_att = cross_last(image[...], w_out[...]).astype(BF16)
    copies[3].wait()
    d_act = cross_last(image[...], w_down[...])
    slope = below + up * jnp.exp(-0.5 * up * up) * (1.0 / math.sqrt(2.0 * math.pi))
    message[:rows, ff + 4 * HD :] = (d_act * slope).astype(BF16)
    d_qkv[:, 2 * HD :] = inner_rows(probs.astype(BF16), d_att).astype(BF16)
    d_probs = rounded(cross_last(d_att, values_in))
    d_scores = probs * (d_probs - jnp.sum(d_probs * probs, axis=-1, keepdims=True))
    d_scores = (d_scores / math.sqrt(HD)).astype(BF16)
    d_q = rounded(jnp.dot(d_scores, k_normed, preferred_element_type=F32))
    d_k = rounded(inner_rows(d_scores, q_normed))
    d_qkv[:, :HD] = unit_rows_back(unit_q, inverse_q, d_q * qk_gain[0:1]).astype(BF16)
    d_qkv[:, HD : 2 * HD] = unit_rows_back(unit_k, inverse_k, d_k * qk_gain[1:2]).astype(BF16)
    scales[0:1] = jnp.sum(d_q * unit_q, axis=0, keepdims=True)
    scales[1:2] = jnp.sum(d_k * unit_k, axis=0, keepdims=True)

    values = message[:rows, ff + HD :].astype(F32)
    first = jnp.sum(values * pre[rows : rows + 1], axis=1, keepdims=True)
    second = jnp.sum(values * pre[:rows], axis=1, keepdims=True)
    sums[...] = as_rows(as_columns(first, second))

    tail = packed(sums[...])
    away[32 * rows : 32 * rows + 16] = tail[:, :HD]
    away[32 * rows + 16 :] = tail[:, HD:]
    mine_first = pos[2] == 0

    def put(dy, at, block):
        block = block.astype(BF16)
        low, high = block[:, :HD], block[:, HD:]
        mine[dy, at] = jnp.where(mine_first, low, high)
        start = (dy * 8 + at) * rows
        away[start : start + rows] = jnp.where(mine_first, high, low)

    for dy in range(4):
        for dz in range(4):
            index = (pos[0] + dy) % 4 * 4 + (pos[1] + dz) % 4
            at = pl.ds(pl.multiple_of(index * 256, 256), 256)
            put(
                dy,
                dz,
                jnp.dot(message[:rows, :ff], w_down[:, at], preferred_element_type=F32)
                + jnp.dot(
                    message[:rows, ff : ff + HD], w_out[:, at], preferred_element_type=F32
                ),
            )
            put(
                dy,
                4 + dz,
                cross_last(message[:rows, ff + HD : ff + 4 * HD], w_qkv[at, :])
                + cross_last(message[:rows, ff + 4 * HD :], w_up[at, :]),
            )


def pair_sum_kernel(mine, came, sums, other, low, high, *outs):
    *outs, to_right, to_left = outs
    rows = other.shape[0]
    to_right[:rows] = other[...]
    to_right[rows:] = low[:UPPER]
    to_left[:rows] = other[...]
    to_left[rows:] = high[UPPER:]
    n = mine.shape[2]
    tail = packed(sums[...] + tail_sums([came], 32 * n))
    for dy, out in enumerate(outs):
        for at in range(8):
            start = (dy * 8 + at) * n
            both = mine[dy, at].astype(F32) + came[start : start + n].astype(F32)
            out[at * n : (at + 1) * n] = both.astype(BF16)
        out[8 * n : 8 * n + 16] = tail[:, :HD]
        out[8 * n + 16 :] = tail[:, HD:]


def tail_sums(parts, n):
    total = None
    for part in parts:
        one = jnp.concatenate([unpacked(part[n : n + 16]), unpacked(part[n + 16 :])], axis=1)
        total = one if total is None else total + one
    return total


def ring_sum_kernel(*refs):
    parts, outs = refs[:4], refs[4:]
    n = (outs[0].shape[0] - 32) // 2
    tail = packed(tail_sums(parts, 8 * n))
    for dz, out in enumerate(outs):
        for half in range(2):
            at = slice((half * 4 + dz) * n, (half * 4 + dz + 1) * n)
            total = parts[0][at].astype(F32)
            for part in parts[1:]:
                total = total + part[at].astype(F32)
            out[half * n : (half + 1) * n] = total.astype(BF16)
        out[2 * n : 2 * n + 16] = tail[:, :HD]
        out[2 * n + 16 :] = tail[:, HD:]


def finish_kernel(*refs):
    parts, (tokens, cotangent, gain, stats, d_scales, mixed, d_tokens, scales) = refs[:4], refs[4:]
    n = tokens.shape[0]
    branch = parts[0][:n].astype(F32)
    d_normed = parts[0][n : 2 * n].astype(F32)
    for part in parts[1:]:
        branch = branch + part[:n].astype(F32)
        d_normed = d_normed + part[n : 2 * n].astype(F32)
    image = tokens[...].astype(F32)
    mixed[...] = (image + branch).astype(BF16)
    means = from_rows(tail_sums(parts, 2 * n)) / D
    mean, inverse = stats[:, 0:1], stats[:, 1:2]
    unit = (image - mean) * inverse
    scaled = d_normed * gain[...].astype(F32)
    d_tokens[...] = (
        cotangent[...].astype(F32) + inverse * (scaled - means[:, 0:1] - unit * means[:, 1:2])
    ).astype(BF16)
    scales[...] = jnp.zeros_like(scales)
    scales[0:1] = jnp.sum(d_normed * unit, axis=0, keepdims=True)
    scales[1:3] = d_scales[...]


def image_of(pos, r):
    return (pos[3] + r // 2) % 4 * 2 + (pos[4] + r) % 2


def grads_kernel(pos, gains, *refs):
    columns, (own, other, high, left, right, far_other, low) = refs[:2], refs[2:9]
    g_out, g_down, g_qkv, g_up, *scratch = refs[9:]
    forward, backward, tails, blocks, normed, upstream, sems = scratch
    rows = blocks.shape[3] // 2
    ff = g_down.shape[0]
    cut, split, width = rows + 16, ff + HD, 4 * HD
    moves = []
    for core in range(2):
        for r in range(8):
            odd = (pos[2] + core) % 2
            moves.append((columns[core].at[image_of(pos, r)], blocks.at[odd, r]))
    pieces = [
        (own, [(0, 0, rows)], rows),
        (other, [(0, 0, rows)], rows),
        (high, [(0, 0, rows)], rows),
        (left, [(0, 0, rows)], rows),
        (right, [(cut, 0, UPPER)], None),
        (far_other, [(0, 0, rows)], rows),
        (low, [(0, 0, rows)], rows),
        (right, [(0, 0, rows)], rows),
        (left, [(cut, UPPER, rows - UPPER)], 2 * cut - UPPER - 16),
    ]
    for r, (ref, spans, tail) in enumerate(pieces):
        r = r if r < 8 else 4
        for src, dst, n in spans:
            here = slice(r * rows + dst, r * rows + dst + n)
            moves.append((ref.at[src : src + n, :split], forward.at[here]))
            moves.append((ref.at[src : src + n, split:], backward.at[here]))
        if tail is not None:
            moves.append((ref.at[tail : tail + 16, :split], tails.at[r]))
    copies = [
        pltpu.make_async_copy(src, dst, sems.at[k]) for k, (src, dst) in enumerate(moves)
    ]
    for copy in copies:
        copy.start()
    for copy in copies:
        copy.wait()
    first = pl.multiple_of((pos[3] * 2 + pos[4]) * width, width)
    scale = gains[0:1, pl.ds(first, width)].astype(F32)
    for r in range(8):
        here = slice(r * rows, (r + 1) * rows)
        tail = tails[r].astype(F32)
        stats = from_rows(
            tail[:8, :rows] + tail[8:, :rows] + tail[:8, rows : 2 * rows]
        )
        mean, inverse = stats[:, 0:1], stats[:, 1:2]
        for group in range(4):
            lanes = slice(group * HD, (group + 1) * HD)
            block = blocks.at[group % 2, r, group // 2]
            centred = block[:rows].astype(F32) - mean
            normed[here, lanes] = (centred * inverse * scale[:, lanes]).astype(BF16)
            upstream[here, lanes] = block[rows:]
    grads = inner_rows(forward[...], upstream[...]).astype(BF16)
    g_down[...] = grads[:ff]
    g_out[...] = grads[ff:]
    grads = inner_rows(normed[...], backward[...]).astype(BF16)
    g_qkv[...] = grads[:, : 3 * HD]
    g_up[...] = grads[:, 3 * HD :]


def ring4(block, shift):
    return [block, shift(block, -1), shift(block, 2), shift(block, 1)]


def to_ring(messages, shift):
    return [messages[0], shift(messages[1], 1), shift(messages[2], 2), shift(messages[3], -1)]


def body(tokens, gain, w_qkv, qk_gain, w_up, w_attn_out, w_down, cotangent):
    mp, dp = lax.axis_index("mp"), lax.axis_index("dp")
    rows, ff = tokens.shape[0], w_up.shape[1]
    pos = jnp.stack([mp // 8, mp // 2 % 4, mp % 2, dp // 2, dp % 2]).astype(jnp.int32)

    own = jnp.concatenate([tokens, jnp.broadcast_to(gain[None, :], (16, HD)), cotangent])
    cut, both = rows + 16, 2 * rows + 16
    ring = whole(stack_kernel, struct(4, both, HD), ring4(own, shift_z), 1)
    share, _ = lax.optimization_barrier((jnp.concatenate([tokens, cotangent]), ring))
    spread = lax.ppermute(share, ("dp", "mp"), SPREAD)
    columns = lax.all_gather(spread, "mp", axis=0, tiled=False, axis_index_groups=ONE_CORE)
    columns = columns.reshape(8, 2, 2 * rows, HD)
    rings = whole(
        stack_kernel, struct(4, 4, both, HD), ring4(ring, shift_y), 1, extra=(spread,)
    )

    width = 2 * ff + 4 * HD
    hbm, vmem = [HBM] * 4, [VMEM] * 2
    away, mine, message, sums, d_scales, stats, gains = pl.pallas_call(
        layer_kernel,
        out_shape=(
            struct(32 * rows + 32, HD),
            struct(4, 8, rows, HD),
            struct(cut, width),
            struct(8, rows, kind=F32),
            struct(2, HD, kind=F32),
            struct(rows, HD, kind=F32),
            struct(16, D),
        ),
        in_specs=[SMEM, *vmem, *hbm, VMEM],
        out_specs=[VMEM] * 7,
        scratch_shapes=[
            pltpu.VMEM((rows, D), BF16),
            pltpu.VMEM((cut, D), BF16),
            pltpu.VMEM((cut, 3 * HD + ff), F32),
            *(pltpu.VMEM(w.shape, BF16) for w in (w_qkv, w_up, w_attn_out, w_down)),
            pltpu.SemaphoreType.DMA((4,)),
        ],
        cost_estimate=cost(15),
        compiler_params=pltpu.CompilerParams(vmem_limit_bytes=44 * MIB),
    )(
        pos,
        rings,
        swap_core(rings),
        w_qkv,
        w_up,
        w_attn_out,
        w_down,
        qk_gain,
    )
    other, low, high = swap_z(message), shift_x(message, 1), shift_x(message, -1)
    *messages, to_right, to_left = whole(
        pair_sum_kernel,
        [struct(8 * rows + 32, HD)] * 4
        + [struct(cut + UPPER, width), struct(2 * cut - UPPER, width)],
        [mine, swap_core(away), sums, other, low, high],
        1,
        limit=32,
    )
    right, left = shift_x(to_right, 1), shift_x(to_left, -1)
    messages = whole(
        ring_sum_kernel,
        [struct(2 * rows + 32, HD)] * 4,
        to_ring(messages, shift_y),
        1,
        extra=(right, left),
    )
    last, _ = lax.optimization_barrier((right[:cut], messages[0]))
    far_other = shift_x(last, 1)
    mixed, d_tokens, scales = whole(
        finish_kernel,
        (
            struct(rows, HD),
            struct(rows, HD),
            struct(8, HD, kind=F32),
        ),
        [
            *to_ring(messages, shift_z),
            *(tokens, cotangent, gain[None, :], stats, d_scales),
        ],
        1,
        extra=(far_other,),
    )
    columns, _ = lax.optimization_barrier((columns, mixed))
    columns_other = swap_core(columns)
    scales = sum(ring4(scales + swap_z(scales), shift_x))
    images = [message, other, high, left, right, far_other, low]

    g_attn_out, g_down, g_qkv, g_up = pl.pallas_call(
        grads_kernel,
        out_shape=(
            struct(HD, 4 * HD),
            struct(ff, 4 * HD),
            struct(4 * HD, 3 * HD),
            struct(4 * HD, ff),
        ),
        in_specs=[SMEM, VMEM, *[ANY] * 9],
        out_specs=[VMEM] * 4,
        scratch_shapes=[
            pltpu.VMEM((8 * rows, ff + HD), BF16),
            pltpu.VMEM((8 * rows, 3 * HD + ff), BF16),
            pltpu.VMEM((8, 16, ff + HD), BF16),
            pltpu.VMEM((2, 8, 2, 2 * rows, HD), BF16),
            pltpu.VMEM((8 * rows, 4 * HD), BF16),
            pltpu.VMEM((8 * rows, 4 * HD), BF16),
            pltpu.SemaphoreType.DMA((64,)),
        ],
        cost_estimate=cost(8),
        compiler_params=pltpu.CompilerParams(vmem_limit_bytes=28 * MIB),
    )(pos, gains, columns, columns_other, *images)
    return mixed, d_tokens, scales[0], scales[1:3], g_qkv, g_up, g_attn_out, g_down


def solution(mesh):
    in_specs = (
        P("dp", "mp"),
        P("mp"),
        P(None, "mp"),
        P(None, "mp"),
        P(None, "mp"),
        P("mp", None),
        P("mp", None),
        P("dp", "mp"),
    )
    out_specs = (
        P("dp", "mp"),
        P("dp", "mp"),
        P("mp"),
        P(None, "mp"),
        P("dp", "mp"),
        P("dp", "mp"),
        P("mp", "dp"),
        P("mp", "dp"),
    )
    return jax.shard_map(body, mesh=mesh, in_specs=in_specs, out_specs=out_specs, check_vma=False)
```

```python
import functools
import math

import jax
import jax.numpy as jnp
from jax import lax
from jax.experimental import pallas as pl
from jax.experimental.pallas import tpu as pltpu
from jax.sharding import PartitionSpec as P

D = 4096
HD = 128
EPS = 1e-06
F32 = jnp.float32
BF16 = jnp.bfloat16


def mp_perm(dy, dz, dc):
    return [
        (
            (y * 4 + z) * 2 + c,
            ((y + dy) % 4 * 4 + (z + dz) % 4) * 2 + (c + dc) % 2,
        )
        for y in range(4)
        for z in range(4)
        for c in range(2)
    ]


def dp_perm(dx, dz):
    return [
        (x * 2 + z, (x + dx) % 4 * 2 + (z + dz) % 2) for x in range(4) for z in range(2)
    ]


SPREAD = [(i * 32 + m, m // 4 * 32 + i * 4 + m % 4) for i in range(8) for m in range(32)]


def shift_y(block, by):
    return lax.ppermute(block, "mp", mp_perm(by, 0, 0))


def shift_z(block, by):
    return lax.ppermute(block, "mp", mp_perm(0, by, 0))


def swap_core(block):
    return lax.ppermute(block, "mp", mp_perm(0, 0, 1))


def shift_x(block, by):
    return lax.ppermute(block, "dp", dp_perm(by, 0))


def swap_z(block):
    return lax.ppermute(block, "dp", dp_perm(0, 1))


MIB = 1 << 20
UPPER = 144
VMEM = pl.BlockSpec(memory_space=pltpu.VMEM)
SMEM = pl.BlockSpec(memory_space=pltpu.SMEM)
ANY = pl.BlockSpec(memory_space=pl.ANY)
HBM = pl.BlockSpec(memory_space=pltpu.HBM)


def struct(*shape, kind=BF16):
    return jax.ShapeDtypeStruct(shape, kind)


def cost(us):
    return pl.CostEstimate(flops=0, bytes_accessed=int(us * 3.5e6), transcendentals=0)


def whole(kernel, out_shape, operands, us, scalars=0, extra=(), limit=16, scratch=()):
    n = len(operands)

    def run(*refs):
        kernel(*refs[:n], *refs[n + len(extra) :])

    specs = [SMEM] * scalars + [VMEM] * (n - scalars) + [ANY] * len(extra)
    return pl.pallas_call(
        run,
        out_shape=out_shape,
        in_specs=specs,
        out_specs=jax.tree.map(lambda _: VMEM, out_shape),
        scratch_shapes=scratch,
        cost_estimate=cost(us),
        compiler_params=pltpu.CompilerParams(vmem_limit_bytes=limit * MIB),
    )(*operands, *extra)


def inner_rows(left, right):
    return lax.dot_general(left, right, (((0,), (0,)), ((), ())), preferred_element_type=F32)


def cross_last(left, right):
    return lax.dot_general(left, right, (((1,), (1,)), ((), ())), preferred_element_type=F32)


def mean_last(block):
    return jnp.mean(block, axis=-1, keepdims=True)


def as_columns(first, second):
    lane = lax.broadcasted_iota(jnp.int32, (first.shape[0], HD), 1)
    return jnp.where(lane == 0, first, jnp.where(lane == 1, second, 0.0))


def as_rows(columns):
    return jnp.transpose(columns)[:8]


def from_rows(rows):
    pad = jnp.zeros((HD - 8, rows.shape[1]), F32)
    return jnp.transpose(jnp.concatenate([rows, pad]))


def rounded(values):
    return values.astype(BF16).astype(F32)


def stacked(upper, lower):
    twice = jnp.concatenate([upper, lower])
    return twice.astype(BF16)


def packed(rows):
    high = rounded(rows)
    return stacked(high, rows - high)


def unpacked(rows):
    rows = rows.astype(F32)
    return rows[:8] + rows[8:]


def unit_rows(block):
    centred = block - mean_last(block)
    inverse = lax.rsqrt(mean_last(centred * centred) + EPS)
    return centred * inverse, inverse


def unit_rows_back(unit, inverse, grad):
    return inverse * (grad - mean_last(grad) - unit * mean_last(grad * unit))


def place(pos, pieces, span, out, at):
    own, other = pieces
    first = pos[2] == 0
    for y in range(4):
        for z in range(4):
            here = (y + 4 - pos[0]) % 4, (z + 4 - pos[1]) % 4
            mine, came = own[(*here, span)], other[(*here, span)]
            lanes = (y * 4 + z) * 256
            out[at, lanes : lanes + HD] = jnp.where(first, mine, came)
            out[at, lanes + HD : lanes + 256] = jnp.where(first, came, mine)


def stack_kernel(*refs):
    pieces, (out,) = refs[:4], refs[4:]
    for k, piece in enumerate(pieces):
        out[k] = piece[...]


def layer_kernel(pos, *refs):
    pieces, weights, (qk_gain, *outs) = refs[:2], refs[2:6], refs[6:]
    away, mine, message, sums, scales, stats_ref, gains, *scratch = outs
    image, normed, pre, *held, sems = scratch
    rows = image.shape[0]
    cut = normed.shape[0]
    w_qkv, w_up, w_out, w_down = held
    ff = w_up.shape[1]
    copies = [
        pltpu.make_async_copy(weight, place, sems.at[k])
        for k, (weight, place) in enumerate(zip(weights, held))
    ]
    for copy in copies:
        copy.start()

    place(pos, pieces, slice(0, rows), image, slice(0, rows))
    place(pos, pieces, slice(rows, cut), normed, slice(rows, cut))
    step = 64
    for r in range(0, rows, step):
        values = image[r : r + step].astype(F32)
        mean = mean_last(values)
        centred = values - mean
        inverse = lax.rsqrt(mean_last(centred * centred) + EPS)
        scale = normed[rows : rows + 1].astype(F32)
        normed[r : r + step] = (centred * inverse * scale).astype(BF16)
        stats_ref[r : r + step] = as_columns(mean, inverse)
    gains[...] = normed[rows:]
    stats = as_rows(stats_ref[...])
    high = rounded(stats)
    middle = rounded(stats - high)
    message[rows:, :rows] = stacked(high, middle)
    message[rows:, rows : 2 * rows] = stacked(stats - high - middle, jnp.zeros_like(stats))
    message[rows:, 2 * rows :] = jnp.zeros((cut - rows, message.shape[1] - 2 * rows), BF16)

    copies[0].wait()
    pre[:, : 3 * HD] = jnp.dot(normed[...], w_qkv[...], preferred_element_type=F32)
    copies[1].wait()
    pre[:, 3 * HD :] = jnp.dot(normed[...], w_up[...], preferred_element_type=F32)
    place(pos, pieces, slice(cut, cut + rows), image, slice(0, rows))
    up = pre[:rows, 3 * HD :]
    below = 0.5 * (1.0 + lax.erf(up * math.sqrt(0.5)))
    message[:rows, :ff] = (up * below).astype(BF16)
    unit_q, inverse_q = unit_rows(pre[:rows, :HD])
    unit_k, inverse_k = unit_rows(pre[:rows, HD : 2 * HD])
    q_normed = (unit_q * qk_gain[0:1]).astype(BF16)
    k_normed = (unit_k * qk_gain[1:2]).astype(BF16)
    values_in = pre[:rows, 2 * HD : 3 * HD].astype(BF16)
    scores = cross_last(q_normed, k_normed) / math.sqrt(HD)
    powers = jnp.exp(scores - jnp.max(scores, axis=-1, keepdims=True))
    probs = powers / jnp.sum(powers, axis=-1, keepdims=True)
    message[:rows, ff : ff + HD] = jnp.dot(
        probs.astype(BF16), values_in, preferred_element_type=F32
    ).astype(BF16)

    d_qkv = message.at[:rows, ff + HD : ff + 4 * HD]
    copies[2].wait()
    d_att = cross_last(image[...], w_out[...]).astype(BF16)
    copies[3].wait()
    d_act = cross_last(image[...], w_down[...])
    slope = below + up * jnp.exp(-0.5 * up * up) * (1.0 / math.sqrt(2.0 * math.pi))
    message[:rows, ff + 4 * HD :] = (d_act * slope).astype(BF16)
    d_qkv[:, 2 * HD :] = inner_rows(probs.astype(BF16), d_att).astype(BF16)
    d_probs = rounded(cross_last(d_att, values_in))
    d_scores = probs * (d_probs - jnp.sum(d_probs * probs, axis=-1, keepdims=True))
    d_scores = (d_scores / math.sqrt(HD)).astype(BF16)
    d_q = rounded(jnp.dot(d_scores, k_normed, preferred_element_type=F32))
    d_k = rounded(inner_rows(d_scores, q_normed))
    d_qkv[:, :HD] = unit_rows_back(unit_q, inverse_q, d_q * qk_gain[0:1]).astype(BF16)
    d_qkv[:, HD : 2 * HD] = unit_rows_back(unit_k, inverse_k, d_k * qk_gain[1:2]).astype(BF16)
    scales[0:1] = jnp.sum(d_q * unit_q, axis=0, keepdims=True)
    scales[1:2] = jnp.sum(d_k * unit_k, axis=0, keepdims=True)

    values = message[:rows, ff + HD :].astype(F32)
    first = jnp.sum(values * pre[rows : rows + 1], axis=1, keepdims=True)
    second = jnp.sum(values * pre[:rows], axis=1, keepdims=True)
    sums[...] = as_rows(as_columns(first, second))

    tail = packed(sums[...])
    away[32 * rows : 32 * rows + 16] = tail[:, :HD]
    away[32 * rows + 16 :] = tail[:, HD:]
    mine_first = pos[2] == 0

    def put(dy, at, block):
        block = block.astype(BF16)
        low, high = block[:, :HD], block[:, HD:]
        mine[dy, at] = jnp.where(mine_first, low, high)
        start = (dy * 8 + at) * rows
        away[start : start + rows] = jnp.where(mine_first, high, low)

    for dy in range(4):
        for dz in range(4):
            index = (pos[0] + dy) % 4 * 4 + (pos[1] + dz) % 4
            at = pl.ds(pl.multiple_of(index * 256, 256), 256)
            put(
                dy,
                dz,
                jnp.dot(message[:rows, :ff], w_down[:, at], preferred_element_type=F32)
                + jnp.dot(
                    message[:rows, ff : ff + HD], w_out[:, at], preferred_element_type=F32
                ),
            )
            put(
                dy,
                4 + dz,
                cross_last(message[:rows, ff + HD : ff + 4 * HD], w_qkv[at, :])
                + cross_last(message[:rows, ff + 4 * HD :], w_up[at, :]),
            )


def pair_sum_kernel(mine, came, sums, other, low, high, *outs):
    *outs, to_right, to_left = outs
    rows = other.shape[0]
    to_right[:rows] = other[...]
    to_right[rows:] = low[:UPPER]
    to_left[:rows] = other[...]
    to_left[rows:] = high[UPPER:]
    n = mine.shape[2]
    tail = packed(sums[...] + tail_sums([came], 32 * n))
    for dy, out in enumerate(outs):
        for at in range(8):
            start = (dy * 8 + at) * n
            both = mine[dy, at].astype(F32) + came[start : start + n].astype(F32)
            out[at * n : (at + 1) * n] = both.astype(BF16)
        out[8 * n : 8 * n + 16] = tail[:, :HD]
        out[8 * n + 16 :] = tail[:, HD:]


def tail_sums(parts, n):
    total = None
    for part in parts:
        one = jnp.concatenate([unpacked(part[n : n + 16]), unpacked(part[n + 16 :])], axis=1)
        total = one if total is None else total + one
    return total


def ring_sum_kernel(*refs):
    parts, outs = refs[:4], refs[4:]
    n = (outs[0].shape[0] - 32) // 2
    tail = packed(tail_sums(parts, 8 * n))
    for dz, out in enumerate(outs):
        for half in range(2):
            at = slice((half * 4 + dz) * n, (half * 4 + dz + 1) * n)
            total = parts[0][at].astype(F32)
            for part in parts[1:]:
                total = total + part[at].astype(F32)
            out[half * n : (half + 1) * n] = total.astype(BF16)
        out[2 * n : 2 * n + 16] = tail[:, :HD]
        out[2 * n + 16 :] = tail[:, HD:]


def finish_kernel(*refs):
    parts, shares, refs = refs[:4], refs[4:7], refs[7:]
    tokens, cotangent, gain, stats, d_scales, mixed, d_tokens, scales, near = refs
    for k, share in enumerate(shares):
        near[k] = share[...]
    n = tokens.shape[0]
    branch = parts[0][:n].astype(F32)
    d_normed = parts[0][n : 2 * n].astype(F32)
    for part in parts[1:]:
        branch = branch + part[:n].astype(F32)
        d_normed = d_normed + part[n : 2 * n].astype(F32)
    image = tokens[...].astype(F32)
    mixed[...] = (image + branch).astype(BF16)
    means = from_rows(tail_sums(parts, 2 * n)) / D
    mean, inverse = stats[:, 0:1], stats[:, 1:2]
    unit = (image - mean) * inverse
    scaled = d_normed * gain[...].astype(F32)
    d_tokens[...] = (
        cotangent[...].astype(F32) + inverse * (scaled - means[:, 0:1] - unit * means[:, 1:2])
    ).astype(BF16)
    scales[...] = jnp.zeros_like(scales)
    scales[0:1] = jnp.sum(d_normed * unit, axis=0, keepdims=True)
    scales[1:3] = d_scales[...]


def image_of(pos, r):
    return (pos[3] + r // 2) % 4 * 2 + (pos[4] + r) % 2


def grads_kernel(pos, gains, *refs):
    shares, (own, other, high, left, right, far_other, low) = refs[:4], refs[4:11]
    g_out, g_down, g_qkv, g_up, *scratch = refs[11:]
    forward, backward, tails, blocks, normed, upstream, sems = scratch
    rows = blocks.shape[3] // 2
    ff = g_down.shape[0]
    cut, split, width = rows + 16, ff + HD, 4 * HD
    moves = []
    for core in range(2):
        near, share_far = shares[core * 2 : core * 2 + 2]
        share_rings = [near.at[0], near.at[1], share_far, near.at[2]]
        for dy in range(4):
            for dz in range(4):
                index = (pos[0] + dy) % 4 * 4 + (pos[1] + dz) % 4
                image, k = index // 2, index % 2
                r = (image // 2 + 4 - pos[3]) % 4 * 2 + (image % 2 + pos[4]) % 2
                odd = (pos[2] + core) % 2
                moves.append((share_rings[dy].at[dz], blocks.at[odd, r, k]))
    pieces = [
        (own, [(0, 0, rows)], rows),
        (other, [(0, 0, rows)], rows),
        (high, [(0, 0, rows)], rows),
        (left, [(0, 0, rows)], rows),
        (right, [(cut, 0, UPPER)], None),
        (far_other, [(0, 0, rows)], rows),
        (low, [(0, 0, rows)], rows),
        (right, [(0, 0, rows)], rows),
        (left, [(cut, UPPER, rows - UPPER)], 2 * cut - UPPER - 16),
    ]
    for r, (ref, spans, tail) in enumerate(pieces):
        r = r if r < 8 else 4
        for src, dst, n in spans:
            here = slice(r * rows + dst, r * rows + dst + n)
            moves.append((ref.at[src : src + n, :split], forward.at[here]))
            moves.append((ref.at[src : src + n, split:], backward.at[here]))
        if tail is not None:
            moves.append((ref.at[tail : tail + 16, :split], tails.at[r]))
    copies = [
        pltpu.make_async_copy(src, dst, sems.at[k]) for k, (src, dst) in enumerate(moves)
    ]
    for copy in copies:
        copy.start()
    for copy in copies:
        copy.wait()
    first = pl.multiple_of((pos[3] * 2 + pos[4]) * width, width)
    scale = gains[0:1, pl.ds(first, width)].astype(F32)
    for r in range(8):
        here = slice(r * rows, (r + 1) * rows)
        tail = tails[r].astype(F32)
        stats = from_rows(
            tail[:8, :rows] + tail[8:, :rows] + tail[:8, rows : 2 * rows]
        )
        mean, inverse = stats[:, 0:1], stats[:, 1:2]
        for group in range(4):
            lanes = slice(group * HD, (group + 1) * HD)
            block = blocks.at[group % 2, r, group // 2]
            centred = block[:rows].astype(F32) - mean
            normed[here, lanes] = (centred * inverse * scale[:, lanes]).astype(BF16)
            upstream[here, lanes] = block[rows:]
    grads = inner_rows(forward[...], upstream[...]).astype(BF16)
    g_down[...] = grads[:ff]
    g_out[...] = grads[ff:]
    grads = inner_rows(normed[...], backward[...]).astype(BF16)
    g_qkv[...] = grads[:, : 3 * HD]
    g_up[...] = grads[:, 3 * HD :]


def ring4(block, shift):
    return [block, shift(block, -1), shift(block, 2), shift(block, 1)]


def to_ring(messages, shift):
    return [messages[0], shift(messages[1], 1), shift(messages[2], 2), shift(messages[3], -1)]


def body(tokens, gain, w_qkv, qk_gain, w_up, w_attn_out, w_down, cotangent):
    mp, dp = lax.axis_index("mp"), lax.axis_index("dp")
    rows, ff = tokens.shape[0], w_up.shape[1]
    pos = jnp.stack([mp // 8, mp // 2 % 4, mp % 2, dp // 2, dp % 2]).astype(jnp.int32)

    own = jnp.concatenate([tokens, jnp.broadcast_to(gain[None, :], (16, HD)), cotangent])
    cut, both = rows + 16, 2 * rows + 16
    spread = lax.ppermute(jnp.concatenate([tokens, cotangent]), ("dp", "mp"), SPREAD)
    ring = whole(
        stack_kernel, struct(4, both, HD), ring4(own, shift_z), 1, extra=(spread,)
    )
    share_ring = whole(
        stack_kernel, struct(4, 2 * rows, HD), ring4(spread, shift_z), 1, extra=(ring,)
    )
    rings = whole(
        stack_kernel,
        struct(4, 4, both, HD),
        ring4(ring, shift_y),
        1,
        extra=(share_ring,),
    )

    width = 2 * ff + 4 * HD
    hbm, vmem = [HBM] * 4, [VMEM] * 2
    away, mine, message, sums, d_scales, stats, gains = pl.pallas_call(
        layer_kernel,
        out_shape=(
            struct(32 * rows + 32, HD),
            struct(4, 8, rows, HD),
            struct(cut, width),
            struct(8, rows, kind=F32),
            struct(2, HD, kind=F32),
            struct(rows, HD, kind=F32),
            struct(16, D),
        ),
        in_specs=[SMEM, *vmem, *hbm, VMEM],
        out_specs=[VMEM] * 7,
        scratch_shapes=[
            pltpu.VMEM((rows, D), BF16),
            pltpu.VMEM((cut, D), BF16),
            pltpu.VMEM((cut, 3 * HD + ff), F32),
            *(pltpu.VMEM(w.shape, BF16) for w in (w_qkv, w_up, w_attn_out, w_down)),
            pltpu.SemaphoreType.DMA((4,)),
        ],
        cost_estimate=cost(15),
        compiler_params=pltpu.CompilerParams(vmem_limit_bytes=44 * MIB),
    )(
        pos,
        rings,
        swap_core(rings),
        w_qkv,
        w_up,
        w_attn_out,
        w_down,
        qk_gain,
    )
    other, low, high = swap_z(message), shift_x(message, 1), shift_x(message, -1)
    share_behind = shift_y(share_ring, 1)
    *messages, to_right, to_left = whole(
        pair_sum_kernel,
        [struct(8 * rows + 32, HD)] * 4
        + [struct(cut + UPPER, width), struct(2 * cut - UPPER, width)],
        [mine, swap_core(away), sums, other, low, high],
        1,
        limit=32,
        extra=(share_behind,),
    )
    right, left = shift_x(to_right, 1), shift_x(to_left, -1)
    messages = whole(
        ring_sum_kernel,
        [struct(2 * rows + 32, HD)] * 4,
        to_ring(messages, shift_y),
        1,
        extra=(right, left),
    )
    (last, share_last), _ = lax.optimization_barrier(((right[:cut], share_ring), messages[0]))
    far_other, share_ahead = shift_x(last, 1), shift_y(share_last, -1)
    mixed, d_tokens, scales, near = whole(
        finish_kernel,
        (
            struct(rows, HD),
            struct(rows, HD),
            struct(8, HD, kind=F32),
            struct(3, 4, 2 * rows, HD),
        ),
        [
            *to_ring(messages, shift_z),
            *(share_ring, share_ahead, share_behind),
            *(tokens, cotangent, gain[None, :], stats, d_scales),
        ],
        1,
        extra=(far_other,),
    )
    share_last, _ = lax.optimization_barrier((share_ring, mixed))
    share_far = shift_y(share_last, 2)
    scales = sum(ring4(scales + swap_z(scales), shift_x))
    share_last, _ = lax.optimization_barrier((share_far, scales))
    shares = [near, share_far, swap_core(near), swap_core(share_last)]
    images = [message, other, high, left, right, far_other, low]

    g_attn_out, g_down, g_qkv, g_up = pl.pallas_call(
        grads_kernel,
        out_shape=(
            struct(HD, 4 * HD),
            struct(ff, 4 * HD),
            struct(4 * HD, 3 * HD),
            struct(4 * HD, ff),
        ),
        in_specs=[SMEM, VMEM, *[ANY] * 11],
        out_specs=[VMEM] * 4,
        scratch_shapes=[
            pltpu.VMEM((8 * rows, ff + HD), BF16),
            pltpu.VMEM((8 * rows, 3 * HD + ff), BF16),
            pltpu.VMEM((8, 16, ff + HD), BF16),
            pltpu.VMEM((2, 8, 2, 2 * rows, HD), BF16),
            pltpu.VMEM((8 * rows, 4 * HD), BF16),
            pltpu.VMEM((8 * rows, 4 * HD), BF16),
            pltpu.SemaphoreType.DMA((64,)),
        ],
        cost_estimate=cost(8),
        compiler_params=pltpu.CompilerParams(vmem_limit_bytes=28 * MIB),
    )(pos, gains, *shares, *images)
    return mixed, d_tokens, scales[0], scales[1:3], g_qkv, g_up, g_attn_out, g_down


def solution(mesh):
    in_specs = (
        P("dp", "mp"),
        P("mp"),
        P(None, "mp"),
        P(None, "mp"),
        P(None, "mp"),
        P("mp", None),
        P("mp", None),
        P("dp", "mp"),
    )
    out_specs = (
        P("dp", "mp"),
        P("dp", "mp"),
        P("mp"),
        P(None, "mp"),
        P("dp", "mp"),
        P("dp", "mp"),
        P("mp", "dp"),
        P("mp", "dp"),
    )
    return jax.shard_map(body, mesh=mesh, in_specs=in_specs, out_specs=out_specs, check_vma=False)
```

```python
import functools
import math

import jax
import jax.numpy as jnp
from jax import lax
from jax.experimental import pallas as pl
from jax.experimental.pallas import tpu as pltpu
from jax.sharding import PartitionSpec as P

D = 4096
HD = 128
EPS = 1e-06
F32 = jnp.float32
BF16 = jnp.bfloat16


def mp_perm(dy, dz, dc):
    return [
        (
            (y * 4 + z) * 2 + c,
            ((y + dy) % 4 * 4 + (z + dz) % 4) * 2 + (c + dc) % 2,
        )
        for y in range(4)
        for z in range(4)
        for c in range(2)
    ]


def dp_perm(dx, dz):
    return [
        (x * 2 + z, (x + dx) % 4 * 2 + (z + dz) % 2) for x in range(4) for z in range(2)
    ]


SPREAD = [(i * 32 + m, m // 4 * 32 + i * 4 + m % 4) for i in range(8) for m in range(32)]


def shift_y(block, by):
    return lax.ppermute(block, "mp", mp_perm(by, 0, 0))


def shift_z(block, by):
    return lax.ppermute(block, "mp", mp_perm(0, by, 0))


def swap_core(block):
    return lax.ppermute(block, "mp", mp_perm(0, 0, 1))


def shift_x(block, by):
    return lax.ppermute(block, "dp", dp_perm(by, 0))


def swap_z(block):
    return lax.ppermute(block, "dp", dp_perm(0, 1))


MIB = 1 << 20
UPPER = 144
VMEM = pl.BlockSpec(memory_space=pltpu.VMEM)
SMEM = pl.BlockSpec(memory_space=pltpu.SMEM)
ANY = pl.BlockSpec(memory_space=pl.ANY)
HBM = pl.BlockSpec(memory_space=pltpu.HBM)


def struct(*shape, kind=BF16):
    return jax.ShapeDtypeStruct(shape, kind)


def cost(us):
    return pl.CostEstimate(flops=0, bytes_accessed=int(us * 3.5e6), transcendentals=0)


def whole(kernel, out_shape, operands, us, scalars=0, extra=(), limit=16, scratch=()):
    n = len(operands)

    def run(*refs):
        kernel(*refs[:n], *refs[n + len(extra) :])

    specs = [SMEM] * scalars + [VMEM] * (n - scalars) + [ANY] * len(extra)
    return pl.pallas_call(
        run,
        out_shape=out_shape,
        in_specs=specs,
        out_specs=jax.tree.map(lambda _: VMEM, out_shape),
        scratch_shapes=scratch,
        cost_estimate=cost(us),
        compiler_params=pltpu.CompilerParams(vmem_limit_bytes=limit * MIB),
    )(*operands, *extra)


def inner_rows(left, right):
    return lax.dot_general(left, right, (((0,), (0,)), ((), ())), preferred_element_type=F32)


def cross_last(left, right):
    return lax.dot_general(left, right, (((1,), (1,)), ((), ())), preferred_element_type=F32)


def mean_last(block):
    return jnp.mean(block, axis=-1, keepdims=True)


def as_columns(first, second):
    lane = lax.broadcasted_iota(jnp.int32, (first.shape[0], HD), 1)
    return jnp.where(lane == 0, first, jnp.where(lane == 1, second, 0.0))


def as_rows(columns):
    return jnp.transpose(columns)[:8]


def from_rows(rows):
    pad = jnp.zeros((HD - 8, rows.shape[1]), F32)
    return jnp.transpose(jnp.concatenate([rows, pad]))


def rounded(values):
    return values.astype(BF16).astype(F32)


def stacked(upper, lower):
    twice = jnp.concatenate([upper, lower])
    return twice.astype(BF16)


def packed(rows):
    high = rounded(rows)
    return stacked(high, rows - high)


def unpacked(rows):
    rows = rows.astype(F32)
    return rows[:8] + rows[8:]


def unit_rows(block):
    centred = block - mean_last(block)
    inverse = lax.rsqrt(mean_last(centred * centred) + EPS)
    return centred * inverse, inverse


def unit_rows_back(unit, inverse, grad):
    return inverse * (grad - mean_last(grad) - unit * mean_last(grad * unit))


def place(pos, pieces, span, out, at):
    own, other = pieces
    first = pos[2] == 0
    for y in range(4):
        for z in range(4):
            here = (y + 4 - pos[0]) % 4, (z + 4 - pos[1]) % 4
            mine, came = own[(*here, span)], other[(*here, span)]
            lanes = (y * 4 + z) * 256
            out[at, lanes : lanes + HD] = jnp.where(first, mine, came)
            out[at, lanes + HD : lanes + 256] = jnp.where(first, came, mine)


def stack_kernel(*refs):
    pieces, (out,) = refs[:4], refs[4:]
    for k, piece in enumerate(pieces):
        out[k] = piece[...]


def layer_kernel(pos, *refs):
    pieces, weights, (qk_gain, *outs) = refs[:2], refs[2:6], refs[6:]
    away, mine, message, sums, scales, stats_ref, gains, *scratch = outs
    image, normed, pre, *held, sems = scratch
    rows = image.shape[0]
    cut = normed.shape[0]
    w_qkv, w_up, w_out, w_down = held
    ff = w_up.shape[1]
    copies = [
        pltpu.make_async_copy(weight, place, sems.at[k])
        for k, (weight, place) in enumerate(zip(weights, held))
    ]
    for copy in copies:
        copy.start()

    place(pos, pieces, slice(0, rows), image, slice(0, rows))
    place(pos, pieces, slice(rows, cut), normed, slice(rows, cut))
    step = 64
    for r in range(0, rows, step):
        values = image[r : r + step].astype(F32)
        mean = mean_last(values)
        centred = values - mean
        inverse = lax.rsqrt(mean_last(centred * centred) + EPS)
        scale = normed[rows : rows + 1].astype(F32)
        normed[r : r + step] = (centred * inverse * scale).astype(BF16)
        stats_ref[r : r + step] = as_columns(mean, inverse)
    gains[...] = normed[rows:]
    stats = as_rows(stats_ref[...])
    high = rounded(stats)
    middle = rounded(stats - high)
    message[rows:, :rows] = stacked(high, middle)
    message[rows:, rows : 2 * rows] = stacked(stats - high - middle, jnp.zeros_like(stats))
    message[rows:, 2 * rows :] = jnp.zeros((cut - rows, message.shape[1] - 2 * rows), BF16)

    copies[0].wait()
    pre[:, : 3 * HD] = jnp.dot(normed[...], w_qkv[...], preferred_element_type=F32)
    copies[1].wait()
    pre[:, 3 * HD :] = jnp.dot(normed[...], w_up[...], preferred_element_type=F32)
    place(pos, pieces, slice(cut, cut + rows), image, slice(0, rows))
    up = pre[:rows, 3 * HD :]
    below = 0.5 * (1.0 + lax.erf(up * math.sqrt(0.5)))
    message[:rows, :ff] = (up * below).astype(BF16)
    unit_q, inverse_q = unit_rows(pre[:rows, :HD])
    unit_k, inverse_k = unit_rows(pre[:rows, HD : 2 * HD])
    q_normed = (unit_q * qk_gain[0:1]).astype(BF16)
    k_normed = (unit_k * qk_gain[1:2]).astype(BF16)
    values_in = pre[:rows, 2 * HD : 3 * HD].astype(BF16)
    scores = cross_last(q_normed, k_normed) / math.sqrt(HD)
    powers = jnp.exp(scores - jnp.max(scores, axis=-1, keepdims=True))
    probs = powers / jnp.sum(powers, axis=-1, keepdims=True)
    message[:rows, ff : ff + HD] = jnp.dot(
        probs.astype(BF16), values_in, preferred_element_type=F32
    ).astype(BF16)

    d_qkv = message.at[:rows, ff + HD : ff + 4 * HD]
    copies[2].wait()
    d_att = cross_last(image[...], w_out[...]).astype(BF16)
    copies[3].wait()
    d_act = cross_last(image[...], w_down[...])
    slope = below + up * jnp.exp(-0.5 * up * up) * (1.0 / math.sqrt(2.0 * math.pi))
    message[:rows, ff + 4 * HD :] = (d_act * slope).astype(BF16)
    d_qkv[:, 2 * HD :] = inner_rows(probs.astype(BF16), d_att).astype(BF16)
    d_probs = rounded(cross_last(d_att, values_in))
    d_scores = probs * (d_probs - jnp.sum(d_probs * probs, axis=-1, keepdims=True))
    d_scores = (d_scores / math.sqrt(HD)).astype(BF16)
    d_q = rounded(jnp.dot(d_scores, k_normed, preferred_element_type=F32))
    d_k = rounded(inner_rows(d_scores, q_normed))
    d_qkv[:, :HD] = unit_rows_back(unit_q, inverse_q, d_q * qk_gain[0:1]).astype(BF16)
    d_qkv[:, HD : 2 * HD] = unit_rows_back(unit_k, inverse_k, d_k * qk_gain[1:2]).astype(BF16)
    scales[0:1] = jnp.sum(d_q * unit_q, axis=0, keepdims=True)
    scales[1:2] = jnp.sum(d_k * unit_k, axis=0, keepdims=True)

    values = message[:rows, ff + HD :].astype(F32)
    first = jnp.sum(values * pre[rows : rows + 1], axis=1, keepdims=True)
    second = jnp.sum(values * pre[:rows], axis=1, keepdims=True)
    sums[...] = as_rows(as_columns(first, second))

    tail = packed(sums[...])
    away[32 * rows : 32 * rows + 16] = tail[:, :HD]
    away[32 * rows + 16 :] = tail[:, HD:]
    mine_first = pos[2] == 0

    def put(dy, at, block):
        block = block.astype(BF16)
        low, high = block[:, :HD], block[:, HD:]
        mine[dy, at] = jnp.where(mine_first, low, high)
        start = (dy * 8 + at) * rows
        away[start : start + rows] = jnp.where(mine_first, high, low)

    for dy in range(4):
        for dz in range(4):
            index = (pos[0] + dy) % 4 * 4 + (pos[1] + dz) % 4
            at = pl.ds(pl.multiple_of(index * 256, 256), 256)
            put(
                dy,
                dz,
                jnp.dot(message[:rows, :ff], w_down[:, at], preferred_element_type=F32)
                + jnp.dot(
                    message[:rows, ff : ff + HD], w_out[:, at], preferred_element_type=F32
                ),
            )
            put(
                dy,
                4 + dz,
                cross_last(message[:rows, ff + HD : ff + 4 * HD], w_qkv[at, :])
                + cross_last(message[:rows, ff + 4 * HD :], w_up[at, :]),
            )


def pair_sum_kernel(mine, came, sums, other, low, high, *outs):
    *outs, to_right, to_left = outs
    rows = other.shape[0]
    to_right[:rows] = other[...]
    to_right[rows:] = low[:UPPER]
    to_left[:rows] = other[...]
    to_left[rows:] = high[UPPER:]
    n = mine.shape[2]
    tail = packed(sums[...] + tail_sums([came], 32 * n))
    for dy, out in enumerate(outs):
        for at in range(8):
            start = (dy * 8 + at) * n
            both = mine[dy, at].astype(F32) + came[start : start + n].astype(F32)
            out[at * n : (at + 1) * n] = both.astype(BF16)
        out[8 * n : 8 * n + 16] = tail[:, :HD]
        out[8 * n + 16 :] = tail[:, HD:]


def tail_sums(parts, n):
    total = None
    for part in parts:
        one = jnp.concatenate([unpacked(part[n : n + 16]), unpacked(part[n + 16 :])], axis=1)
        total = one if total is None else total + one
    return total


def ring_sum_kernel(*refs):
    parts, outs = refs[:4], refs[4:]
    n = (outs[0].shape[0] - 32) // 2
    tail = packed(tail_sums(parts, 8 * n))
    for dz, out in enumerate(outs):
        for half in range(2):
            at = slice((half * 4 + dz) * n, (half * 4 + dz + 1) * n)
            total = parts[0][at].astype(F32)
            for part in parts[1:]:
                total = total + part[at].astype(F32)
            out[half * n : (half + 1) * n] = total.astype(BF16)
        out[2 * n : 2 * n + 16] = tail[:, :HD]
        out[2 * n + 16 :] = tail[:, HD:]


def finish_kernel(*refs):
    parts, shares, refs = refs[:4], refs[4:8], refs[8:]
    tokens, cotangent, gain, stats, d_scales, mixed, d_tokens, scales, all_shares = refs
    for k, share in enumerate(shares):
        all_shares[k] = share[...]
    n = tokens.shape[0]
    branch = parts[0][:n].astype(F32)
    d_normed = parts[0][n : 2 * n].astype(F32)
    for part in parts[1:]:
        branch = branch + part[:n].astype(F32)
        d_normed = d_normed + part[n : 2 * n].astype(F32)
    image = tokens[...].astype(F32)
    mixed[...] = (image + branch).astype(BF16)
    means = from_rows(tail_sums(parts, 2 * n)) / D
    mean, inverse = stats[:, 0:1], stats[:, 1:2]
    unit = (image - mean) * inverse
    scaled = d_normed * gain[...].astype(F32)
    d_tokens[...] = (
        cotangent[...].astype(F32) + inverse * (scaled - means[:, 0:1] - unit * means[:, 1:2])
    ).astype(BF16)
    scales[...] = jnp.zeros_like(scales)
    scales[0:1] = jnp.sum(d_normed * unit, axis=0, keepdims=True)
    scales[1:3] = d_scales[...]


def image_of(pos, r):
    return (pos[3] + r // 2) % 4 * 2 + (pos[4] + r) % 2


def grads_kernel(pos, gains, *refs):
    shares, (own, other, high, left, right, far_right, far_left, low) = refs[:2], refs[2:10]
    g_out, g_down, g_qkv, g_up, *scratch = refs[10:]
    forward, backward, tails, blocks, normed, upstream, sum_forward, sum_backward, sems = scratch
    rows = blocks.shape[3] // 2
    ff = g_down.shape[0]
    cut, split, width = rows + 16, ff + HD, 4 * HD
    moves = []
    for core in range(2):
        for dy in range(4):
            for dz in range(4):
                index = (pos[0] + dy) % 4 * 4 + (pos[1] + dz) % 4
                image, k = index // 2, index % 2
                r = (image // 2 + 4 - pos[3]) % 4 * 2 + (image % 2 + pos[4]) % 2
                odd = (pos[2] + core) % 2
                moves.append((shares[core].at[dy, dz], blocks.at[odd, r, k]))
    tail = rows - UPPER
    pieces = [
        (0, [(own, 0, 0, rows)], (own, rows)),
        (1, [(other, 0, 0, rows)], (other, rows)),
        (2, [(high, 0, 0, rows)], (high, rows)),
        (3, [(left, 0, 0, rows)], (left, rows)),
        (6, [(low, 0, 0, rows)], (low, rows)),
        (7, [(right, 0, 0, rows)], (right, rows)),
        (4, [(right, cut, 0, UPPER), (left, cut, UPPER, tail)], (left, cut + tail)),
        (5, [(far_right, 0, 0, UPPER), (far_left, 0, UPPER, tail)], (far_left, tail)),
    ]
    waits = []
    for r, spans, (last, at) in pieces:
        mine = [(last.at[at : at + 16, :split], tails.at[r])]
        for ref, src, dst, n in spans:
            here = slice(r * rows + dst, r * rows + dst + n)
            mine.append((ref.at[src : src + n, :split], forward.at[here]))
            mine.append((ref.at[src : src + n, split:], backward.at[here]))
        waits.append((r, len(moves), len(moves) + len(mine)))
        moves += mine
    copies = [
        pltpu.make_async_copy(src, dst, sems.at[k]) for k, (src, dst) in enumerate(moves)
    ]
    for copy in copies:
        copy.start()
    first = pl.multiple_of((pos[3] * 2 + pos[4]) * width, width)
    scale = gains[0:1, pl.ds(first, width)].astype(F32)
    for copy in copies[: waits[0][1]]:
        copy.wait()
    for step, (r, start, stop) in enumerate(waits):
        for copy in copies[start:stop]:
            copy.wait()
        here = slice(r * rows, (r + 1) * rows)
        tail = tails[r].astype(F32)
        stats = from_rows(
            tail[:8, :rows] + tail[8:, :rows] + tail[:8, rows : 2 * rows]
        )
        mean, inverse = stats[:, 0:1], stats[:, 1:2]
        for group in range(4):
            lanes = slice(group * HD, (group + 1) * HD)
            block = blocks.at[group % 2, r, group // 2]
            centred = block[:rows].astype(F32) - mean
            normed[here, lanes] = (centred * inverse * scale[:, lanes]).astype(BF16)
            upstream[here, lanes] = block[rows:]
        if step % 4 == 3:
            here = slice(0, 4 * rows) if step == 3 else slice(4 * rows, 8 * rows)
            one = inner_rows(forward[here], upstream[here])
            two = inner_rows(normed[here], backward[here])
            if step == 3:
                sum_forward[...] = one
                sum_backward[...] = two
            else:
                one = (sum_forward[...] + one).astype(BF16)
                two = (sum_backward[...] + two).astype(BF16)
                g_down[...] = one[:ff]
                g_out[...] = one[ff:]
                g_qkv[...] = two[:, : 3 * HD]
                g_up[...] = two[:, 3 * HD :]


def ring4(block, shift):
    return [block, shift(block, -1), shift(block, 2), shift(block, 1)]


def to_ring(messages, shift):
    return [messages[0], shift(messages[1], 1), shift(messages[2], 2), shift(messages[3], -1)]


def body(tokens, gain, w_qkv, qk_gain, w_up, w_attn_out, w_down, cotangent):
    mp, dp = lax.axis_index("mp"), lax.axis_index("dp")
    rows, ff = tokens.shape[0], w_up.shape[1]
    pos = jnp.stack([mp // 8, mp // 2 % 4, mp % 2, dp // 2, dp % 2]).astype(jnp.int32)

    own = jnp.concatenate([tokens, jnp.broadcast_to(gain[None, :], (16, HD)), cotangent])
    cut, both = rows + 16, 2 * rows + 16
    spread = lax.ppermute(jnp.concatenate([tokens, cotangent]), ("dp", "mp"), SPREAD)
    ring = whole(
        stack_kernel, struct(4, both, HD), ring4(own, shift_z), 1, extra=(spread,)
    )
    share_ring = whole(
        stack_kernel, struct(4, 2 * rows, HD), ring4(spread, shift_z), 1, extra=(ring,)
    )
    rings = whole(
        stack_kernel,
        struct(4, 4, both, HD),
        ring4(ring, shift_y),
        1,
        extra=(share_ring,),
    )

    width = 2 * ff + 4 * HD
    hbm, vmem = [HBM] * 4, [VMEM] * 2
    away, mine, message, sums, d_scales, stats, gains = pl.pallas_call(
        layer_kernel,
        out_shape=(
            struct(32 * rows + 32, HD),
            struct(4, 8, rows, HD),
            struct(cut, width),
            struct(8, rows, kind=F32),
            struct(2, HD, kind=F32),
            struct(rows, HD, kind=F32),
            struct(16, D),
        ),
        in_specs=[SMEM, *vmem, *hbm, VMEM],
        out_specs=[VMEM] * 7,
        scratch_shapes=[
            pltpu.VMEM((rows, D), BF16),
            pltpu.VMEM((cut, D), BF16),
            pltpu.VMEM((cut, 3 * HD + ff), F32),
            *(pltpu.VMEM(w.shape, BF16) for w in (w_qkv, w_up, w_attn_out, w_down)),
            pltpu.SemaphoreType.DMA((4,)),
        ],
        cost_estimate=cost(15),
        compiler_params=pltpu.CompilerParams(vmem_limit_bytes=44 * MIB),
    )(
        pos,
        rings,
        swap_core(rings),
        w_qkv,
        w_up,
        w_attn_out,
        w_down,
        qk_gain,
    )
    other, low, high = swap_z(message), shift_x(message, 1), shift_x(message, -1)
    share_behind = shift_y(share_ring, 1)
    *messages, to_right, to_left = whole(
        pair_sum_kernel,
        [struct(8 * rows + 32, HD)] * 4
        + [struct(cut + UPPER, width), struct(2 * cut - UPPER, width)],
        [mine, swap_core(away), sums, other, low, high],
        1,
        limit=32,
        extra=(share_behind,),
    )
    messages = to_ring(messages, shift_y)
    right, left = shift_x(to_right, 1), shift_x(to_left, -1)
    messages = whole(
        ring_sum_kernel,
        [struct(2 * rows + 32, HD)] * 4,
        messages,
        1,
        extra=(right, left),
    )
    share_last, _ = lax.optimization_barrier((share_ring, messages[0]))
    share_ahead, share_far = shift_y(share_last, -1), shift_y(share_last, 2)
    mixed, d_tokens, scales, shares = whole(
        finish_kernel,
        (
            struct(rows, HD),
            struct(rows, HD),
            struct(8, HD, kind=F32),
            struct(4, 4, 2 * rows, HD),
        ),
        [
            *to_ring(messages, shift_z),
            *(share_ring, share_ahead, share_far, share_behind),
            *(tokens, cotangent, gain[None, :], stats, d_scales),
        ],
        1,
    )
    (upper, lower), _ = lax.optimization_barrier(
        ((right[:UPPER], left[UPPER:cut]), messages[0])
    )
    (upper, lower), _ = lax.optimization_barrier(((upper, lower), mixed))
    far = shift_x(upper, 1), shift_x(lower, -1)
    scales, far = lax.optimization_barrier((scales + swap_z(scales), far))
    scales = sum(ring4(scales, shift_x))
    images = [message, other, high, left, right, *far, low]

    g_attn_out, g_down, g_qkv, g_up = pl.pallas_call(
        grads_kernel,
        out_shape=(
            struct(HD, 4 * HD),
            struct(ff, 4 * HD),
            struct(4 * HD, 3 * HD),
            struct(4 * HD, ff),
        ),
        in_specs=[SMEM, VMEM, *[ANY] * 10],
        out_specs=[VMEM] * 4,
        scratch_shapes=[
            pltpu.VMEM((8 * rows, ff + HD), BF16),
            pltpu.VMEM((8 * rows, 3 * HD + ff), BF16),
            pltpu.VMEM((8, 16, ff + HD), BF16),
            pltpu.VMEM((2, 8, 2, 2 * rows, HD), BF16),
            pltpu.VMEM((8 * rows, 4 * HD), BF16),
            pltpu.VMEM((8 * rows, 4 * HD), BF16),
            pltpu.VMEM((ff + HD, 4 * HD), F32),
            pltpu.VMEM((4 * HD, 3 * HD + ff), F32),
            pltpu.SemaphoreType.DMA((64,)),
        ],
        cost_estimate=cost(8),
        compiler_params=pltpu.CompilerParams(vmem_limit_bytes=28 * MIB),
    )(pos, gains, shares, swap_core(shares), *images)
    return mixed, d_tokens, scales[0], scales[1:3], g_qkv, g_up, g_attn_out, g_down


def solution(mesh):
    in_specs = (
        P("dp", "mp"),
        P("mp"),
        P(None, "mp"),
        P(None, "mp"),
        P(None, "mp"),
        P("mp", None),
        P("mp", None),
        P("dp", "mp"),
    )
    out_specs = (
        P("dp", "mp"),
        P("dp", "mp"),
        P("mp"),
        P(None, "mp"),
        P("dp", "mp"),
        P("dp", "mp"),
        P("mp", "dp"),
        P("mp", "dp"),
    )
    return jax.shard_map(body, mesh=mesh, in_specs=in_specs, out_specs=out_specs, check_vma=False)
```

```python
import functools
import math

import jax
import jax.numpy as jnp
from jax import lax
from jax.experimental import pallas as pl
from jax.experimental.pallas import tpu as pltpu
from jax.sharding import PartitionSpec as P

D = 4096
HD = 128
EPS = 1e-06
F32 = jnp.float32
BF16 = jnp.bfloat16


def mp_perm(dy, dz, dc):
    return [
        (
            (y * 4 + z) * 2 + c,
            ((y + dy) % 4 * 4 + (z + dz) % 4) * 2 + (c + dc) % 2,
        )
        for y in range(4)
        for z in range(4)
        for c in range(2)
    ]


def dp_perm(dx, dz):
    return [
        (x * 2 + z, (x + dx) % 4 * 2 + (z + dz) % 2) for x in range(4) for z in range(2)
    ]


SPREAD = [(i * 32 + m, m // 4 * 32 + i * 4 + m % 4) for i in range(8) for m in range(32)]


def shift_y(block, by):
    return lax.ppermute(block, "mp", mp_perm(by, 0, 0))


def shift_z(block, by):
    return lax.ppermute(block, "mp", mp_perm(0, by, 0))


def swap_core(block):
    return lax.ppermute(block, "mp", mp_perm(0, 0, 1))


def shift_x(block, by):
    return lax.ppermute(block, "dp", dp_perm(by, 0))


def swap_z(block):
    return lax.ppermute(block, "dp", dp_perm(0, 1))


MIB = 1 << 20
UPPER = 144
VMEM = pl.BlockSpec(memory_space=pltpu.VMEM)
SMEM = pl.BlockSpec(memory_space=pltpu.SMEM)
ANY = pl.BlockSpec(memory_space=pl.ANY)
HBM = pl.BlockSpec(memory_space=pltpu.HBM)


def struct(*shape, kind=BF16):
    return jax.ShapeDtypeStruct(shape, kind)


def cost(us):
    return pl.CostEstimate(flops=0, bytes_accessed=int(us * 3.5e6), transcendentals=0)


def whole(kernel, out_shape, operands, us, scalars=0, extra=(), limit=16, scratch=()):
    n = len(operands)

    def run(*refs):
        kernel(*refs[:n], *refs[n + len(extra) :])

    specs = [SMEM] * scalars + [VMEM] * (n - scalars) + [ANY] * len(extra)
    return pl.pallas_call(
        run,
        out_shape=out_shape,
        in_specs=specs,
        out_specs=jax.tree.map(lambda _: VMEM, out_shape),
        scratch_shapes=scratch,
        cost_estimate=cost(us),
        compiler_params=pltpu.CompilerParams(vmem_limit_bytes=limit * MIB),
    )(*operands, *extra)


def inner_rows(left, right):
    return lax.dot_general(left, right, (((0,), (0,)), ((), ())), preferred_element_type=F32)


def cross_last(left, right):
    return lax.dot_general(left, right, (((1,), (1,)), ((), ())), preferred_element_type=F32)


def mean_last(block):
    return jnp.mean(block, axis=-1, keepdims=True)


def as_columns(first, second):
    lane = lax.broadcasted_iota(jnp.int32, (first.shape[0], HD), 1)
    return jnp.where(lane == 0, first, jnp.where(lane == 1, second, 0.0))


def as_rows(columns):
    return jnp.transpose(columns)[:8]


def from_rows(rows):
    pad = jnp.zeros((HD - 8, rows.shape[1]), F32)
    return jnp.transpose(jnp.concatenate([rows, pad]))


def rounded(values):
    return values.astype(BF16).astype(F32)


def stacked(upper, lower):
    twice = jnp.concatenate([upper, lower])
    return twice.astype(BF16)


def packed(rows):
    high = rounded(rows)
    return stacked(high, rows - high)


def unpacked(rows):
    rows = rows.astype(F32)
    return rows[:8] + rows[8:]


def unit_rows(block):
    centred = block - mean_last(block)
    inverse = lax.rsqrt(mean_last(centred * centred) + EPS)
    return centred * inverse, inverse


def unit_rows_back(unit, inverse, grad):
    return inverse * (grad - mean_last(grad) - unit * mean_last(grad * unit))


def place(pos, pieces, span, out, at):
    own, other = pieces
    first = pos[2] == 0
    for y in range(4):
        for z in range(4):
            here = (y + 4 - pos[0]) % 4, (z + 4 - pos[1]) % 4
            mine, came = own[(*here, span)], other[(*here, span)]
            lanes = (y * 4 + z) * 256
            out[at, lanes : lanes + HD] = jnp.where(first, mine, came)
            out[at, lanes + HD : lanes + 256] = jnp.where(first, came, mine)


def first_kernel(tokens, gain, cotangent, own, share):
    n = tokens.shape[0]
    own[:n] = tokens[...]
    own[n : n + 16] = jnp.broadcast_to(gain[...], (16, gain.shape[1]))
    own[n + 16 :] = cotangent[...]
    share[:n] = tokens[...]
    share[n:] = cotangent[...]


def stack_kernel(*refs):
    pieces, (out,) = refs[:4], refs[4:]
    for k, piece in enumerate(pieces):
        out[k] = piece[...]


def layer_kernel(pos, *refs):
    pieces, weights, (qk_gain, *outs) = refs[:2], refs[2:6], refs[6:]
    away, mine, message, sums, scales, stats_ref, gains, *scratch = outs
    image, normed, pre, *held, sems = scratch
    rows = image.shape[0]
    cut = normed.shape[0]
    w_qkv, w_up, w_out, w_down = held
    ff = w_up.shape[1]
    copies = [
        pltpu.make_async_copy(weight, place, sems.at[k])
        for k, (weight, place) in enumerate(zip(weights, held))
    ]
    for copy in copies:
        copy.start()

    place(pos, pieces, slice(0, rows), image, slice(0, rows))
    place(pos, pieces, slice(rows, cut), normed, slice(rows, cut))
    step = 64
    for r in range(0, rows, step):
        values = image[r : r + step].astype(F32)
        mean = mean_last(values)
        centred = values - mean
        inverse = lax.rsqrt(mean_last(centred * centred) + EPS)
        scale = normed[rows : rows + 1].astype(F32)
        normed[r : r + step] = (centred * inverse * scale).astype(BF16)
        stats_ref[r : r + step] = as_columns(mean, inverse)
    gains[...] = normed[rows:]
    stats = as_rows(stats_ref[...])
    high = rounded(stats)
    middle = rounded(stats - high)
    message[rows:, :rows] = stacked(high, middle)
    message[rows:, rows : 2 * rows] = stacked(stats - high - middle, jnp.zeros_like(stats))
    message[rows:, 2 * rows :] = jnp.zeros((cut - rows, message.shape[1] - 2 * rows), BF16)

    copies[0].wait()
    pre[:, : 3 * HD] = jnp.dot(normed[...], w_qkv[...], preferred_element_type=F32)
    copies[1].wait()
    pre[:, 3 * HD :] = jnp.dot(normed[...], w_up[...], preferred_element_type=F32)
    place(pos, pieces, slice(cut, cut + rows), image, slice(0, rows))
    up = pre[:rows, 3 * HD :]
    below = 0.5 * (1.0 + lax.erf(up * math.sqrt(0.5)))
    message[:rows, :ff] = (up * below).astype(BF16)
    unit_q, inverse_q = unit_rows(pre[:rows, :HD])
    unit_k, inverse_k = unit_rows(pre[:rows, HD : 2 * HD])
    q_normed = (unit_q * qk_gain[0:1]).astype(BF16)
    k_normed = (unit_k * qk_gain[1:2]).astype(BF16)
    values_in = pre[:rows, 2 * HD : 3 * HD].astype(BF16)
    scores = cross_last(q_normed, k_normed) / math.sqrt(HD)
    powers = jnp.exp(scores - jnp.max(scores, axis=-1, keepdims=True))
    probs = powers / jnp.sum(powers, axis=-1, keepdims=True)
    message[:rows, ff : ff + HD] = jnp.dot(
        probs.astype(BF16), values_in, preferred_element_type=F32
    ).astype(BF16)

    d_qkv = message.at[:rows, ff + HD : ff + 4 * HD]
    copies[2].wait()
    d_att = cross_last(image[...], w_out[...]).astype(BF16)
    copies[3].wait()
    d_act = cross_last(image[...], w_down[...])
    slope = below + up * jnp.exp(-0.5 * up * up) * (1.0 / math.sqrt(2.0 * math.pi))
    message[:rows, ff + 4 * HD :] = (d_act * slope).astype(BF16)
    d_qkv[:, 2 * HD :] = inner_rows(probs.astype(BF16), d_att).astype(BF16)
    d_probs = rounded(cross_last(d_att, values_in))
    d_scores = probs * (d_probs - jnp.sum(d_probs * probs, axis=-1, keepdims=True))
    d_scores = (d_scores / math.sqrt(HD)).astype(BF16)
    d_q = rounded(jnp.dot(d_scores, k_normed, preferred_element_type=F32))
    d_k = rounded(inner_rows(d_scores, q_normed))
    d_qkv[:, :HD] = unit_rows_back(unit_q, inverse_q, d_q * qk_gain[0:1]).astype(BF16)
    d_qkv[:, HD : 2 * HD] = unit_rows_back(unit_k, inverse_k, d_k * qk_gain[1:2]).astype(BF16)
    scales[0:1] = jnp.sum(d_q * unit_q, axis=0, keepdims=True)
    scales[1:2] = jnp.sum(d_k * unit_k, axis=0, keepdims=True)

    values = message[:rows, ff + HD :].astype(F32)
    first = jnp.sum(values * pre[rows : rows + 1], axis=1, keepdims=True)
    second = jnp.sum(values * pre[:rows], axis=1, keepdims=True)
    sums[...] = as_rows(as_columns(first, second))

    tail = packed(sums[...])
    away[32 * rows : 32 * rows + 16] = tail[:, :HD]
    away[32 * rows + 16 :] = tail[:, HD:]
    mine_first = pos[2] == 0

    def put(dy, at, block):
        block = block.astype(BF16)
        low, high = block[:, :HD], block[:, HD:]
        mine[dy, at] = jnp.where(mine_first, low, high)
        start = (dy * 8 + at) * rows
        away[start : start + rows] = jnp.where(mine_first, high, low)

    for dy in range(4):
        for dz in range(4):
            index = (pos[0] + dy) % 4 * 4 + (pos[1] + dz) % 4
            at = pl.ds(pl.multiple_of(index * 256, 256), 256)
            put(
                dy,
                dz,
                jnp.dot(message[:rows, :ff], w_down[:, at], preferred_element_type=F32)
                + jnp.dot(
                    message[:rows, ff : ff + HD], w_out[:, at], preferred_element_type=F32
                ),
            )
            put(
                dy,
                4 + dz,
                cross_last(message[:rows, ff + HD : ff + 4 * HD], w_qkv[at, :])
                + cross_last(message[:rows, ff + 4 * HD :], w_up[at, :]),
            )


def pair_sum_kernel(mine, came, sums, other, low, high, *outs):
    *outs, to_right, to_left = outs
    rows = other.shape[0]
    to_right[:rows] = other[...]
    to_right[rows:] = low[:UPPER]
    to_left[:rows] = other[...]
    to_left[rows:] = high[UPPER:]
    n = mine.shape[2]
    tail = packed(sums[...] + tail_sums([came], 32 * n))
    for dy, out in enumerate(outs):
        for at in range(8):
            start = (dy * 8 + at) * n
            both = mine[dy, at].astype(F32) + came[start : start + n].astype(F32)
            out[at * n : (at + 1) * n] = both.astype(BF16)
        out[8 * n : 8 * n + 16] = tail[:, :HD]
        out[8 * n + 16 :] = tail[:, HD:]


def tail_sums(parts, n):
    total = None
    for part in parts:
        one = jnp.concatenate([unpacked(part[n : n + 16]), unpacked(part[n + 16 :])], axis=1)
        total = one if total is None else total + one
    return total


def ring_sum_kernel(*refs):
    parts, outs = refs[:4], refs[4:]
    n = (outs[0].shape[0] - 32) // 2
    tail = packed(tail_sums(parts, 8 * n))
    for dz, out in enumerate(outs):
        for half in range(2):
            at = slice((half * 4 + dz) * n, (half * 4 + dz + 1) * n)
            total = parts[0][at].astype(F32)
            for part in parts[1:]:
                total = total + part[at].astype(F32)
            out[half * n : (half + 1) * n] = total.astype(BF16)
        out[2 * n : 2 * n + 16] = tail[:, :HD]
        out[2 * n + 16 :] = tail[:, HD:]


def finish_kernel(*refs):
    parts, shares, refs = refs[:4], refs[4:7], refs[7:]
    tokens, cotangent, gain, stats, d_scales, mixed, d_tokens, scales, near = refs
    for k, share in enumerate(shares):
        near[k] = share[...]
    n = tokens.shape[0]
    branch = parts[0][:n].astype(F32)
    d_normed = parts[0][n : 2 * n].astype(F32)
    for part in parts[1:]:
        branch = branch + part[:n].astype(F32)
        d_normed = d_normed + part[n : 2 * n].astype(F32)
    image = tokens[...].astype(F32)
    mixed[...] = (image + branch).astype(BF16)
    means = from_rows(tail_sums(parts, 2 * n)) / D
    mean, inverse = stats[:, 0:1], stats[:, 1:2]
    unit = (image - mean) * inverse
    scaled = d_normed * gain[...].astype(F32)
    d_tokens[...] = (
        cotangent[...].astype(F32) + inverse * (scaled - means[:, 0:1] - unit * means[:, 1:2])
    ).astype(BF16)
    scales[...] = jnp.zeros_like(scales)
    scales[0:1] = jnp.sum(d_normed * unit, axis=0, keepdims=True)
    scales[1:3] = d_scales[...]


def image_of(pos, r):
    return (pos[3] + r // 2) % 4 * 2 + (pos[4] + r) % 2


def grads_kernel(pos, gains, *refs):
    shares, (own, other, high, left, right, far_other, low) = refs[:4], refs[4:11]
    g_out, g_down, g_qkv, g_up, *scratch = refs[11:]
    forward, backward, tails, blocks, normed, upstream = scratch
    rows = blocks.shape[3] // 2
    ff = g_down.shape[0]
    cut, split, width = rows + 16, ff + HD, 4 * HD
    for core in range(2):
        near, share_far = shares[core * 2 : core * 2 + 2]
        share_rings = [near.at[0], near.at[1], share_far, near.at[2]]
        for dy in range(4):
            for dz in range(4):
                index = (pos[0] + dy) % 4 * 4 + (pos[1] + dz) % 4
                image, k = index // 2, index % 2
                r = (image // 2 + 4 - pos[3]) % 4 * 2 + (image % 2 + pos[4]) % 2
                odd = (pos[2] + core) % 2
                blocks[odd, r, k] = share_rings[dy][dz]
    pieces = [
        (own, [(0, 0, rows)], rows),
        (other, [(0, 0, rows)], rows),
        (high, [(0, 0, rows)], rows),
        (left, [(0, 0, rows)], rows),
        (right, [(cut, 0, UPPER)], None),
        (far_other, [(0, 0, rows)], rows),
        (low, [(0, 0, rows)], rows),
        (right, [(0, 0, rows)], rows),
        (left, [(cut, UPPER, rows - UPPER)], 2 * cut - UPPER - 16),
    ]
    for r, (ref, spans, tail) in enumerate(pieces):
        r = r if r < 8 else 4
        for src, dst, n in spans:
            here = slice(r * rows + dst, r * rows + dst + n)
            forward[here] = ref[src : src + n, :split]
            backward[here] = ref[src : src + n, split:]
        if tail is not None:
            tails[r] = ref[tail : tail + 16, :split]
    first = pl.multiple_of((pos[3] * 2 + pos[4]) * width, width)
    scale = gains[0:1, pl.ds(first, width)].astype(F32)
    for r in range(8):
        here = slice(r * rows, (r + 1) * rows)
        tail = tails[r].astype(F32)
        stats = from_rows(
            tail[:8, :rows] + tail[8:, :rows] + tail[:8, rows : 2 * rows]
        )
        mean, inverse = stats[:, 0:1], stats[:, 1:2]
        for group in range(4):
            lanes = slice(group * HD, (group + 1) * HD)
            block = blocks.at[group % 2, r, group // 2]
            centred = block[:rows].astype(F32) - mean
            normed[here, lanes] = (centred * inverse * scale[:, lanes]).astype(BF16)
            upstream[here, lanes] = block[rows:]
    grads = inner_rows(forward[...], upstream[...]).astype(BF16)
    g_down[...] = grads[:ff]
    g_out[...] = grads[ff:]
    grads = inner_rows(normed[...], backward[...]).astype(BF16)
    g_qkv[...] = grads[:, : 3 * HD]
    g_up[...] = grads[:, 3 * HD :]


def ring4(block, shift):
    return [block, shift(block, -1), shift(block, 2), shift(block, 1)]


def to_ring(messages, shift):
    return [messages[0], shift(messages[1], 1), shift(messages[2], 2), shift(messages[3], -1)]


def body(tokens, gain, w_qkv, qk_gain, w_up, w_attn_out, w_down, cotangent):
    mp, dp = lax.axis_index("mp"), lax.axis_index("dp")
    rows, ff = tokens.shape[0], w_up.shape[1]
    pos = jnp.stack([mp // 8, mp // 2 % 4, mp % 2, dp // 2, dp % 2]).astype(jnp.int32)

    cut, both = rows + 16, 2 * rows + 16
    own, share = whole(
        first_kernel,
        (struct(both, HD), struct(2 * rows, HD)),
        [tokens, gain[None, :], cotangent],
        1,
    )
    spread = lax.ppermute(share, ("dp", "mp"), SPREAD)
    ring = whole(
        stack_kernel, struct(4, both, HD), ring4(own, shift_z), 1, extra=(spread,)
    )
    share_ring = whole(
        stack_kernel, struct(4, 2 * rows, HD), ring4(spread, shift_z), 1, extra=(ring,)
    )
    rings = whole(
        stack_kernel,
        struct(4, 4, both, HD),
        ring4(ring, shift_y),
        1,
        extra=(share_ring,),
    )

    width = 2 * ff + 4 * HD
    hbm, vmem = [HBM] * 4, [VMEM] * 2
    away, mine, message, sums, d_scales, stats, gains = pl.pallas_call(
        layer_kernel,
        out_shape=(
            struct(32 * rows + 32, HD),
            struct(4, 8, rows, HD),
            struct(cut, width),
            struct(8, rows, kind=F32),
            struct(2, HD, kind=F32),
            struct(rows, HD, kind=F32),
            struct(16, D),
        ),
        in_specs=[SMEM, *vmem, *hbm, VMEM],
        out_specs=[VMEM] * 7,
        scratch_shapes=[
            pltpu.VMEM((rows, D), BF16),
            pltpu.VMEM((cut, D), BF16),
            pltpu.VMEM((cut, 3 * HD + ff), F32),
            *(pltpu.VMEM(w.shape, BF16) for w in (w_qkv, w_up, w_attn_out, w_down)),
            pltpu.SemaphoreType.DMA((4,)),
        ],
        cost_estimate=cost(15),
        compiler_params=pltpu.CompilerParams(vmem_limit_bytes=44 * MIB),
    )(
        pos,
        rings,
        swap_core(rings),
        w_qkv,
        w_up,
        w_attn_out,
        w_down,
        qk_gain,
    )
    other, low, high = swap_z(message), shift_x(message, 1), shift_x(message, -1)
    share_behind = shift_y(share_ring, 1)
    *messages, to_right, to_left = whole(
        pair_sum_kernel,
        [struct(8 * rows + 32, HD)] * 4
        + [struct(cut + UPPER, width), struct(2 * cut - UPPER, width)],
        [mine, swap_core(away), sums, other, low, high],
        1,
        limit=32,
        extra=(share_behind,),
    )
    right, left = shift_x(to_right, 1), shift_x(to_left, -1)
    messages = whole(
        ring_sum_kernel,
        [struct(2 * rows + 32, HD)] * 4,
        to_ring(messages, shift_y),
        1,
        extra=(right, left),
    )
    (last, share_last), _ = lax.optimization_barrier(((right[:cut], share_ring), messages[0]))
    far_other, share_ahead = shift_x(last, 1), shift_y(share_last, -1)
    mixed, d_tokens, scales, near = whole(
        finish_kernel,
        (
            struct(rows, HD),
            struct(rows, HD),
            struct(8, HD, kind=F32),
            struct(3, 4, 2 * rows, HD),
        ),
        [
            *to_ring(messages, shift_z),
            *(share_ring, share_ahead, share_behind),
            *(tokens, cotangent, gain[None, :], stats, d_scales),
        ],
        1,
        extra=(far_other,),
    )
    share_last, _ = lax.optimization_barrier((share_ring, mixed))
    share_far = shift_y(share_last, 2)
    scales = sum(ring4(scales + swap_z(scales), shift_x))
    share_last, _ = lax.optimization_barrier((share_far, scales))
    shares = [near, share_far, swap_core(near), swap_core(share_last)]
    images = [message, other, high, left, right, far_other, low]

    g_attn_out, g_down, g_qkv, g_up = pl.pallas_call(
        grads_kernel,
        out_shape=(
            struct(HD, 4 * HD),
            struct(ff, 4 * HD),
            struct(4 * HD, 3 * HD),
            struct(4 * HD, ff),
        ),
        in_specs=[SMEM, *[VMEM] * 12],
        out_specs=[VMEM] * 4,
        scratch_shapes=[
            pltpu.VMEM((8 * rows, ff + HD), BF16),
            pltpu.VMEM((8 * rows, 3 * HD + ff), BF16),
            pltpu.VMEM((8, 16, ff + HD), BF16),
            pltpu.VMEM((2, 8, 2, 2 * rows, HD), BF16),
            pltpu.VMEM((8 * rows, 4 * HD), BF16),
            pltpu.VMEM((8 * rows, 4 * HD), BF16),
        ],
        cost_estimate=cost(8),
        compiler_params=pltpu.CompilerParams(vmem_limit_bytes=36 * MIB),
    )(pos, gains, *shares, *images)
    return mixed, d_tokens, scales[0], scales[1:3], g_qkv, g_up, g_attn_out, g_down


def solution(mesh):
    in_specs = (
        P("dp", "mp"),
        P("mp"),
        P(None, "mp"),
        P(None, "mp"),
        P(None, "mp"),
        P("mp", None),
        P("mp", None),
        P("dp", "mp"),
    )
    out_specs = (
        P("dp", "mp"),
        P("dp", "mp"),
        P("mp"),
        P(None, "mp"),
        P("dp", "mp"),
        P("dp", "mp"),
        P("mp", "dp"),
        P("mp", "dp"),
    )
    return jax.shard_map(body, mesh=mesh, in_specs=in_specs, out_specs=out_specs, check_vma=False)
```

```python
import functools
import math

import jax
import jax.numpy as jnp
from jax import lax
from jax.experimental import pallas as pl
from jax.experimental.pallas import tpu as pltpu
from jax.sharding import PartitionSpec as P

D = 4096
HD = 128
EPS = 1e-06
F32 = jnp.float32
BF16 = jnp.bfloat16


def mp_perm(dy, dz, dc):
    return [
        (
            (y * 4 + z) * 2 + c,
            ((y + dy) % 4 * 4 + (z + dz) % 4) * 2 + (c + dc) % 2,
        )
        for y in range(4)
        for z in range(4)
        for c in range(2)
    ]


def dp_perm(dx, dz):
    return [
        (x * 2 + z, (x + dx) % 4 * 2 + (z + dz) % 2) for x in range(4) for z in range(2)
    ]


SPREAD = [(i * 32 + m, m // 4 * 32 + i * 4 + m % 4) for i in range(8) for m in range(32)]


def shift_y(block, by):
    return lax.ppermute(block, "mp", mp_perm(by, 0, 0))


def shift_z(block, by):
    return lax.ppermute(block, "mp", mp_perm(0, by, 0))


def swap_core(block):
    return lax.ppermute(block, "mp", mp_perm(0, 0, 1))


def shift_x(block, by):
    return lax.ppermute(block, "dp", dp_perm(by, 0))


def swap_z(block):
    return lax.ppermute(block, "dp", dp_perm(0, 1))


MIB = 1 << 20
UPPER = 144
VMEM = pl.BlockSpec(memory_space=pltpu.VMEM)
SMEM = pl.BlockSpec(memory_space=pltpu.SMEM)
ANY = pl.BlockSpec(memory_space=pl.ANY)
HBM = pl.BlockSpec(memory_space=pltpu.HBM)


def struct(*shape, kind=BF16):
    return jax.ShapeDtypeStruct(shape, kind)


def cost(us):
    return pl.CostEstimate(flops=0, bytes_accessed=int(us * 3.5e6), transcendentals=0)


def whole(kernel, out_shape, operands, us, scalars=0, extra=(), limit=16, scratch=()):
    n = len(operands)

    def run(*refs):
        kernel(*refs[:n], *refs[n + len(extra) :])

    specs = [SMEM] * scalars + [VMEM] * (n - scalars) + [ANY] * len(extra)
    return pl.pallas_call(
        run,
        out_shape=out_shape,
        in_specs=specs,
        out_specs=jax.tree.map(lambda _: VMEM, out_shape),
        scratch_shapes=scratch,
        cost_estimate=cost(us),
        compiler_params=pltpu.CompilerParams(vmem_limit_bytes=limit * MIB),
    )(*operands, *extra)


def inner_rows(left, right):
    return lax.dot_general(left, right, (((0,), (0,)), ((), ())), preferred_element_type=F32)


def cross_last(left, right):
    return lax.dot_general(left, right, (((1,), (1,)), ((), ())), preferred_element_type=F32)


def mean_last(block):
    return jnp.mean(block, axis=-1, keepdims=True)


def as_columns(first, second):
    lane = lax.broadcasted_iota(jnp.int32, (first.shape[0], HD), 1)
    return jnp.where(lane == 0, first, jnp.where(lane == 1, second, 0.0))


def as_rows(columns):
    return jnp.transpose(columns)[:8]


def from_rows(rows):
    pad = jnp.zeros((HD - 8, rows.shape[1]), F32)
    return jnp.transpose(jnp.concatenate([rows, pad]))


def rounded(values):
    return values.astype(BF16).astype(F32)


def stacked(upper, lower):
    twice = jnp.concatenate([upper, lower])
    return twice.astype(BF16)


def packed(rows):
    high = rounded(rows)
    return stacked(high, rows - high)


def unpacked(rows):
    rows = rows.astype(F32)
    return rows[:8] + rows[8:]


def unit_rows(block):
    centred = block - mean_last(block)
    inverse = lax.rsqrt(mean_last(centred * centred) + EPS)
    return centred * inverse, inverse


def unit_rows_back(unit, inverse, grad):
    return inverse * (grad - mean_last(grad) - unit * mean_last(grad * unit))


def place(pos, pieces, span, out, at):
    own, other = pieces
    first = pos[2] == 0
    for y in range(4):
        for z in range(4):
            here = (y + 4 - pos[0]) % 4, (z + 4 - pos[1]) % 4
            mine, came = own[(*here, span)], other[(*here, span)]
            lanes = (y * 4 + z) * 256
            out[at, lanes : lanes + HD] = jnp.where(first, mine, came)
            out[at, lanes + HD : lanes + 256] = jnp.where(first, came, mine)


def stack_kernel(*refs):
    pieces, (out,) = refs[:4], refs[4:]
    for k, piece in enumerate(pieces):
        out[k] = piece[...]


def layer_kernel(pos, *refs):
    pieces, weights, (qk_gain, *outs) = refs[:2], refs[2:6], refs[6:]
    away, mine, message, sums, scales, stats_ref, gains, *scratch = outs
    image, normed, pre, *held, sems = scratch
    rows = image.shape[0]
    cut = normed.shape[0]
    w_qkv, w_up, w_out, w_down = held
    ff = w_up.shape[1]
    copies = [
        pltpu.make_async_copy(weight, place, sems.at[k])
        for k, (weight, place) in enumerate(zip(weights, held))
    ]
    for copy in copies:
        copy.start()

    place(pos, pieces, slice(0, rows), image, slice(0, rows))
    place(pos, pieces, slice(rows, cut), normed, slice(rows, cut))
    step = 64
    for r in range(0, rows, step):
        values = image[r : r + step].astype(F32)
        mean = mean_last(values)
        centred = values - mean
        inverse = lax.rsqrt(mean_last(centred * centred) + EPS)
        scale = normed[rows : rows + 1].astype(F32)
        normed[r : r + step] = (centred * inverse * scale).astype(BF16)
        stats_ref[r : r + step] = as_columns(mean, inverse)
    gains[...] = normed[rows:]
    stats = as_rows(stats_ref[...])
    high = rounded(stats)
    middle = rounded(stats - high)
    message[rows:, :rows] = stacked(high, middle)
    message[rows:, rows : 2 * rows] = stacked(stats - high - middle, jnp.zeros_like(stats))
    message[rows:, 2 * rows :] = jnp.zeros((cut - rows, message.shape[1] - 2 * rows), BF16)

    copies[0].wait()
    pre[:, : 3 * HD] = jnp.dot(normed[...], w_qkv[...], preferred_element_type=F32)
    copies[1].wait()
    pre[:, 3 * HD :] = jnp.dot(normed[...], w_up[...], preferred_element_type=F32)
    place(pos, pieces, slice(cut, cut + rows), image, slice(0, rows))
    up = pre[:rows, 3 * HD :]
    below = 0.5 * (1.0 + lax.erf(up * math.sqrt(0.5)))
    message[:rows, :ff] = (up * below).astype(BF16)
    unit_q, inverse_q = unit_rows(pre[:rows, :HD])
    unit_k, inverse_k = unit_rows(pre[:rows, HD : 2 * HD])
    q_normed = (unit_q * qk_gain[0:1]).astype(BF16)
    k_normed = (unit_k * qk_gain[1:2]).astype(BF16)
    values_in = pre[:rows, 2 * HD : 3 * HD].astype(BF16)
    scores = cross_last(q_normed, k_normed) / math.sqrt(HD)
    powers = jnp.exp(scores - jnp.max(scores, axis=-1, keepdims=True))
    probs = powers / jnp.sum(powers, axis=-1, keepdims=True)
    message[:rows, ff : ff + HD] = jnp.dot(
        probs.astype(BF16), values_in, preferred_element_type=F32
    ).astype(BF16)

    d_qkv = message.at[:rows, ff + HD : ff + 4 * HD]
    copies[2].wait()
    d_att = cross_last(image[...], w_out[...]).astype(BF16)
    copies[3].wait()
    d_act = cross_last(image[...], w_down[...])
    slope = below + up * jnp.exp(-0.5 * up * up) * (1.0 / math.sqrt(2.0 * math.pi))
    message[:rows, ff + 4 * HD :] = (d_act * slope).astype(BF16)
    d_qkv[:, 2 * HD :] = inner_rows(probs.astype(BF16), d_att).astype(BF16)
    d_probs = rounded(cross_last(d_att, values_in))
    d_scores = probs * (d_probs - jnp.sum(d_probs * probs, axis=-1, keepdims=True))
    d_scores = (d_scores / math.sqrt(HD)).astype(BF16)
    d_q = rounded(jnp.dot(d_scores, k_normed, preferred_element_type=F32))
    d_k = rounded(inner_rows(d_scores, q_normed))
    d_qkv[:, :HD] = unit_rows_back(unit_q, inverse_q, d_q * qk_gain[0:1]).astype(BF16)
    d_qkv[:, HD : 2 * HD] = unit_rows_back(unit_k, inverse_k, d_k * qk_gain[1:2]).astype(BF16)
    scales[0:1] = jnp.sum(d_q * unit_q, axis=0, keepdims=True)
    scales[1:2] = jnp.sum(d_k * unit_k, axis=0, keepdims=True)

    values = message[:rows, ff + HD :].astype(F32)
    first = jnp.sum(values * pre[rows : rows + 1], axis=1, keepdims=True)
    second = jnp.sum(values * pre[:rows], axis=1, keepdims=True)
    sums[...] = as_rows(as_columns(first, second))

    tail = packed(sums[...])
    away[32 * rows : 32 * rows + 16] = tail[:, :HD]
    away[32 * rows + 16 :] = tail[:, HD:]
    mine_first = pos[2] == 0

    def put(dy, at, block):
        block = block.astype(BF16)
        low, high = block[:, :HD], block[:, HD:]
        mine[dy, at] = jnp.where(mine_first, low, high)
        start = (dy * 8 + at) * rows
        away[start : start + rows] = jnp.where(mine_first, high, low)

    for dy in range(4):
        for dz in range(4):
            index = (pos[0] + dy) % 4 * 4 + (pos[1] + dz) % 4
            at = pl.ds(pl.multiple_of(index * 256, 256), 256)
            put(
                dy,
                dz,
                jnp.dot(message[:rows, :ff], w_down[:, at], preferred_element_type=F32)
                + jnp.dot(
                    message[:rows, ff : ff + HD], w_out[:, at], preferred_element_type=F32
                ),
            )
            put(
                dy,
                4 + dz,
                cross_last(message[:rows, ff + HD : ff + 4 * HD], w_qkv[at, :])
                + cross_last(message[:rows, ff + 4 * HD :], w_up[at, :]),
            )


def pair_sum_kernel(mine, came, sums, other, low, high, *outs):
    *outs, to_right, to_left = outs
    rows = other.shape[0]
    to_right[:rows] = other[...]
    to_right[rows:] = low[:UPPER]
    to_left[:rows] = other[...]
    to_left[rows:] = high[UPPER:]
    n = mine.shape[2]
    tail = packed(sums[...] + tail_sums([came], 32 * n))
    for dy, out in enumerate(outs):
        for at in range(8):
            start = (dy * 8 + at) * n
            both = mine[dy, at].astype(F32) + came[start : start + n].astype(F32)
            out[at * n : (at + 1) * n] = both.astype(BF16)
        out[8 * n : 8 * n + 16] = tail[:, :HD]
        out[8 * n + 16 :] = tail[:, HD:]


def tail_sums(parts, n):
    total = None
    for part in parts:
        one = jnp.concatenate([unpacked(part[n : n + 16]), unpacked(part[n + 16 :])], axis=1)
        total = one if total is None else total + one
    return total


def ring_sum_kernel(*refs):
    parts, outs = refs[:4], refs[4:]
    n = (outs[0].shape[0] - 32) // 2
    tail = packed(tail_sums(parts, 8 * n))
    for dz, out in enumerate(outs):
        for half in range(2):
            at = slice((half * 4 + dz) * n, (half * 4 + dz + 1) * n)
            total = parts[0][at].astype(F32)
            for part in parts[1:]:
                total = total + part[at].astype(F32)
            out[half * n : (half + 1) * n] = total.astype(BF16)
        out[2 * n : 2 * n + 16] = tail[:, :HD]
        out[2 * n + 16 :] = tail[:, HD:]


def finish_kernel(*refs):
    parts, shares, refs = refs[:4], refs[4:7], refs[7:]
    tokens, cotangent, gain, stats, d_scales, mixed, d_tokens, scales, near = refs
    for k, share in enumerate(shares):
        near[k] = share[...]
    n = tokens.shape[0]
    branch = parts[0][:n].astype(F32)
    d_normed = parts[0][n : 2 * n].astype(F32)
    for part in parts[1:]:
        branch = branch + part[:n].astype(F32)
        d_normed = d_normed + part[n : 2 * n].astype(F32)
    image = tokens[...].astype(F32)
    mixed[...] = (image + branch).astype(BF16)
    means = from_rows(tail_sums(parts, 2 * n)) / D
    mean, inverse = stats[:, 0:1], stats[:, 1:2]
    unit = (image - mean) * inverse
    scaled = d_normed * gain[...].astype(F32)
    d_tokens[...] = (
        cotangent[...].astype(F32) + inverse * (scaled - means[:, 0:1] - unit * means[:, 1:2])
    ).astype(BF16)
    scales[...] = jnp.zeros_like(scales)
    scales[0:1] = jnp.sum(d_normed * unit, axis=0, keepdims=True)
    scales[1:3] = d_scales[...]


def image_of(pos, r):
    return (pos[3] + r // 2) % 4 * 2 + (pos[4] + r) % 2


def grads_kernel(pos, gains, *refs):
    shares, (own, other, high, left, right, far_other, low) = refs[:4], refs[4:11]
    g_out, g_down, g_qkv, g_up, *scratch = refs[11:]
    forward, backward, tails, blocks, normed, upstream = scratch
    rows = blocks.shape[3] // 2
    ff = g_down.shape[0]
    cut, split, width = rows + 16, ff + HD, 4 * HD
    for core in range(2):
        near, share_far = shares[core * 2 : core * 2 + 2]
        share_rings = [near.at[0], near.at[1], share_far, near.at[2]]
        for dy in range(4):
            for dz in range(4):
                index = (pos[0] + dy) % 4 * 4 + (pos[1] + dz) % 4
                image, k = index // 2, index % 2
                r = (image // 2 + 4 - pos[3]) % 4 * 2 + (image % 2 + pos[4]) % 2
                odd = (pos[2] + core) % 2
                blocks[odd, r, k] = share_rings[dy][dz]
    pieces = [
        (own, [(0, 0, rows)], rows),
        (other, [(0, 0, rows)], rows),
        (high, [(0, 0, rows)], rows),
        (left, [(0, 0, rows)], rows),
        (right, [(cut, 0, UPPER)], None),
        (far_other, [(0, 0, rows)], rows),
        (low, [(0, 0, rows)], rows),
        (right, [(0, 0, rows)], rows),
        (left, [(cut, UPPER, rows - UPPER)], 2 * cut - UPPER - 16),
    ]
    for r, (ref, spans, tail) in enumerate(pieces):
        r = r if r < 8 else 4
        for src, dst, n in spans:
            here = slice(r * rows + dst, r * rows + dst + n)
            forward[here] = ref[src : src + n, :split]
            backward[here] = ref[src : src + n, split:]
        if tail is not None:
            tails[r] = ref[tail : tail + 16, :split]
    first = pl.multiple_of((pos[3] * 2 + pos[4]) * width, width)
    scale = gains[0:1, pl.ds(first, width)].astype(F32)
    for r in range(8):
        here = slice(r * rows, (r + 1) * rows)
        tail = tails[r].astype(F32)
        stats = from_rows(
            tail[:8, :rows] + tail[8:, :rows] + tail[:8, rows : 2 * rows]
        )
        mean, inverse = stats[:, 0:1], stats[:, 1:2]
        for group in range(4):
            lanes = slice(group * HD, (group + 1) * HD)
            block = blocks.at[group % 2, r, group // 2]
            centred = block[:rows].astype(F32) - mean
            normed[here, lanes] = (centred * inverse * scale[:, lanes]).astype(BF16)
            upstream[here, lanes] = block[rows:]
    grads = inner_rows(forward[...], upstream[...]).astype(BF16)
    g_down[...] = grads[:ff]
    g_out[...] = grads[ff:]
    grads = inner_rows(normed[...], backward[...]).astype(BF16)
    g_qkv[...] = grads[:, : 3 * HD]
    g_up[...] = grads[:, 3 * HD :]


def ring4(block, shift):
    return [block, shift(block, -1), shift(block, 2), shift(block, 1)]


def to_ring(messages, shift):
    return [messages[0], shift(messages[1], 1), shift(messages[2], 2), shift(messages[3], -1)]


def body(tokens, gain, w_qkv, qk_gain, w_up, w_attn_out, w_down, cotangent):
    mp, dp = lax.axis_index("mp"), lax.axis_index("dp")
    rows, ff = tokens.shape[0], w_up.shape[1]
    pos = jnp.stack([mp // 8, mp // 2 % 4, mp % 2, dp // 2, dp % 2]).astype(jnp.int32)

    cut, both = rows + 16, 2 * rows + 16
    own = jnp.concatenate([tokens, jnp.broadcast_to(gain[None, :], (16, HD)), cotangent])
    spread = lax.ppermute(jnp.concatenate([tokens, cotangent]), ("dp", "mp"), SPREAD)
    ring = whole(
        stack_kernel, struct(4, both, HD), ring4(own, shift_z), 1, extra=(spread,)
    )
    share_ring = whole(
        stack_kernel, struct(4, 2 * rows, HD), ring4(spread, shift_z), 1, extra=(ring,)
    )
    rings = whole(
        stack_kernel,
        struct(4, 4, both, HD),
        ring4(ring, shift_y),
        1,
        extra=(share_ring,),
    )

    width = 2 * ff + 4 * HD
    hbm, vmem = [HBM] * 4, [VMEM] * 2
    away, mine, message, sums, d_scales, stats, gains = pl.pallas_call(
        layer_kernel,
        out_shape=(
            struct(32 * rows + 32, HD),
            struct(4, 8, rows, HD),
            struct(cut, width),
            struct(8, rows, kind=F32),
            struct(2, HD, kind=F32),
            struct(rows, HD, kind=F32),
            struct(16, D),
        ),
        in_specs=[SMEM, *vmem, *hbm, VMEM],
        out_specs=[VMEM] * 7,
        scratch_shapes=[
            pltpu.VMEM((rows, D), BF16),
            pltpu.VMEM((cut, D), BF16),
            pltpu.VMEM((cut, 3 * HD + ff), F32),
            *(pltpu.VMEM(w.shape, BF16) for w in (w_qkv, w_up, w_attn_out, w_down)),
            pltpu.SemaphoreType.DMA((4,)),
        ],
        cost_estimate=cost(15),
        compiler_params=pltpu.CompilerParams(vmem_limit_bytes=44 * MIB),
    )(
        pos,
        rings,
        swap_core(rings),
        w_qkv,
        w_up,
        w_attn_out,
        w_down,
        qk_gain,
    )
    other, low, high = swap_z(message), shift_x(message, 1), shift_x(message, -1)
    share_behind = shift_y(share_ring, 1)
    *messages, to_right, to_left = whole(
        pair_sum_kernel,
        [struct(8 * rows + 32, HD)] * 4
        + [struct(cut + UPPER, width), struct(2 * cut - UPPER, width)],
        [mine, swap_core(away), sums, other, low, high],
        1,
        limit=32,
        extra=(share_behind,),
    )
    right, left = shift_x(to_right, 1), shift_x(to_left, -1)
    messages = whole(
        ring_sum_kernel,
        [struct(2 * rows + 32, HD)] * 4,
        to_ring(messages, shift_y),
        1,
        extra=(right, left),
    )
    (last, share_last), _ = lax.optimization_barrier(((right[:cut], share_ring), messages[0]))
    far_other, share_ahead = shift_x(last, 1), shift_y(share_last, -1)
    mixed, d_tokens, scales, near = whole(
        finish_kernel,
        (
            struct(rows, HD),
            struct(rows, HD),
            struct(8, HD, kind=F32),
            struct(3, 4, 2 * rows, HD),
        ),
        [
            *to_ring(messages, shift_z),
            *(share_ring, share_ahead, share_behind),
            *(tokens, cotangent, gain[None, :], stats, d_scales),
        ],
        1,
        extra=(far_other,),
    )
    share_last, _ = lax.optimization_barrier((share_ring, mixed))
    share_far = shift_y(share_last, 2)
    scales = sum(ring4(scales + swap_z(scales), shift_x))
    share_last, _ = lax.optimization_barrier((share_far, scales))
    shares = [near, share_far, swap_core(near), swap_core(share_last)]
    images = [message, other, high, left, right, far_other, low]

    g_attn_out, g_down, g_qkv, g_up = pl.pallas_call(
        grads_kernel,
        out_shape=(
            struct(HD, 4 * HD),
            struct(ff, 4 * HD),
            struct(4 * HD, 3 * HD),
            struct(4 * HD, ff),
        ),
        in_specs=[SMEM, *[VMEM] * 12],
        out_specs=[VMEM] * 4,
        scratch_shapes=[
            pltpu.VMEM((8 * rows, ff + HD), BF16),
            pltpu.VMEM((8 * rows, 3 * HD + ff), BF16),
            pltpu.VMEM((8, 16, ff + HD), BF16),
            pltpu.VMEM((2, 8, 2, 2 * rows, HD), BF16),
            pltpu.VMEM((8 * rows, 4 * HD), BF16),
            pltpu.VMEM((8 * rows, 4 * HD), BF16),
        ],
        cost_estimate=cost(8),
        compiler_params=pltpu.CompilerParams(vmem_limit_bytes=36 * MIB),
    )(pos, gains, *shares, *images)
    return mixed, d_tokens, scales[0], scales[1:3], g_qkv, g_up, g_attn_out, g_down


def solution(mesh):
    in_specs = (
        P("dp", "mp"),
        P("mp"),
        P(None, "mp"),
        P(None, "mp"),
        P(None, "mp"),
        P("mp", None),
        P("mp", None),
        P("dp", "mp"),
    )
    out_specs = (
        P("dp", "mp"),
        P("dp", "mp"),
        P("mp"),
        P(None, "mp"),
        P("dp", "mp"),
        P("dp", "mp"),
        P("mp", "dp"),
        P("mp", "dp"),
    )
    return jax.shard_map(body, mesh=mesh, in_specs=in_specs, out_specs=out_specs, check_vma=False)
```
